32 devices in a mesh: fsdp: 4 (over x, core), ctx: 4 (over z), tp: 2 (over y).
Axes of the slice: x: 2, y: 2, z: 4, core: 2. Of those that a mesh axis runs over, the one named last changes fastest.
Arguments:
- tokens: float32 [8192, 1536], P(('fsdp', 'ctx')), may hold values from -6 to 6
- cotangent: float32 [8192, 1536], P(('fsdp', 'ctx')), may hold values from -6 to 6
- seq_lengths: int32 [4, 6], P('fsdp'), may hold values from 1 to 1280, as said below
- deal: int32 [4, 8], P('fsdp'), may hold values from 0 to 7, as said below
- norm_gains: bfloat16 [2, 2, 1536], P(None, None, 'fsdp'), may hold values from 0.5 to 1.5
- query_key_value: bfloat16 [2, 3, 1536, 1536], P(None, None, 'fsdp', 'tp'), may hold values from -0.15625 to 0.15625
- forget_weight: bfloat16 [2, 1536, 24], P(None, 'fsdp', 'tp'), may hold values from -0.078125 to 0.078125
- forget_bias: bfloat16 [2, 24], P(None, 'tp'), may hold values from 1.5 to 7
- out_weight: bfloat16 [2, 1536, 1536], P(None, 'tp', 'fsdp'), may hold values from -0.75 to 0.75
- gate_up_weight: bfloat16 [2, 2, 1536, 4096], P(None, None, 'fsdp', 'tp'), may hold values from -0.15625 to 0.15625
- down_weight: bfloat16 [2, 4096, 1536], P(None, 'tp', 'fsdp'), may hold values from -0.09375 to 0.09375
Outputs:
- mixed_out: float32 [8192, 1536], P(('fsdp', 'ctx'))
- grad_tokens: float32 [8192, 1536], P(('fsdp', 'ctx'))
- grad_norm_gains: float32 [2, 2, 1536], P(None, None, 'fsdp')
- grad_query_key_value: float32 [2, 3, 1536, 1536], P(None, None, 'fsdp', 'tp')
- grad_forget_weight: float32 [2, 1536, 24], P(None, 'fsdp', 'tp')
- grad_forget_bias: float32 [2, 24], P(None, 'tp')
- grad_out_weight: float32 [2, 1536, 1536], P(None, 'tp', 'fsdp')
- grad_gate_up_weight: float32 [2, 2, 1536, 4096], P(None, None, 'fsdp', 'tp')
- grad_down_weight: float32 [2, 4096, 1536], P(None, 'tp', 'fsdp')
- rms_values: float32 [2, 3], replicated
The draws below stay inside these ranges and needn't reach their ends.
Inputs may be any that keep to these rules, and one draw needn't show every extreme that they name: `seq_lengths`: the first sequence of each pack has 1280 tokens; each row sums to 2048. `deal`: each row is a permutation; entry 2 c lies below 4 and entry 2 c + 1 does not.
All inputs are finite; a program needn't handle non-finite values.
Results may differ from the reference program's by a relative error of at most 0.038.
Values may be sent and summed in bfloat16 or wider, within the bound.
A program may use at most 448 MiB of HBM per device.

```python
import math
from functools import partial
import jax
import jax.numpy as jnp
from jax import lax

D = 1536
H = 24
HD = 64
FF = 4096
LAYERS = 2
SEQS = 6
BLK = 256
PACK = 2048
BLOCKS = 8
PACKS = 4
TOKENS = 8192
LONGEST = 1280


def draw_seq_lengths(key, part):
    key = jax.random.fold_in(key, 11)
    rest_tokens = PACK - LONGEST

    def one_row(row_key):
        cut_points = jnp.sort(jax.random.permutation(row_key, rest_tokens - 1)[:SEQS - 2] + 1).astype(jnp.int32)
        bounds = jnp.concatenate([jnp.zeros((1,), jnp.int32), cut_points, jnp.full((1,), rest_tokens, jnp.int32)])
        return jnp.concatenate([jnp.full((1,), LONGEST, jnp.int32), bounds[1:] - bounds[:-1]])
    return jax.vmap(one_row)(jax.random.split(key, PACKS))


def draw_deal(key, part):
    key = jax.random.fold_in(key, 23)
    half_count = BLOCKS // 2

    def one_row(row_key):
        first_key, second_key = jax.random.split(row_key)
        early_blocks = jax.random.permutation(first_key, half_count)
        late_blocks = jax.random.permutation(second_key, half_count) + half_count
        return jnp.stack([early_blocks, late_blocks], axis=1).reshape(BLOCKS).astype(jnp.int32)
    return jax.vmap(one_row)(jax.random.split(key, PACKS))


def block_levels(own_key, dims, shards, low, top_value):
    def one(position, shards_of):
        steps = jax.random.uniform(jax.random.fold_in(jax.random.fold_in(own_key, 6), position), (shards_of,), jnp.float32, low / len(shards), top_value / len(shards))
        return jnp.repeat(jnp.exp(steps), dims[position] // shards_of).reshape((-1,) + (1,) * (len(dims) - position - 1))

    gain = one(*shards[0])
    for cut in shards[1:]:
        gain = gain * one(*cut)
    return gain


def bell_draw(key, shape, spread, bound, cuts=(), kind=jnp.bfloat16):
    drawn = jax.random.normal(key, shape, jnp.float32) * spread
    if len(cuts) > 0:
        drawn = block_levels(key, shape, cuts, -0.22, 0.18) * drawn
    return jnp.clip(drawn, min=-bound, max=bound).astype(kind)


def setup_inputs(seed: int = 0) -> dict:
    streams_of = jax.random.split(jax.random.key(seed), 12)
    return {
        "tokens": bell_draw(streams_of[0], (TOKENS, D), 1.0, 6.0, ((0, 16),), jnp.float32),
        "cotangent": bell_draw(streams_of[1], (TOKENS, D), 1.0, 6.0, ((0, 16),), jnp.float32),
        "seq_lengths": draw_seq_lengths(jax.random.fold_in(streams_of[11], 71), 0),
        "deal": draw_deal(jax.random.fold_in(streams_of[11], 71), 0),
        "norm_gains": jnp.clip(1.0 + 0.1 * jax.random.normal(streams_of[4], (LAYERS, 2, D), jnp.float32), 0.5, 1.5).astype(jnp.bfloat16),
        "query_key_value": bell_draw(streams_of[5], (LAYERS, 3, D, H * HD), D ** -0.5, 0.15625, ((2, 4), (3, 2))),
        "forget_weight": bell_draw(streams_of[6], (LAYERS, D, H), (4 * D) ** -0.5, 0.078125, ((1, 4), (2, 2))),
        "forget_bias": jnp.clip(1.5 + 5.5 * jax.random.uniform(streams_of[7], (LAYERS, H), jnp.float32) ** block_levels(streams_of[7], (LAYERS, H), ((1, 2),), -0.2, 0.2), 1.5, 7.0).astype(jnp.bfloat16),
        "out_weight": bell_draw(streams_of[8], (LAYERS, H * HD, D), HD ** -0.5, 0.75, ((1, 2), (2, 4))),
        "gate_up_weight": bell_draw(streams_of[9], (LAYERS, 2, D, FF), D ** -0.5, 0.15625, ((2, 4), (3, 2))),
        "down_weight": bell_draw(streams_of[10], (LAYERS, FF, D), FF ** -0.5, 0.09375, ((1, 2), (2, 4))),
    }


@jax.custom_vjp
def low(v):
    return lax.optimization_barrier(v.astype(jnp.bfloat16)).astype(jnp.float32)

@jax.custom_vjp
def low_back(v):
    return v

def low_keep(v):
    return (low(v), None)

def low_pass(kept, grad):
    return (grad,)

def back_keep(v):
    return (v, None)

def back_low(kept, grad):
    return (low(grad),)
low.defvjp(low_keep, low_pass)
low_back.defvjp(back_keep, back_low)
EPSILON = 1e-06
NEG_BIG = -1e+30

def matmul_high(left, right):
    return jnp.dot(left, right, precision=lax.Precision.HIGHEST)

def rms_norm(values):
    return values * lax.rsqrt(lax.optimization_barrier(jnp.mean(values * values, axis=-1, keepdims=True)) + EPSILON)

def deal_inverse(deal_row):
    block_count = deal_row.shape[0]
    return jnp.zeros((block_count,), jnp.int32).at[deal_row].set(jnp.arange(block_count, dtype=jnp.int32))

def take_blocks(block_values, block_index):
    return jnp.take(block_values, block_index, axis=0)

def regroup(values, index):
    shaped = values.reshape((PACKS, BLOCKS, BLK) + values.shape[1:])
    moved = jax.vmap(take_blocks)(shaped, index)
    return moved.reshape(values.shape)

def pack_attention(item):
    queries, keys, values, decay, seq_ids = item
    positions = jnp.arange(PACK, dtype=jnp.int32)
    allowed = (seq_ids[:, None] == seq_ids[None, :]) & (positions[None, :] <= positions[:, None])
    score_scale = 1.0 / math.sqrt(HD)

    def one_head(head_item):
        query_rows, key_rows, value_rows, decay_rows = head_item
        scores = matmul_high(query_rows, key_rows.T) * score_scale + decay_rows[:, None] - decay_rows[None, :]
        scores = jnp.where(allowed, low_back(scores), NEG_BIG)
        peak_score = lax.optimization_barrier(jnp.max(scores, axis=1, keepdims=True))
        exponent = jnp.exp(scores - peak_score)
        probabilities = exponent / lax.optimization_barrier(jnp.sum(exponent, axis=1, keepdims=True))
        return matmul_high(low(probabilities), value_rows)
    heads_first = (jnp.swapaxes(queries, 0, 1), jnp.swapaxes(keys, 0, 1), jnp.swapaxes(values, 0, 1), decay.T)
    return jnp.swapaxes(lax.map(jax.checkpoint(one_head), heads_first), 0, 1)

def forward(residual, gains, qkv_weight, forget_weight, bias, out_weight, gate_up_weight, down_weight, seq_ids):
    stat_rows = []
    for layer_index in range(LAYERS):
        normed_one = low(rms_norm(residual) * gains[layer_index, 0])
        projected = [low(low_back(matmul_high(normed_one, qkv_weight[layer_index, slot]))) for slot in range(3)]
        logits = low_back(matmul_high(normed_one, forget_weight[layer_index]) + bias[layer_index])
        forget_log = low(jax.nn.log_sigmoid(logits))
        decay = jnp.cumsum(forget_log.reshape(PACKS, PACK, H), axis=1)
        shaped = [item.reshape(PACKS, PACK, H, HD) for item in projected]
        attended = lax.map(pack_attention, (shaped[0], shaped[1], shaped[2], decay, seq_ids))
        attended = low(low_back(attended.reshape(TOKENS, H * HD)))
        branch = low_back(matmul_high(attended, out_weight[layer_index]))
        middle = residual + branch
        normed_two = low(rms_norm(middle) * gains[layer_index, 1])
        gate = low_back(matmul_high(normed_two, gate_up_weight[layer_index, 0]))
        upper = low_back(matmul_high(normed_two, gate_up_weight[layer_index, 1]))
        hidden = low(jax.nn.silu(gate) * upper)
        ffn_branch = low_back(matmul_high(hidden, down_weight[layer_index]))
        stat_rows.append(jnp.stack([jnp.sum(residual * residual), jnp.sum(branch * branch), jnp.sum(ffn_branch * ffn_branch)]))
        residual = middle + ffn_branch
    return (residual, jnp.stack(stat_rows))

def reference(tokens, cotangent, seq_lengths, deal, norm_gains, query_key_value, forget_weight, forget_bias, out_weight, gate_up_weight, down_weight):
    inverse = jax.vmap(deal_inverse)(deal)
    positions = jnp.arange(PACK, dtype=jnp.int32)
    seq_ends = jnp.cumsum(seq_lengths, axis=1)
    seq_ids = lax.optimization_barrier(jnp.sum((positions[None, :, None] >= seq_ends[:, None, :]).astype(jnp.int32), axis=2))
    start_residual = regroup(tokens.astype(jnp.float32), inverse)
    mixed_out, pullback, sums = jax.vjp(partial(forward, seq_ids=seq_ids), start_residual, norm_gains.astype(jnp.float32), query_key_value.astype(jnp.float32), forget_weight.astype(jnp.float32), forget_bias.astype(jnp.float32), out_weight.astype(jnp.float32), gate_up_weight.astype(jnp.float32), down_weight.astype(jnp.float32), has_aux=True)
    grads = pullback(cotangent.astype(jnp.float32))
    grad_tokens = regroup(grads[0], deal)
    rms_values = jnp.sqrt(sums / (TOKENS * D))
    return (mixed_out, grad_tokens, grads[1], grads[2], grads[3], grads[4], grads[5], grads[6], grads[7], rms_values)
```

```python
import functools
import math

import jax
import jax.numpy as jnp
from jax import lax
from jax.experimental import pallas as pl
from jax.experimental.pallas import tpu as pltpu
from jax.sharding import PartitionSpec as P

EPSILON = 1e-06
NEG_BIG = -1e30
FIRST_LENGTH = 1280
BF16 = jnp.bfloat16
F32 = jnp.float32


def matmul(left, right):
    return jnp.dot(left, right, preferred_element_type=F32)


def split_three(values):
    high = values.astype(BF16).astype(F32)
    rest = values - high
    middle = rest.astype(BF16).astype(F32)
    return high, middle, rest - middle


def lanes_of(shape):
    return lax.broadcasted_iota(jnp.int32, shape, 1)


def with_lanes(base, first, columns):
    lane = lanes_of(base.shape)
    for offset, column in enumerate(columns):
        base = jnp.where(lane == first + offset, column, base)
    return base


def widen(values, width):
    rows, lanes = values.shape
    return jnp.concatenate([values, jnp.zeros((rows, width - lanes), values.dtype)], axis=1)


def key_range(block, block_rows):
    first_blocks = FIRST_LENGTH // block_rows
    return (0 if block < first_blocks else first_blocks), block + 1


def tile_mask(ends_ref, key_block, query_block, block_rows):
    shape = (block_rows, block_rows)
    mask = None
    if key_block == query_block:
        mask = lax.broadcasted_iota(jnp.int32, shape, 0) <= lax.broadcasted_iota(jnp.int32, shape, 1)
    if (query_block + 1) * block_rows > FIRST_LENGTH:
        key_pos = key_block * block_rows + lax.broadcasted_iota(jnp.int32, (block_rows, 1), 0)
        query_pos = query_block * block_rows + lax.broadcasted_iota(jnp.int32, (1, block_rows), 1)
        key_seq = jnp.zeros((block_rows, 1), jnp.int32)
        query_seq = jnp.zeros((1, block_rows), jnp.int32)
        for entry in range(ends_ref.shape[0]):
            key_seq = key_seq + (key_pos >= ends_ref[entry]).astype(jnp.int32)
            query_seq = query_seq + (query_pos >= ends_ref[entry]).astype(jnp.int32)
        same = key_seq == query_seq
        mask = same if mask is None else mask & same
    return mask


def place_pack(blk_ref, received, pack_ref, block_rows):
    for k, ref in enumerate(received):
        for half in range(2):
            start = pl.multiple_of(blk_ref[2 * k + half] * block_rows, block_rows)
            pack_ref[pl.ds(start, block_rows), :] = ref[half * block_rows : (half + 1) * block_rows, :]


def decay_blocks(pack_ref, forget_lane, block_count, block_rows):
    shape = (block_rows, block_rows)
    lower = (
        lax.broadcasted_iota(jnp.int32, shape, 0) >= lax.broadcasted_iota(jnp.int32, shape, 1)
    ).astype(BF16)
    carry = None
    out = []
    for block in range(block_count):
        rows = slice(block * block_rows, (block + 1) * block_rows)
        sums = matmul(lower, pack_ref[rows, forget_lane : forget_lane + 64])
        if carry is not None:
            sums = sums + carry
        carry = sums[block_rows - 1 : block_rows, :]
        out.append(sums)
    return out


def attend_kernel(hp, head_size, block_rows, blk_ref, ends_ref, *refs):
    count = (len(refs) - 6) // 2
    received, outs = refs[:count], refs[count : 2 * count]
    lse_ref, att_ref, pack_ref, key_ref, value_ref, out_ref = refs[2 * count :]
    block_count = 2 * count
    width = hp * head_size
    scale = 1.0 / math.sqrt(head_size)
    place_pack(blk_ref, received, pack_ref, block_rows)
    decays = decay_blocks(pack_ref, 3 * width, block_count, block_rows)
    masks = {}
    for block in range(block_count):
        for key_block in range(*key_range(block, block_rows)):
            if block not in masks or key_block != block:
                masks[block, key_block] = None
    for head in range(hp):
        query_tiles = []
        for block in range(block_count):
            rows = slice(block * block_rows, (block + 1) * block_rows)
            here = slice(head * head_size, (head + 1) * head_size)
            query = pack_ref[rows, here].astype(F32) * scale
            key = pack_ref[rows, width + here.start : width + here.stop].astype(F32)
            value = pack_ref[rows, 2 * width + here.start : 2 * width + here.stop].astype(F32)
            decay = decays[block][:, head : head + 1]
            high, middle, low = split_three(decay)
            key_ref[rows, :] = with_lanes(
                widen(key, 128), head_size, (-high, -middle, -low, 1.0, 1.0, 1.0)
            ).astype(BF16)
            value_ref[:, rows] = with_lanes(widen(value, 128), head_size, (1.0,)).T.astype(BF16)
            query_tiles.append(
                with_lanes(
                    widen(query, 128), head_size, (1.0, 1.0, 1.0, high, middle, low)
                ).T.astype(BF16)
            )
        for block in range(block_count):
            rows = slice(block * block_rows, (block + 1) * block_rows)
            first, last = key_range(block, block_rows)
            tiles = []
            peak = None
            for key_block in range(first, last):
                key_rows = slice(key_block * block_rows, (key_block + 1) * block_rows)
                scores = matmul(key_ref[key_rows, :], query_tiles[block])
                mask = tile_mask(ends_ref, key_block, block, block_rows)
                if mask is not None:
                    scores = jnp.where(mask, scores, NEG_BIG)
                top = jnp.max(scores, axis=0, keepdims=True)
                peak = top if peak is None else jnp.maximum(peak, top)
                tiles.append(scores)
            total = jnp.zeros((128, block_rows), F32)
            for key_block, scores in zip(range(first, last), tiles):
                key_rows = slice(key_block * block_rows, (key_block + 1) * block_rows)
                exponent = jnp.exp(scores - peak).astype(BF16)
                total = total + matmul(value_ref[:, key_rows], exponent)
            exp_total = total[head_size : head_size + 1, :]
            attended = total * (1.0 / exp_total)
            att_ref[head, :, rows] = attended[:head_size, :]
            lse_ref[head, :, rows] = peak + jnp.log(exp_total)
            out_ref[rows, head * head_size : (head + 1) * head_size] = attended.T[:, :head_size].astype(
                BF16
            )
    for k, ref in enumerate(outs):
        for half in range(2):
            start = pl.multiple_of(blk_ref[2 * k + half] * block_rows, block_rows)
            ref[:, half * width : (half + 1) * width] = out_ref[pl.ds(start, block_rows), :]


def attend_back_kernel(hp, head_size, block_rows, blk_ref, ends_ref, *refs):
    count = (len(refs) - 11) // 3
    received = refs[:count]
    grads = refs[count : 2 * count]
    lse_ref, att_ref = refs[2 * count : 2 * count + 2]
    outs = refs[2 * count + 2 : 3 * count + 2]
    (
        pack_ref,
        grad_ref,
        key_ref,
        value_ref,
        key_turned_ref,
        grad_key_ref,
        grad_value_ref,
        decay_ref,
        out_ref,
    ) = refs[3 * count + 2 :]
    block_count = 2 * count
    width = hp * head_size
    group = pack_ref.shape[1]
    scale = 1.0 / math.sqrt(head_size)
    place_pack(blk_ref, received, pack_ref, block_rows)
    for k, ref in enumerate(grads):
        for half in range(2):
            start = pl.multiple_of(blk_ref[2 * k + half] * block_rows, block_rows)
            grad_ref[pl.ds(start, block_rows), :] = ref[:, half * width : (half + 1) * width]
    decays = decay_blocks(pack_ref, 3 * width, block_count, block_rows)
    for head in range(hp):
        here = slice(head * head_size, (head + 1) * head_size)
        query_tiles = []
        query_plain = []
        grad_tiles = []
        for block in range(block_count):
            rows = slice(block * block_rows, (block + 1) * block_rows)
            query = pack_ref[rows, here].astype(F32) * scale
            key = pack_ref[rows, width + here.start : width + here.stop].astype(F32)
            value = pack_ref[rows, 2 * width + here.start : 2 * width + here.stop].astype(F32)
            grad = grad_ref[rows, here].astype(F32)
            high, middle, low = split_three(decays[block][:, head : head + 1])
            key_ref[rows, :] = with_lanes(
                widen(key, 128), head_size, (-high, -middle, -low, 1.0, 1.0, 1.0, 1.0, 1.0, 1.0)
            ).astype(BF16)
            key_turned_ref[:, rows] = with_lanes(widen(key, 128), head_size, (1.0,)).T.astype(BF16)
            value_ref[rows, :] = with_lanes(widen(value, 128), head_size, (1.0, 1.0, 1.0)).astype(BF16)
            query_wide = with_lanes(widen(query, 128), head_size, (1.0, 1.0, 1.0, high, middle, low)).T
            query_plain.append(with_lanes(widen(query, 128), head_size, (1.0,)).astype(BF16))
            row_index = lax.broadcasted_iota(jnp.int32, query_wide.shape, 0)
            for offset, part in enumerate(split_three(lse_ref[head, :, rows])):
                query_wide = jnp.where(row_index == head_size + 6 + offset, -part, query_wide)
            query_tiles.append(query_wide.astype(BF16))
            grad_turned = widen(grad, 128).T
            inner = jnp.sum(grad_turned[:head_size, :] * att_ref[head, :, rows], axis=0, keepdims=True)
            for offset, part in enumerate(split_three(inner)):
                grad_turned = jnp.where(row_index == head_size + offset, -part, grad_turned)
            grad_tiles.append(grad_turned.astype(BF16))
        for block in range(block_count):
            rows = slice(block * block_rows, (block + 1) * block_rows)
            first, last = key_range(block, block_rows)
            grad_query = jnp.zeros((128, block_rows), F32)
            for key_block in range(first, last):
                key_rows = slice(key_block * block_rows, (key_block + 1) * block_rows)
                scores = matmul(key_ref[key_rows, :], query_tiles[block])
                mask = tile_mask(ends_ref, key_block, block, block_rows)
                if mask is not None:
                    scores = jnp.where(mask, scores, NEG_BIG)
                probs = jnp.exp(scores)
                grad_scores = (probs * matmul(value_ref[key_rows, :], grad_tiles[block])).astype(BF16)
                grad_query = grad_query + matmul(key_turned_ref[:, key_rows], grad_scores)
                add_key = matmul(grad_scores, query_plain[block])
                add_value = matmul(probs.astype(BF16), grad_ref[rows, here])
                if key_block == block:
                    grad_key_ref[key_rows, :] = add_key
                    grad_value_ref[key_rows, :] = add_value
                else:
                    grad_key_ref[key_rows, :] += add_key
                    grad_value_ref[key_rows, :] += add_value
            turned = grad_query.T
            out_ref[rows, here] = (turned[:, :head_size] * scale).astype(BF16)
            decay_ref[rows, head : head + 1] = turned[:, head_size : head_size + 1]
        out_ref[:, width + here.start : width + here.stop] = grad_key_ref[:, :head_size].astype(BF16)
        out_ref[:, 2 * width + here.start : 2 * width + here.stop] = grad_value_ref[...].astype(BF16)
        decay_ref[:, head : head + 1] -= grad_key_ref[:, head_size : head_size + 1]
    shape = (block_rows, block_rows)
    upper = (
        lax.broadcasted_iota(jnp.int32, shape, 0) <= lax.broadcasted_iota(jnp.int32, shape, 1)
    ).astype(BF16)
    carry = None
    tail = group - 3 * width
    for block in reversed(range(block_count)):
        rows = slice(block * block_rows, (block + 1) * block_rows)
        sums = jnp.zeros((block_rows, 128), F32)
        values = jnp.where(lanes_of((block_rows, 128)) < hp, decay_ref[rows, :], 0.0)
        for part in split_three(values):
            sums = sums + matmul(upper, part.astype(BF16))
        if carry is not None:
            sums = sums + carry
        carry = sums[0:1, :]
        out_ref[rows, 3 * width : group] = sums[:, :tail].astype(BF16)
    for k, ref in enumerate(outs):
        for half in range(2):
            start = pl.multiple_of(blk_ref[2 * k + half] * block_rows, block_rows)
            ref[half * block_rows : (half + 1) * block_rows, :] = out_ref[pl.ds(start, block_rows), :]


def vmem_spec():
    return pl.BlockSpec(memory_space=pltpu.VMEM)


def smem_spec():
    return pl.BlockSpec(memory_space=pltpu.SMEM)


def attend(blk, ends, received, hp, head_size, block_rows):
    count = len(received)
    pack_rows = 2 * count * block_rows
    width = hp * head_size
    group = received[0].shape[1]
    out = pl.pallas_call(
        functools.partial(attend_kernel, hp, head_size, block_rows),
        out_shape=[jax.ShapeDtypeStruct((block_rows, 2 * width), BF16)] * count
        + [
            jax.ShapeDtypeStruct((hp, 1, pack_rows), F32),
            jax.ShapeDtypeStruct((hp, head_size, pack_rows), F32),
        ],
        in_specs=[smem_spec(), smem_spec()] + [vmem_spec()] * count,
        out_specs=[vmem_spec()] * (count + 2),
        scratch_shapes=[
            pltpu.VMEM((pack_rows, group), BF16),
            pltpu.VMEM((pack_rows, 128), BF16),
            pltpu.VMEM((128, pack_rows), BF16),
            pltpu.VMEM((pack_rows, width), BF16),
        ],
        compiler_params=pltpu.CompilerParams(vmem_limit_bytes=48 << 20),
        name="attend",
    )(blk, ends, *received)
    return out[:count], out[count], out[count + 1]


def attend_back(blk, ends, received, grads, lse, att, hp, head_size, block_rows):
    count = len(received)
    pack_rows = 2 * count * block_rows
    width = hp * head_size
    group = received[0].shape[1]
    return pl.pallas_call(
        functools.partial(attend_back_kernel, hp, head_size, block_rows),
        out_shape=[jax.ShapeDtypeStruct((2 * block_rows, group), BF16)] * count,
        in_specs=[smem_spec(), smem_spec()] + [vmem_spec()] * (2 * count + 2),
        out_specs=[vmem_spec()] * count,
        scratch_shapes=[
            pltpu.VMEM((pack_rows, group), BF16),
            pltpu.VMEM((pack_rows, width), BF16),
            pltpu.VMEM((pack_rows, 128), BF16),
            pltpu.VMEM((pack_rows, 128), BF16),
            pltpu.VMEM((128, pack_rows), BF16),
            pltpu.VMEM((pack_rows, 128), F32),
            pltpu.VMEM((pack_rows, head_size), F32),
            pltpu.VMEM((pack_rows, 128), F32),
            pltpu.VMEM((pack_rows, group), BF16),
        ],
        compiler_params=pltpu.CompilerParams(vmem_limit_bytes=48 << 20),
        name="attend_back",
    )(blk, ends, *received, *grads, lse, att)


def rms_factor(values):
    return lax.rsqrt(jnp.mean(values * values, axis=-1, keepdims=True) + EPSILON)


def norm_back(grad_normed, values, factor, gain_row):
    unit_rows = values * factor
    grad_gain = jnp.sum(grad_normed * unit_rows, axis=0)
    grad_unit = grad_normed * gain_row.astype(F32)
    inner_mean = jnp.mean(grad_unit * unit_rows, axis=-1, keepdims=True)
    return (factor * (grad_unit - unit_rows * inner_mean), grad_gain)


def swap(values, axis, size, step):
    return lax.ppermute(values, axis, [(i, i ^ step) for i in range(size)])


def halving(size):
    steps = []
    while size > 1:
        size //= 2
        steps.append(size)
    return steps


def shards(
    sizes,
    tokens,
    cotangent,
    seq_lengths,
    deal,
    norm_gains,
    query_key_value,
    forget_weight,
    forget_bias,
    out_weight,
    gate_up_weight,
    down_weight,
):
    fsdp, ctx, tp = sizes
    layer_count = query_key_value.shape[0]
    row_count, model_width = tokens.shape
    heads_here = forget_weight.shape[2]
    head_size = query_key_value.shape[3] // heads_here
    block_rows = row_count // 2
    piece = model_width // fsdp
    half_width = model_width // 2
    hp = -(-heads_here // ctx)
    heads_padded = hp * ctx
    width = hp * head_size
    group = -(-(3 * width + hp) // 128) * 128
    f_index = lax.axis_index("fsdp")
    c_index = lax.axis_index("ctx")
    fsdp_steps = halving(fsdp)
    offsets = [0]
    for step in fsdp_steps:
        offsets = offsets + [item ^ step for item in offsets]

    def gather(values, axis):
        for step in fsdp_steps:
            values = jnp.concatenate([values, swap(values, "fsdp", fsdp, step)], axis=axis)
        return values

    def add_low(left, right):
        return (left.astype(F32) + right.astype(F32)).astype(BF16)

    def scatter(near, far, axis):
        for step in reversed(fsdp_steps):
            near = add_low(near, swap(far, "fsdp", fsdp, step))
            if step != fsdp_steps[0]:
                size = near.shape[axis] // 2
                near, far = (
                    lax.slice_in_dim(near, 0, size, axis=axis),
                    lax.slice_in_dim(near, size, 2 * size, axis=axis),
                )
        return near

    def sum_ctx(values, kind):
        if ctx != 4:
            return lax.psum(values, "ctx")
        inward = (values + lax.ppermute(values, "ctx", [(0, 1), (3, 2)])).astype(kind)
        total = (inward + lax.ppermute(inward, "ctx", [(1, 2), (2, 1)])).astype(kind)
        outward = lax.ppermute(total, "ctx", [(1, 0), (2, 3)])
        return jnp.where((c_index == 0) | (c_index == 3), outward, total)

    def sum_tp(values):
        values = values.astype(BF16)
        step = 1
        while step < tp:
            values = values.astype(F32) + swap(values, "tp", tp, step).astype(F32)
            step *= 2
            if step < tp:
                values = values.astype(BF16)
        return values.astype(F32)

    def exchange(sends):
        return [sends[0]] + [swap(sends[k], "ctx", ctx, k) for k in range(1, ctx)]

    def to_local(values):
        return jnp.concatenate(
            [
                lax.dynamic_slice_in_dim(values, (f_index ^ item) * piece, piece, axis=1)
                for item in offsets
            ],
            axis=1,
        )

    def from_local(values):
        places = jnp.asarray([offsets.index(item) for item in range(fsdp)], jnp.int32)
        return jnp.concatenate(
            [
                lax.dynamic_slice_in_dim(values, places[f_index ^ item] * piece, piece, axis=1)
                for item in range(fsdp)
            ],
            axis=1,
        )

    def pick(items, index):
        out = items[0]
        for entry in range(1, len(items)):
            out = jnp.where(index == entry, items[entry], out)
        return out

    deal_order = deal[0]
    inverse = (
        jnp.zeros((2 * ctx,), jnp.int32).at[deal_order].set(jnp.arange(2 * ctx, dtype=jnp.int32))
    )
    seq_ends = jnp.cumsum(seq_lengths[0]).astype(jnp.int32)
    peers = jnp.bitwise_xor(jnp.arange(ctx, dtype=jnp.int32), c_index)
    blk = jnp.take(deal_order.reshape(ctx, 2), peers, axis=0).reshape(2 * ctx)

    def arrange_qkv(layer):
        weights = query_key_value[layer].reshape(3, piece, heads_here, head_size)
        forget = forget_weight[layer]
        if heads_padded != heads_here:
            more = heads_padded - heads_here
            weights = jnp.pad(weights, ((0, 0), (0, 0), (0, more), (0, 0)))
            forget = jnp.pad(forget, ((0, 0), (0, more)))
        weights = weights.reshape(3, piece, ctx, width).transpose(1, 2, 0, 3)
        parts = [
            weights.reshape(piece, ctx, 3 * width),
            forget.reshape(piece, ctx, hp),
            jnp.zeros((piece, ctx, group - 3 * width - hp), BF16),
        ]
        return jnp.concatenate(parts, axis=2).reshape(piece, ctx * group)

    gains = gather(norm_gains.reshape(2 * layer_count, piece), 1)
    weights = []
    for layer in range(layer_count):
        weights.append(
            (
                gather(arrange_qkv(layer), 0),
                gather(out_weight[layer], 1),
                gather(gate_up_weight[layer], 1),
                gather(down_weight[layer], 1),
            )
        )

    cot_blocks = cotangent.astype(BF16).reshape(2, block_rows, model_width)
    late_side = (c_index >= ctx // 2).astype(jnp.int32)
    cot_sends = []
    for k in range(ctx):
        wanted = deal_order[2 * (c_index ^ k) + late_side]
        cot_sends.append(lax.dynamic_index_in_dim(cot_blocks, wanted % 2, 0, keepdims=False))
    cot_got = exchange(cot_sends)
    cot_dealt = jnp.concatenate(
        [pick(cot_got, (deal_order[2 * c_index + half] // 2) ^ c_index) for half in range(2)], axis=0
    )
    grad_residual = to_local(cot_dealt).astype(F32)

    bias_all = forget_bias.astype(F32)
    if heads_padded != heads_here:
        bias_all = jnp.pad(bias_all, ((0, 0), (0, heads_padded - heads_here)))
    bias_all = bias_all.reshape(layer_count, ctx, hp)

    residual = to_local(tokens)
    kept = []
    stat_terms = []
    for layer in range(layer_count):
        qkv_rows, out_rows, gate_up_rows, down_rows = weights[layer]
        gain_one, gain_two = gains[2 * layer], gains[2 * layer + 1]
        factor_one = rms_factor(residual)
        normed_one = (residual * factor_one * gain_one.astype(F32)).astype(BF16)
        projected = matmul(normed_one, qkv_rows).reshape(row_count, ctx, group)
        logits = projected[:, :, 3 * width : 3 * width + hp] + bias_all[layer][None]
        forget_log = jax.nn.log_sigmoid(logits).astype(BF16)
        packed = jnp.concatenate(
            [
                projected[:, :, : 3 * width].astype(BF16),
                forget_log,
                jnp.zeros((row_count, ctx, group - 3 * width - hp), BF16),
            ],
            axis=2,
        )
        sends = [
            lax.dynamic_index_in_dim(packed, c_index ^ k, 1, keepdims=False) for k in range(ctx)
        ]
        received = exchange(sends)
        att_sends, lse, att_turned = attend(
            blk, seq_ends, received, hp, head_size, block_rows
        )
        att_got = jnp.stack(exchange(att_sends)).reshape(ctx, block_rows, 2, width)
        attended = jnp.take(att_got, peers, axis=0).transpose(2, 1, 0, 3)
        attended = attended.reshape(row_count, heads_padded * head_size)[:, : heads_here * head_size]
        branch = sum_tp(matmul(attended, out_rows))
        middle = residual + branch
        factor_two = rms_factor(middle)
        normed_two = (middle * factor_two * gain_two.astype(F32)).astype(BF16)
        gate_up = jnp.einsum("td,jdf->jtf", normed_two, gate_up_rows, preferred_element_type=F32)
        hidden = (jax.nn.silu(gate_up[0]) * gate_up[1]).astype(BF16)
        ffn_branch = sum_tp(matmul(hidden, down_rows))
        stat_terms += [
            jnp.sum(residual * residual),
            jnp.sum(branch * branch),
            jnp.sum(ffn_branch * ffn_branch),
        ]
        kept.append(
            dict(
                residual=residual,
                factor_one=factor_one,
                normed_one=normed_one,
                logits=logits,
                received=received,
                lse=lse,
                att_turned=att_turned,
                attended=attended,
                middle=middle,
                factor_two=factor_two,
                normed_two=normed_two,
                gate_up=gate_up,
                hidden=hidden,
            )
        )
        residual = middle + ffn_branch

    final_blocks = residual.astype(BF16).reshape(2, block_rows, model_width)
    out_got = exchange(
        [
            lax.dynamic_index_in_dim(
                final_blocks, ((c_index ^ k) >= ctx // 2).astype(jnp.int32), 0, keepdims=False
            )
            for k in range(ctx)
        ]
    )
    mixed_local = jnp.concatenate(
        [pick(out_got, (inverse[2 * c_index + half] // 2) ^ c_index) for half in range(2)], axis=0
    )
    mixed_out = from_local(mixed_local).astype(F32)

    grads = {}
    gain_grads = [None] * (2 * layer_count)
    bias_grads = [None] * layer_count
    for layer in reversed(range(layer_count)):
        state = kept[layer]
        qkv_rows, out_rows, gate_up_rows, down_rows = weights[layer]
        gain_one, gain_two = gains[2 * layer], gains[2 * layer + 1]
        grad_ffn = grad_residual.astype(BF16)
        grad_hidden = jnp.einsum("td,fd->tf", grad_ffn, down_rows, preferred_element_type=F32)
        gate_values, up_values = state["gate_up"][0], state["gate_up"][1]
        gate_sigmoid = jax.nn.sigmoid(gate_values)
        grad_gate = (
            grad_hidden * up_values * gate_sigmoid * (1.0 + gate_values * (1.0 - gate_sigmoid))
        ).astype(BF16)
        grad_up = (grad_hidden * gate_values * gate_sigmoid).astype(BF16)
        grad_gate_up = jnp.stack([grad_gate, grad_up])
        two_part = jnp.einsum("jtf,jdf->td", grad_gate_up, gate_up_rows, preferred_element_type=F32)
        grad_normed_two = sum_tp(two_part)

        def halves(values):
            return values[:, :half_width], values[:, half_width:]

        down_grad = scatter(
            *[
                jnp.einsum("tf,td->fd", state["hidden"], part, preferred_element_type=F32).astype(BF16)
                for part in halves(grad_ffn)
            ],
            1,
        )
        gate_up_grad = scatter(
            *[
                jnp.einsum("td,jtf->jdf", part, grad_gate_up, preferred_element_type=F32).astype(BF16)
                for part in halves(state["normed_two"])
            ],
            1,
        )
        grads["down", layer] = sum_ctx(down_grad, BF16).astype(F32)
        grads["gate_up", layer] = sum_ctx(gate_up_grad, BF16).astype(F32)
        grad_from_two, gain_grads[2 * layer + 1] = norm_back(
            grad_normed_two, state["middle"], state["factor_two"], gain_two
        )
        grad_residual = grad_residual + grad_from_two
        grad_branch = grad_residual.astype(BF16)
        grad_attended = jnp.einsum(
            "td,ed->te", grad_branch, out_rows, preferred_element_type=F32
        ).astype(BF16)
        out_grad = scatter(
            *[
                jnp.einsum("te,td->ed", state["attended"], part, preferred_element_type=F32).astype(BF16)
                for part in halves(grad_branch)
            ],
            1,
        )
        grads["out", layer] = sum_ctx(out_grad, BF16).astype(F32)
        if heads_padded != heads_here:
            more = (heads_padded - heads_here) * head_size
            grad_attended = jnp.pad(grad_attended, ((0, 0), (0, more)))
        grad_attended = grad_attended.reshape(2, block_rows, ctx, width).transpose(2, 1, 0, 3)
        grad_attended = grad_attended.reshape(ctx, block_rows, 2 * width)
        grad_got = exchange(
            [
                lax.dynamic_index_in_dim(grad_attended, c_index ^ k, 0, keepdims=False)
                for k in range(ctx)
            ]
        )
        back_sends = attend_back(
            blk,
            seq_ends,
            state["received"],
            grad_got,
            state["lse"],
            state["att_turned"],
            hp,
            head_size,
            block_rows,
        )
        back_got = jnp.take(jnp.stack(exchange(back_sends)), peers, axis=0).transpose(1, 0, 2)
        grad_forget = back_got[:, :, 3 * width : 3 * width + hp].astype(F32)
        grad_logits = (grad_forget * jax.nn.sigmoid(-state["logits"])).astype(BF16)
        grad_qkv = jnp.concatenate(
            [
                back_got[:, :, : 3 * width],
                grad_logits,
                jnp.zeros((row_count, ctx, group - 3 * width - hp), BF16),
            ],
            axis=2,
        ).reshape(row_count, ctx * group)
        bias_grads[layer] = jnp.sum(grad_logits.astype(F32), axis=0).reshape(heads_padded)[:heads_here]
        one_part = jnp.einsum("te,de->td", grad_qkv, qkv_rows, preferred_element_type=F32)
        grad_normed_one = sum_tp(one_part)
        qkv_grad = sum_ctx(
            scatter(
                *[
                    jnp.einsum("td,te->de", part, grad_qkv, preferred_element_type=F32).astype(BF16)
                    for part in halves(state["normed_one"])
                ],
                0,
            ),
            BF16,
        ).reshape(piece, ctx, group)
        grads["qkv", layer] = (
            qkv_grad[:, :, : 3 * width]
            .reshape(piece, ctx, 3, width)
            .transpose(2, 0, 1, 3)
            .reshape(3, piece, heads_padded * head_size)[:, :, : heads_here * head_size]
            .astype(F32)
        )
        grads["forget", layer] = (
            qkv_grad[:, :, 3 * width : 3 * width + hp]
            .reshape(piece, heads_padded)[:, :heads_here]
            .astype(F32)
        )
        grad_from_one, gain_grads[2 * layer] = norm_back(
            grad_normed_one, state["residual"], state["factor_one"], gain_one
        )
        grad_residual = grad_residual + grad_from_one
    grad_tokens = from_local(grad_residual)

    small = jnp.concatenate(
        [from_local(jnp.stack(gain_grads)).reshape(-1), jnp.stack(stat_terms)] + bias_grads
    )
    used = small.shape[0]
    small = jnp.pad(small, (0, -used % 1024)).reshape(-1, 128)
    for step in reversed(fsdp_steps):
        small = small + swap(small, "fsdp", fsdp, step)
    small = sum_ctx(small, F32).reshape(-1)
    gain_size = 2 * layer_count * model_width
    grad_gains = lax.dynamic_slice_in_dim(
        small[:gain_size].reshape(layer_count, 2, model_width), f_index * piece, piece, axis=2
    )
    stat_sums = small[gain_size : gain_size + 3 * layer_count].reshape(layer_count, 3)
    bias_sums = small[gain_size + 3 * layer_count : used].reshape(layer_count, heads_here)
    rms_values = jnp.sqrt(stat_sums / (row_count * model_width * fsdp * ctx))

    def both(name):
        return jnp.stack([grads[name, layer] for layer in range(layer_count)])

    return (
        mixed_out,
        grad_tokens,
        grad_gains,
        both("qkv"),
        both("forget"),
        bias_sums,
        both("out"),
        both("gate_up"),
        both("down"),
        rms_values,
    )


def solution(mesh):
    in_specs = (
        P(("fsdp", "ctx"), None),
        P(("fsdp", "ctx"), None),
        P("fsdp", None),
        P("fsdp", None),
        P(None, None, "fsdp"),
        P(None, None, "fsdp", "tp"),
        P(None, "fsdp", "tp"),
        P(None, "tp"),
        P(None, "tp", "fsdp"),
        P(None, None, "fsdp", "tp"),
        P(None, "tp", "fsdp"),
    )
    out_specs = (
        P(("fsdp", "ctx"), None),
        P(("fsdp", "ctx"), None),
        P(None, None, "fsdp"),
        P(None, None, "fsdp", "tp"),
        P(None, "fsdp", "tp"),
        P(None, "tp"),
        P(None, "tp", "fsdp"),
        P(None, None, "fsdp", "tp"),
        P(None, "tp", "fsdp"),
        P(),
    )
    sizes = (mesh.shape["fsdp"], mesh.shape["ctx"], mesh.shape["tp"])
    return jax.shard_map(
        functools.partial(shards, sizes),
        mesh=mesh,
        in_specs=in_specs,
        out_specs=out_specs,
        check_vma=False,
    )
```

```python
import functools
import math

import jax
import jax.numpy as jnp
from jax import lax
from jax.experimental import pallas as pl
from jax.experimental.layout import Layout, with_layout_constraint
from jax.experimental.pallas import tpu as pltpu
from jax.sharding import PartitionSpec as P

EPSILON = 1e-06
NEG_BIG = -1e30
FIRST_LENGTH = 1280
BF16 = jnp.bfloat16
F32 = jnp.float32


def matmul(left, right):
    return jnp.dot(left, right, preferred_element_type=F32)


def split_three(values):
    high = values.astype(BF16).astype(F32)
    rest = values - high
    middle = rest.astype(BF16).astype(F32)
    return high, middle, rest - middle


def iota(shape, dim):
    return lax.broadcasted_iota(jnp.int32, shape, dim)


def with_lanes(base, first, columns):
    lane = iota(base.shape, 1)
    for offset, column in enumerate(columns):
        base = jnp.where(lane == first + offset, column, base)
    return base


def with_rows(base, first, rows):
    row = iota(base.shape, 0)
    for offset, item in enumerate(rows):
        base = jnp.where(row == first + offset, item, base)
    return base


def first_lanes(values, lanes):
    return jnp.where(iota(values.shape, 1) < lanes, values, 0.0)


def widen(values, width=128):
    rows, lanes = values.shape
    return jnp.concatenate([values, jnp.zeros((rows, width - lanes), values.dtype)], axis=1)


class Pack:
    def __init__(self, hp, head_size):
        self.hp, self.head_size = hp, head_size
        self.value_tiles = (hp + 2) // 2
        self.tiles = hp + self.value_tiles

    def value_place(self, head):
        return self.hp + head // 2, (head % 2) * self.head_size


def peer(c, k):
    out, bit = c, 1
    while bit <= k:
        if k & bit:
            out = out + bit * (1 - 2 * ((c // bit) % 2))
        bit *= 2
    return out


def key_range(block, block_rows):
    first_blocks = FIRST_LENGTH // block_rows
    return (0 if block < first_blocks else first_blocks), block + 1


def score_tiles(block, block_rows, ends_ref):
    first, last = key_range(block, block_rows)
    if (block + 1) * block_rows <= FIRST_LENGTH:
        shape = (block_rows, block_rows)
        diagonal = (slice(block * block_rows, last * block_rows), iota(shape, 0) <= iota(shape, 1))
        if first == block:
            return [diagonal]
        return [(slice(first * block_rows, block * block_rows), None), diagonal]
    rows = (last - first) * block_rows
    key_pos = first * block_rows + iota((rows, 1), 0)
    query_pos = block * block_rows + iota((1, block_rows), 1)
    key_seq = jnp.zeros((rows, 1), jnp.int32)
    query_seq = jnp.zeros((1, block_rows), jnp.int32)
    for entry in range(ends_ref.shape[0]):
        key_seq = key_seq + (key_pos >= ends_ref[entry]).astype(jnp.int32)
        query_seq = query_seq + (query_pos >= ends_ref[entry]).astype(jnp.int32)
    mask = (key_pos <= query_pos) & (key_seq == query_seq)
    return [(slice(first * block_rows, last * block_rows), mask)]


def decay_blocks(load, block_count, block_rows):
    shape = (block_rows, block_rows)
    lower = (iota(shape, 0) >= iota(shape, 1)).astype(BF16)
    carry = None
    out = []
    for block in range(block_count):
        sums = matmul(lower, load(block))
        if carry is not None:
            sums = sums + carry
        carry = sums[block_rows - 1 : block_rows, :]
        out.append(sums)
    return out


def greet(count):
    c = lax.axis_index("ctx")
    barrier = pltpu.get_barrier_semaphore()
    for k in range(1, count):
        pl.semaphore_signal(
            barrier, inc=1, device_id={"ctx": peer(c, k)}, device_id_type=pl.DeviceIdType.MESH
        )
    pl.semaphore_wait(barrier, count - 1)
    return c


def move(k, c, source, target, send_sem, recv_sem):
    if k == 0:
        copy = pltpu.make_async_copy(source, target, recv_sem)
    else:
        copy = pltpu.make_async_remote_copy(
            src_ref=source,
            dst_ref=target,
            send_sem=send_sem,
            recv_sem=recv_sem,
            device_id={"ctx": peer(c, k)},
            device_id_type=pl.DeviceIdType.MESH,
        )
    copy.start()
    return copy


def arrive(k, copy):
    if k == 0:
        copy.wait()
    else:
        copy.wait_recv()


def attend_kernel(
    pack,
    place_ref,
    blk_ref,
    ends_ref,
    send_ref,
    out_ref,
    kept_ref,
    lse_ref,
    att_ref,
    key_ref,
    value_ref,
    block_ref,
    back_ref,
    in_send,
    in_recv,
    out_send,
    out_recv,
    keep_sem,
    *recv_refs,
):
    count = send_ref.shape[0]
    block_rows = send_ref.shape[3]
    block_count = 2 * count
    hp, head_size = pack.hp, pack.head_size
    scale = 1.0 / math.sqrt(head_size)
    c = greet(count)
    copies = {}
    order = [pack.value_place(hp)[0]]
    for head in range(hp):
        order += [item for item in (head, pack.value_place(head)[0]) if item not in order]
    for tile in order:
        for k in reversed(range(count)):
            copies[tile, k] = move(
                k,
                c,
                send_ref.at[k, tile],
                recv_refs[tile].at[pl.ds(2 * k, 2)],
                in_send.at[tile, k],
                in_recv.at[tile, k],
            )
    keeps = []
    here = set()

    def need(tile):
        if tile not in here:
            here.add(tile)
            for k in range(count):
                arrive(k, copies[tile, k])
            keep = pltpu.make_async_copy(recv_refs[tile], kept_ref.at[tile], keep_sem.at[tile])
            keep.start()
            keeps.append(keep)

    tile, lane = pack.value_place(hp)
    need(tile)
    decays = decay_blocks(
        lambda block: recv_refs[tile][place_ref[block]][:, lane : lane + head_size], block_count, block_rows
    )
    returns = []
    for head in range(hp):
        need(head)
        value_tile, value_lane = pack.value_place(head)
        need(value_tile)
        query_tiles = []
        for block in range(block_count):
            rows = slice(block * block_rows, (block + 1) * block_rows)
            pair = recv_refs[head][place_ref[block]].astype(F32)
            value = recv_refs[value_tile][place_ref[block]].astype(F32)
            value = value[:, value_lane : value_lane + head_size]
            high, middle, low = split_three(decays[block][:, head : head + 1])
            key_ref[rows, :] = with_lanes(
                widen(pair[:, head_size:]), head_size, (-high, -middle, -low, 1.0, 1.0, 1.0)
            ).astype(BF16)
            value_ref[:, rows] = with_lanes(widen(value), head_size, (1.0,)).T.astype(BF16)
            query_tiles.append(
                with_lanes(first_lanes(pair * scale, head_size), head_size, (1.0, 1.0, 1.0, high, middle, low))
                .T.astype(BF16)
            )
        for block in range(block_count):
            rows = slice(block * block_rows, (block + 1) * block_rows)
            tiles = []
            peak = None
            for key_rows, mask in score_tiles(block, block_rows, ends_ref):
                scores = matmul(key_ref[key_rows, :], query_tiles[block])
                if mask is not None:
                    scores = jnp.where(mask, scores, NEG_BIG)
                top = jnp.max(scores, axis=0, keepdims=True)
                peak = top if peak is None else jnp.maximum(peak, top)
                tiles.append((key_rows, scores))
            total = jnp.zeros((128, block_rows), F32)
            for key_rows, scores in tiles:
                total = total + matmul(value_ref[:, key_rows], jnp.exp(scores - peak).astype(BF16))
            exp_total = total[head_size : head_size + 1, :]
            attended = total * (1.0 / exp_total)
            att_ref[head, :, rows] = attended[:head_size, :]
            lse_ref[head, :, rows] = peak + jnp.log(exp_total)
            block_ref[head, block] = attended.T.astype(BF16)
        for k in range(count):
            back_ref[k, head] = jnp.concatenate(
                [
                    block_ref[head, blk_ref[2 * k]][:, :head_size],
                    block_ref[head, blk_ref[2 * k + 1]][:, :head_size],
                ],
                axis=1,
            )
        for k in reversed(range(count)):
            returns.append(
                (
                    k,
                    move(
                        k,
                        c,
                        back_ref.at[k, head],
                        out_ref.at[k, head],
                        out_send.at[k, head],
                        out_recv.at[k, head],
                    ),
                )
            )
    for k, copy in returns:
        copy.wait()
    for (tile, k), copy in copies.items():
        if k:
            copy.wait_send()
    for keep in keeps:
        keep.wait()


def attend_back_kernel(
    pack,
    place_ref,
    blk_ref,
    ends_ref,
    kept_ref,
    lse_ref,
    att_ref,
    send_ref,
    out_ref,
    key_ref,
    value_ref,
    turned_ref,
    plain_ref,
    grad_key_ref,
    grad_value_ref,
    decay_ref,
    block_ref,
    back_ref,
    in_send,
    in_recv,
    out_send,
    out_recv,
    *grad_refs,
):
    count = send_ref.shape[0]
    block_rows = send_ref.shape[2]
    block_count = 2 * count
    hp, head_size = pack.hp, pack.head_size
    scale = 1.0 / math.sqrt(head_size)
    c = greet(count)
    copies = {}
    for head in range(hp):
        for k in reversed(range(count)):
            copies[head, k] = move(
                k,
                c,
                send_ref.at[k, head],
                grad_refs[head].at[k],
                in_send.at[head, k],
                in_recv.at[head, k],
            )
    tile, lane = pack.value_place(hp)
    decays = decay_blocks(
        lambda block: kept_ref[tile, place_ref[block]][:, lane : lane + head_size], block_count, block_rows
    )
    returns = []

    def give(tile):
        for k in range(count):
            for half in range(2):
                back_ref[tile, k, half] = block_ref[tile, blk_ref[2 * k + half]]
        for k in reversed(range(count)):
            returns.append(
                move(
                    k,
                    c,
                    back_ref.at[tile, k],
                    out_ref.at[k, tile],
                    out_send.at[tile, k],
                    out_recv.at[tile, k],
                )
            )

    for head in range(hp):
        value_tile, value_lane = pack.value_place(head)
        query_tiles = []
        for block in range(block_count):
            rows = slice(block * block_rows, (block + 1) * block_rows)
            pair = kept_ref[head, place_ref[block]].astype(F32)
            value = kept_ref[value_tile, place_ref[block]].astype(F32)
            value = value[:, value_lane : value_lane + head_size]
            key = pair[:, head_size:]
            query = first_lanes(pair * scale, head_size)
            high, middle, low = split_three(decays[block][:, head : head + 1])
            key_ref[rows, :] = with_lanes(
                widen(key), head_size, (-high, -middle, -low, 1.0, 1.0, 1.0, 1.0, 1.0, 1.0)
            ).astype(BF16)
            turned_ref[:, rows] = with_lanes(widen(key), head_size, (1.0,)).T.astype(BF16)
            value_ref[rows, :] = with_lanes(widen(value), head_size, (1.0, 1.0, 1.0)).astype(BF16)
            plain_ref[rows, :] = with_lanes(query, head_size, (1.0,)).astype(BF16)
            query_wide = with_lanes(query, head_size, (1.0, 1.0, 1.0, high, middle, low)).T
            log_parts = [-part for part in split_three(lse_ref[head, :, rows])]
            query_tiles.append(with_rows(query_wide, head_size + 6, log_parts).astype(BF16))
        for k in range(count):
            arrive(k, copies[head, k])
        grad_plain = []
        grad_tiles = []
        for block in range(block_count):
            rows = slice(block * block_rows, (block + 1) * block_rows)
            place = place_ref[block]
            both = grad_refs[head][place // 2].astype(F32)
            grad = jnp.where(place % 2 == 0, both[:, :head_size], both[:, head_size:])
            grad_plain.append(grad.astype(BF16))
            grad_turned = widen(grad).T
            inner = jnp.sum(grad_turned[:head_size, :] * att_ref[head, :, rows], axis=0, keepdims=True)
            inner_parts = [-part for part in split_three(inner)]
            grad_tiles.append(with_rows(grad_turned, head_size, inner_parts).astype(BF16))
        query_grads = []
        for block in range(block_count):
            rows = slice(block * block_rows, (block + 1) * block_rows)
            grad_query = jnp.zeros((128, block_rows), F32)
            for key_rows, mask in score_tiles(block, block_rows, ends_ref):
                scores = matmul(key_ref[key_rows, :], query_tiles[block])
                if mask is not None:
                    scores = jnp.where(mask, scores, NEG_BIG)
                probs = jnp.exp(scores)
                grad_scores = (probs * matmul(value_ref[key_rows, :], grad_tiles[block])).astype(BF16)
                grad_query = grad_query + matmul(turned_ref[:, key_rows], grad_scores)
                add_key = matmul(grad_scores, plain_ref[rows, :])
                add_value = matmul(probs.astype(BF16), grad_plain[block])
                old = slice(key_rows.start, max(key_rows.start, rows.start))
                split = old.stop - old.start
                if split:
                    grad_key_ref[old, :] += add_key[:split]
                    grad_value_ref[old, :] += add_value[:split]
                if key_rows.stop == rows.stop:
                    grad_key_ref[rows, :] = add_key[split:]
                    grad_value_ref[rows, :] = add_value[split:]
            turned = grad_query.T
            query_grads.append((turned[:, :head_size] * scale).astype(BF16))
            decay_ref[rows, head : head + 1] = turned[:, head_size : head_size + 1]
        for block in range(block_count):
            rows = slice(block * block_rows, (block + 1) * block_rows)
            key_wide = grad_key_ref[rows, :]
            block_ref[head, block] = jnp.concatenate(
                [query_grads[block], key_wide[:, :head_size].astype(BF16)], axis=1
            )
            block_ref[value_tile, block, :, value_lane : value_lane + head_size] = grad_value_ref[
                rows, :
            ].astype(BF16)
            decay_ref[rows, head : head + 1] -= key_wide[:, head_size : head_size + 1]
        give(head)
        if value_lane and value_tile != tile:
            give(value_tile)
    shape = (block_rows, block_rows)
    upper = (iota(shape, 0) <= iota(shape, 1)).astype(BF16)
    carry = None
    for block in reversed(range(block_count)):
        rows = slice(block * block_rows, (block + 1) * block_rows)
        sums = jnp.zeros((block_rows, 128), F32)
        values = jnp.where(iota((block_rows, 128), 1) < hp, decay_ref[rows, :], 0.0)
        for part in split_three(values):
            sums = sums + matmul(upper, part.astype(BF16))
        if carry is not None:
            sums = sums + carry
        carry = sums[0:1, :]
        if lane == 0:
            block_ref[tile, block] = sums.astype(BF16)
        else:
            block_ref[tile, block, :, lane : lane + head_size] = sums[:, :head_size].astype(BF16)
    give(tile)
    for copy in returns:
        copy.wait()
    for (head, k), copy in copies.items():
        if k:
            copy.wait_send()


def spec(space):
    return pl.BlockSpec(memory_space=space)


def attend(pack, place, blk, ends, sends):
    count, tiles, _, block_rows, _ = sends.shape
    hp, head_size = pack.hp, pack.head_size
    pack_rows = 2 * count * block_rows
    dma = pltpu.SemaphoreType.DMA
    return pl.pallas_call(
        functools.partial(attend_kernel, pack),
        out_shape=[
            jax.ShapeDtypeStruct((count, hp, block_rows, 128), BF16),
            jax.ShapeDtypeStruct((tiles, 2 * count, block_rows, 128), BF16),
            jax.ShapeDtypeStruct((hp, 1, pack_rows), F32),
            jax.ShapeDtypeStruct((hp, head_size, pack_rows), F32),
        ],
        in_specs=[spec(pltpu.SMEM)] * 3 + [spec(pl.ANY)],
        out_specs=[spec(pl.ANY), spec(pl.ANY), spec(pltpu.VMEM), spec(pltpu.VMEM)],
        scratch_shapes=[
            pltpu.VMEM((pack_rows, 128), BF16),
            pltpu.VMEM((128, pack_rows), BF16),
            pltpu.VMEM((hp, 2 * count, block_rows, 128), BF16),
            pltpu.VMEM((count, hp, block_rows, 128), BF16),
            dma((tiles, count)),
            dma((tiles, count)),
            dma((count, hp)),
            dma((count, hp)),
            dma((tiles,)),
        ]
        + [pltpu.VMEM((2 * count, block_rows, 128), BF16)] * tiles,
        compiler_params=pltpu.CompilerParams(
            vmem_limit_bytes=40 << 20, collective_id=0, has_side_effects=True
        ),
        name="attend",
    )(place, blk, ends, sends)


def attend_back(pack, place, blk, ends, kept, lse, att, sends):
    count, hp, block_rows, _ = sends.shape
    tiles = kept.shape[0]
    head_size = pack.head_size
    pack_rows = 2 * count * block_rows
    dma = pltpu.SemaphoreType.DMA
    return pl.pallas_call(
        functools.partial(attend_back_kernel, pack),
        out_shape=jax.ShapeDtypeStruct((count, tiles, 2, block_rows, 128), BF16),
        in_specs=[spec(pltpu.SMEM)] * 3 + [spec(pltpu.VMEM)] * 3 + [spec(pl.ANY)],
        out_specs=spec(pl.ANY),
        scratch_shapes=[
            pltpu.VMEM((pack_rows, 128), BF16),
            pltpu.VMEM((pack_rows, 128), BF16),
            pltpu.VMEM((128, pack_rows), BF16),
            pltpu.VMEM((pack_rows, 128), BF16),
            pltpu.VMEM((pack_rows, 128), F32),
            pltpu.VMEM((pack_rows, head_size), F32),
            pltpu.VMEM((pack_rows, 128), F32),
            pltpu.VMEM((tiles, 2 * count, block_rows, 128), BF16),
            pltpu.VMEM((tiles, count, 2, block_rows, 128), BF16),
            dma((hp, count)),
            dma((hp, count)),
            dma((tiles, count)),
            dma((tiles, count)),
        ]
        + [pltpu.VMEM((count, block_rows, 128), BF16)] * hp,
        compiler_params=pltpu.CompilerParams(
            vmem_limit_bytes=40 << 20, collective_id=1, has_side_effects=True
        ),
        name="attend_back",
    )(place, blk, ends, kept, lse, att, sends)


VMEM_BYTES = 60 << 20


def turned_matmul(left, right):
    return lax.dot_general(left, right, (((1,), (1,)), ((), ())), preferred_element_type=F32)


def column_sums(values):
    return jnp.sum(values, axis=0, keepdims=True)


def unit_factor(values):
    return lax.rsqrt(jnp.mean(values * values, axis=-1, keepdims=True) + EPSILON)


def norm_rows_back(grad_normed, values, gain):
    factor = unit_factor(values)
    unit = values * factor
    grad_unit = grad_normed * gain
    inner = jnp.mean(grad_unit * unit, axis=-1, keepdims=True)
    return factor * (grad_unit - unit * inner), column_sums(grad_normed * unit)


class Refs:
    def __init__(self, names, refs):
        for name, ref in zip(names, refs, strict=True):
            setattr(self, name, ref)

    def pieces(self, name):
        out = []
        while hasattr(self, f"{name}_{len(out)}"):
            out.append(getattr(self, f"{name}_{len(out)}"))
        return out


def named_call(kernel, name, inputs, outputs, scratch, collective_id):
    names = list(inputs) + list(outputs) + list(scratch)

    def body(*refs):
        kernel(Refs(names, refs))

    params = dict(vmem_limit_bytes=VMEM_BYTES)
    if collective_id is not None:
        params.update(collective_id=collective_id, has_side_effects=True)
    out = pl.pallas_call(
        body,
        out_shape=[jax.ShapeDtypeStruct(shape, kind) for shape, kind, _ in outputs.values()],
        in_specs=[spec(space) for _, space in inputs.values()],
        out_specs=[spec(space) for _, _, space in outputs.values()],
        scratch_shapes=list(scratch.values()),
        compiler_params=pltpu.CompilerParams(**params),
        name=name,
    )(*[array for array, _ in inputs.values()])
    return dict(zip(outputs, out))


class Copies:
    def __init__(self, sems):
        self.sems, self.used, self.saves = sems, 0, []

    def load(self, source, target):
        copy = pltpu.make_async_copy(source, target, self.sems.at[self.used])
        self.used += 1
        copy.start()
        return copy

    def load_down(self, pieces, target, columns=None):
        rows = pieces[0].shape[0]
        out = []
        for index, item in enumerate(pieces):
            place = target.at[pl.ds(index * rows, rows)]
            if columns is not None:
                place = target.at[pl.ds(index * rows, rows), pl.ds(0, columns)]
            out.append(self.load(item, place))
        return out

    def load_beside(self, pieces, target):
        columns = pieces[0].shape[1]
        return [
            self.load(item, target.at[:, pl.ds(index * columns, columns)])
            for index, item in enumerate(pieces)
        ]

    def save(self, source, target):
        self.saves.append(self.load(source, target))

    def finish(self):
        for copy in self.saves:
            copy.wait()


class PairSums:
    def __init__(self, steps, send_refs, recv_refs, send_sem, recv_sem):
        self.steps, self.send_refs, self.recv_refs = steps, send_refs, recv_refs
        self.send_sem, self.recv_sem = send_sem, recv_sem
        self.t = lax.axis_index("tp")
        self.started = []

    def greet(self):
        barrier = pltpu.get_barrier_semaphore()
        for step in self.steps:
            pl.semaphore_signal(
                barrier, inc=1, device_id={"tp": peer(self.t, step)}, device_id_type=pl.DeviceIdType.MESH
            )
        pl.semaphore_wait(barrier, len(self.steps))

    def copy(self, index):
        copy = pltpu.make_async_remote_copy(
            src_ref=self.send_refs[index],
            dst_ref=self.recv_refs[index],
            send_sem=self.send_sem.at[index],
            recv_sem=self.recv_sem.at[index],
            device_id={"tp": peer(self.t, self.steps[index % len(self.steps)])},
            device_id_type=pl.DeviceIdType.MESH,
        )
        copy.start()
        self.started.append(copy)
        return copy

    def start(self, place):
        self.first = getattr(self, "first", {})
        self.first[place] = self.copy(place * len(self.steps))

    def finish(self, place):
        copy = self.first[place]
        base = place * len(self.steps)
        for offset in range(len(self.steps)):
            if offset:
                self.send_refs[base + offset][...] = total.astype(BF16)
                copy = self.copy(base + offset)
            copy.wait_recv()
            total = self.send_refs[base + offset][...].astype(F32) + self.recv_refs[base + offset][
                ...
            ].astype(F32)
        return total

    def end(self):
        for copy in self.started:
            copy.wait_send()


def pair_scratch(places, steps, rows, columns):
    count = places * len(steps)
    buffers = {f"send{index}": pltpu.VMEM((rows, columns), BF16) for index in range(count)}
    buffers.update({f"recv{index}": pltpu.VMEM((rows, columns), BF16) for index in range(count)})
    buffers["pair_send"] = pltpu.SemaphoreType.DMA((count,))
    buffers["pair_recv"] = pltpu.SemaphoreType.DMA((count,))
    return buffers


def pair_sums(r, places, steps):
    count = places * len(steps)
    return PairSums(
        steps,
        [getattr(r, f"send{index}") for index in range(count)],
        [getattr(r, f"recv{index}") for index in range(count)],
        r.pair_send,
        r.pair_recv,
    )


def over_units(units, block, body):
    def step(index, carry):
        body(pl.ds(pl.multiple_of(index * block, block), block))
        return carry

    lax.fori_loop(0, units // block, step, 0)


def tile_columns(pack, item, head):
    first = (item * pack.hp + head) * pack.head_size
    return slice(first, first + pack.head_size)


def write_tiles(pack, count, packed_ref, half, query, key, value, forget):
    size = pack.head_size
    forget_tile, forget_lane = pack.value_place(pack.hp)
    lane = iota(forget.shape, 1)
    for item in range(count):
        target = peer(lax.axis_index("ctx"), item)
        for head in range(pack.hp):
            columns = tile_columns(pack, item, head)
            packed_ref[target, head, half] = jnp.concatenate([query[:, columns], key[:, columns]], axis=1)
        shift = (forget_lane - item * pack.hp) % 128
        moved = pltpu.roll(forget, shift, 1) if shift else forget
        moved = jnp.where((lane >= forget_lane) & (lane < forget_lane + pack.hp), moved, 0.0)
        for tile in range(pack.hp, pack.tiles):
            parts = []
            for slot in range(2):
                head = 2 * (tile - pack.hp) + slot
                if head < pack.hp:
                    parts.append(value[:, tile_columns(pack, item, head)])
                else:
                    parts.append(moved[:, slot * size : (slot + 1) * size].astype(BF16))
            packed_ref[target, tile, half] = jnp.concatenate(parts, axis=1)


def project_rows(pack, r, count, width, half, rows, normed):
    def part(first, size):
        return matmul(normed, r.w_mix[:, first : first + size])

    query, key, value = [part(index * width, width).astype(BF16) for index in range(3)]
    logits = part(3 * width, 128) + r.bias[...]
    r.logits[rows, :] = logits
    forget = jnp.minimum(logits, 0.0) - jnp.log1p(jnp.exp(-jnp.abs(logits)))
    forget = forget.astype(BF16).astype(F32)
    write_tiles(pack, count, r.packed, half, query, key, value, forget)


def first_kernel(pack, count, width, r):
    copies = Copies(r.sems)
    c = lax.axis_index("ctx")
    block_rows = r.packed.shape[3]
    for copy in copies.load_down(r.pieces("w_qkv"), r.w_mix):
        copy.wait()
    for half in range(2):
        rows = slice(half * block_rows, (half + 1) * block_rows)
        residual = r.residual[rows, :]
        normed = (residual * unit_factor(residual) * r.gain[...]).astype(BF16)
        r.normed[rows, :] = normed
        add = column_sums(residual * residual)
        r.stat[...] = jnp.broadcast_to(add if half == 0 else add + r.stat[0:1, :], r.stat.shape)
        project_rows(pack, r, count, width, half, rows, normed)


def middle_kernel(pack, count, units, unit_block, steps, r):
    copies = Copies(r.sems)
    c = lax.axis_index("ctx")
    sums = pair_sums(r, 4, steps)
    block_rows = r.attended.shape[0] // 2
    load_out = copies.load_beside([item.at[pl.ds(0, r.w_o.shape[0])] for item in r.pieces("w_back")], r.w_o)
    load_base = copies.load(r.residual, r.base)
    load_units = copies.load_down([item.at[0] for item in r.pieces("w_units")], r.w_g)
    load_units += copies.load_down([item.at[1] for item in r.pieces("w_units")], r.w_mix, units)
    load_units += copies.load_beside(
        [item.at[pl.ds(r.w_o.shape[0], units)] for item in r.pieces("w_back")], r.w_d
    )
    sums.greet()
    for copy in load_out:
        copy.wait()
    halves = [slice(half * block_rows, (half + 1) * block_rows) for half in range(2)]
    size = pack.head_size
    for half, rows in enumerate(halves):
        columns = []
        for item in range(count):
            for head in range(pack.hp):
                columns.append(r.att[peer(c, item), head][:, half * size : (half + 1) * size])
        attended = jnp.concatenate(columns, axis=1)
        r.attended[rows, :] = attended
        sums.send_refs[half * len(steps)][...] = matmul(attended, r.w_o[...]).astype(BF16)
        sums.start(half)
    load_base.wait()
    for copy in load_units:
        copy.wait()
    for half, rows in enumerate(halves):
        branch = sums.finish(half)
        add = column_sums(branch * branch)
        r.stat[0:1, :] = add if half == 0 else r.stat[0:1, :] + add
        middle = r.base[rows, :] + branch
        r.base[rows, :] = middle
        copies.save(r.base.at[rows], r.middle.at[rows])
        normed = (middle * unit_factor(middle) * r.gain_two[...]).astype(BF16)
        r.normed_keep[rows, :] = normed
        copies.save(r.normed_keep.at[rows], r.normed_two.at[rows])
        r.total[...] = jnp.zeros(r.total.shape, F32)

        def block(columns, rows=rows):
            gate = matmul(r.normed_keep[rows, :], r.w_g[:, columns])
            up = matmul(r.normed_keep[rows, :], r.w_mix[:, columns])
            hidden = (gate * jax.nn.sigmoid(gate) * up).astype(BF16)
            r.gate_keep[rows, columns] = gate.astype(BF16)
            r.up_keep[rows, columns] = up.astype(BF16)
            r.hidden_keep[rows, columns] = hidden
            r.total[...] += matmul(hidden, r.w_d[columns, :])

        over_units(units, unit_block, block)
        sums.send_refs[(2 + half) * len(steps)][...] = r.total[...].astype(BF16)
        sums.start(2 + half)
        copies.save(r.gate_keep.at[rows], r.gate.at[rows])
        copies.save(r.up_keep.at[rows], r.up.at[rows])
        copies.save(r.hidden_keep.at[rows], r.hidden.at[rows])
    for half, rows in enumerate(halves):
        branch = sums.finish(2 + half)
        add = column_sums(branch * branch)
        r.stat[1:2, :] = add if half == 0 else r.stat[1:2, :] + add
        residual = r.base[rows, :] + branch
        r.after_keep[rows, :] = residual
        copies.save(r.after_keep.at[rows], r.after.at[rows])
    copies.finish()
    sums.end()


def back_kernel(pack, count, width, units, unit_block, steps, upper, feed, r):
    copies = Copies(r.sems)
    c = lax.axis_index("ctx")
    size = pack.head_size
    forget_tile, forget_lane = pack.value_place(pack.hp)
    if feed:
        sums = pair_sums(r, 4 if upper else 2, steps)
        second = 2 if upper else 0
    block_rows = r.total.shape[0]
    halves = [slice(half * block_rows, (half + 1) * block_rows) for half in range(2)]
    if upper:
        load_qkv = copies.load_down(r.pieces("w_qkv"), r.w_mix, 3 * width + 128)
    if feed:
        if upper:
            load_value = [copies.load(r.residual.at[rows], r.values.at[rows]) for rows in halves]
        load_base = copies.load(r.base_in, r.base)
        waits = [copies.load(r.gate, r.gate_keep), copies.load(r.up, r.up_keep)]
        waits += copies.load_beside(
        [item.at[pl.ds(r.w_o.shape[0], units)] for item in r.pieces("w_back")], r.w_d
    )
        waits += copies.load_down([item.at[0] for item in r.pieces("w_units")], r.w_g)
        load_out = copies.load_beside([item.at[pl.ds(0, r.w_o.shape[0])] for item in r.pieces("w_back")], r.w_o)
        sums.greet()

    if upper:
        for copy in load_qkv:
            copy.wait()
        for half, rows in enumerate(halves):
            columns = [[], [], []]
            forget = jnp.zeros((block_rows, 128), F32)
            lane = iota(forget.shape, 1)
            for item in range(count):
                source = peer(c, item)
                for head in range(pack.hp):
                    pair = r.back[source, head, half]
                    columns[0].append(pair[:, :size])
                    columns[1].append(pair[:, size:])
                    value_tile, value_lane = pack.value_place(head)
                    columns[2].append(r.back[source, value_tile, half][:, value_lane : value_lane + size])
                wide = r.back[source, forget_tile, half].astype(F32)
                shift = (item * pack.hp - forget_lane) % 128
                moved = pltpu.roll(wide, shift, 1) if shift else wide
                first = item * pack.hp
                forget = jnp.where((lane >= first) & (lane < first + pack.hp), moved, forget)
            grad_logits = (forget * jax.nn.sigmoid(-r.logits[rows, :])).astype(BF16)
            add = column_sums(grad_logits.astype(F32))
            r.bias_grad[...] = jnp.broadcast_to(
                add if half == 0 else add + r.bias_grad[0:1, :], r.bias_grad.shape
            )
            for index in range(3):
                r.grads_keep[rows, index * width : (index + 1) * width] = jnp.concatenate(
                    columns[index], axis=1
                )
            r.grads_keep[rows, 3 * width :] = grad_logits
            copies.save(r.grads_keep.at[rows], r.grads.at[rows])
            grads = r.grads_keep[rows, :]
            part = turned_matmul(grads, r.w_mix[:, : 3 * width + 128]).astype(BF16)
            if feed:
                sums.send_refs[half * len(steps)][...] = part
                sums.start(half)
            else:
                r.one_part[rows, :] = part
    if feed:
        waits += copies.load_down([item.at[1] for item in r.pieces("w_units")], r.w_mix, units)
        load_base.wait()
        load_middle = []
        for half, rows in enumerate(halves):
            grad = r.base[rows, :].astype(F32)
            if upper:
                load_value[half].wait()
                back, add = norm_rows_back(sums.finish(half), r.values[rows, :], r.gain_one[...])
                r.gain_grad[0:1, :] = add if half == 0 else r.gain_grad[0:1, :] + add
                grad = grad + back
            load_middle.append(copies.load(r.middle.at[rows], r.values.at[rows]))
            r.grad_keep[rows, :] = grad
            r.low_keep[rows, :] = grad.astype(BF16)
            copies.save(r.low_keep.at[rows], r.low.at[rows])
            for copy in waits:
                copy.wait()
            waits = []
            r.total[...] = jnp.zeros(r.total.shape, F32)

            def block(columns, rows=rows):
                grad_hidden = turned_matmul(r.low_keep[rows, :], r.w_d[columns, :])
                gate = r.gate_keep[rows, columns].astype(F32)
                up = r.up_keep[rows, columns].astype(F32)
                sigmoid = jax.nn.sigmoid(gate)
                grad_gate = (grad_hidden * up * sigmoid * (1.0 + gate * (1.0 - sigmoid))).astype(BF16)
                grad_up = (grad_hidden * gate * sigmoid).astype(BF16)
                r.gate_keep[rows, columns] = grad_gate
                r.up_keep[rows, columns] = grad_up
                r.total[...] += turned_matmul(grad_gate, r.w_g[:, columns]) + turned_matmul(
                    grad_up, r.w_mix[:, columns]
                )

            over_units(units, unit_block, block)
            sums.send_refs[(second + half) * len(steps)][...] = r.total[...].astype(BF16)
            sums.start(second + half)
            copies.save(r.gate_keep.at[rows], r.grad_gate.at[rows])
            copies.save(r.up_keep.at[rows], r.grad_up.at[rows])
        for copy in load_out:
            copy.wait()
        for half, rows in enumerate(halves):
            load_middle[half].wait()
            back, add = norm_rows_back(sums.finish(second + half), r.values[rows, :], r.gain_two[...])
            r.gain_grad[1:2, :] = add if half == 0 else r.gain_grad[1:2, :] + add
            grad = r.grad_keep[rows, :] + back
            r.grad_keep[rows, :] = grad
            copies.save(r.grad_keep.at[rows], r.grad.at[rows])
            low = grad.astype(BF16)
            r.branch[rows, :] = low
            r.turned[rows, :] = turned_matmul(low, r.w_o[...]).astype(BF16)
        for item in range(count):
            for head in range(pack.hp):
                columns = tile_columns(pack, item, head)
                r.sends[peer(c, item), head] = jnp.concatenate(
                    [r.turned[rows, columns] for rows in halves], axis=1
                )
    copies.finish()
    if feed:
        sums.end()


def tail_kernel(chunks, halved, fsdp_step, fsdp_axis, counts, *refs):
    units = counts
    own = refs[:units]
    far = refs[units : units + len(halved)]
    outs = refs[units + len(halved) : 2 * units + len(halved)]
    rest = refs[2 * units + len(halved) :]
    inward = rest[:units]
    crossed = rest[units : units + len(halved)]
    x_send, x_recv, a_send, a_recv, b_send, b_recv, c_send, c_recv = rest[units + len(halved) :]
    c = lax.axis_index("ctx")
    f = lax.axis_index(fsdp_axis)
    mesh_id = pl.DeviceIdType.MESH
    barrier = pltpu.get_barrier_semaphore()
    pl.semaphore_signal(
        barrier, inc=1, device_id={fsdp_axis: peer(f, fsdp_step)}, device_id_type=mesh_id
    )
    for k in range(1, 4):
        pl.semaphore_signal(barrier, inc=1, device_id={"ctx": peer(c, k)}, device_id_type=mesh_id)
    pl.semaphore_wait(barrier, 4)
    is_end = c * (3 - c) == 0
    is_middle = c * (3 - c) != 0

    def remote(source, target, send, recv, where):
        return pltpu.make_async_remote_copy(
            src_ref=source,
            dst_ref=target,
            send_sem=send,
            recv_sem=recv,
            device_id=where,
            device_id_type=mesh_id,
        )

    def mine(unit):
        return crossed[halved.index(unit)] if unit in halved else own[unit]

    def rows_of(index):
        unit, first, count = chunks[index]
        return unit, pl.ds(first, count)

    def x_copy(index):
        unit, rows = rows_of(index)
        place = halved.index(unit)
        return remote(
            far[place].at[rows],
            crossed[place].at[rows],
            x_send.at[index],
            x_recv.at[index],
            {fsdp_axis: peer(f, fsdp_step)},
        )

    def a_copy(index):
        unit, rows = rows_of(index)
        return remote(
            mine(unit).at[rows], inward[unit].at[rows], a_send.at[index], a_recv.at[index], {"ctx": 1 + c // 2}
        )

    def b_copy(index):
        unit, rows = rows_of(index)
        return remote(
            inward[unit].at[rows], outs[unit].at[rows], b_send.at[index], b_recv.at[index], {"ctx": 3 - c}
        )

    def c_copy(index):
        unit, rows = rows_of(index)
        return remote(
            outs[unit].at[rows], outs[unit].at[rows], c_send.at[index], c_recv.at[index], {"ctx": 3 * (c - 1)}
        )

    def add(left, right, kind):
        return (left.astype(F32) + right.astype(F32)).astype(kind)

    total = len(chunks)
    for index in range(total):
        if chunks[index][0] in halved:
            x_copy(index).start()

    def from_x(index):
        unit, rows = rows_of(index)
        if unit in halved:
            place = halved.index(unit)
            x_copy(index).wait_recv()
            crossed[place][rows, :] = add(own[unit][rows, :], crossed[place][rows, :], own[unit].dtype)

    @pl.when(is_end)
    def _():
        for index in range(total):
            from_x(index)
            a_copy(index).start()
        for index in range(total):
            a_copy(index).wait_send()

    @pl.when(is_middle)
    def _():
        lag = 2
        for index in range(total + lag):
            if index < total:
                unit, rows = rows_of(index)
                from_x(index)
                a_copy(index).wait_recv()
                inward[unit][rows, :] = add(mine(unit)[rows, :], inward[unit][rows, :], own[unit].dtype)
                b_copy(index).start()
            if index >= lag:
                late = index - lag
                unit, rows = rows_of(late)
                b_copy(late).wait_recv()
                outs[unit][rows, :] = add(inward[unit][rows, :], outs[unit][rows, :], outs[unit].dtype)
                c_copy(late).start()
        for index in range(total):
            b_copy(index).wait_send()
            c_copy(index).wait_send()

    @pl.when(is_end)
    def _():
        for index in range(total):
            c_copy(index).wait_recv()

    for index in range(total):
        if chunks[index][0] in halved:
            x_copy(index).wait_send()


def tail(arrays, far, fsdp_step, chunk_bytes=200 << 10):
    halved = tuple(sorted(far))
    chunks = []
    for unit, item in enumerate(arrays):
        rows, row_bytes = item.shape[0], item.shape[1] * item.dtype.itemsize
        pieces = 1
        while rows % (2 * pieces) == 0 and (rows // (2 * pieces)) % 16 == 0 and (
            rows // pieces * row_bytes > chunk_bytes
        ):
            pieces *= 2
        chunks += [(unit, step * (rows // pieces), rows // pieces) for step in range(pieces)]
    dma = pltpu.SemaphoreType.DMA
    buffers = [pltpu.VMEM(item.shape, item.dtype) for item in arrays]
    return pl.pallas_call(
        functools.partial(tail_kernel, tuple(chunks), halved, fsdp_step, "fsdp", len(arrays)),
        out_shape=[jax.ShapeDtypeStruct(item.shape, item.dtype) for item in arrays],
        in_specs=[spec(pltpu.VMEM)] * (len(arrays) + len(halved)),
        out_specs=[spec(pltpu.VMEM)] * len(arrays),
        scratch_shapes=buffers
        + [buffers[unit] for unit in halved]
        + [dma((len(chunks),))] * 8,
        compiler_params=pltpu.CompilerParams(
            vmem_limit_bytes=56 << 20, collective_id=2, has_side_effects=True
        ),
        name="tail",
    )(*arrays, *[far[unit] for unit in halved])


def small_sum_kernel(steps, fsdp_axis, value_ref, out_ref, held_ref, *refs):
    fsdp_refs, ctx_refs = refs[: len(steps)], refs[len(steps) : len(steps) + 3]
    send_sem, recv_sem = refs[len(steps) + 3 :]
    c = lax.axis_index("ctx")
    f = lax.axis_index(fsdp_axis)
    mesh_id = pl.DeviceIdType.MESH
    barrier = pltpu.get_barrier_semaphore()
    for step in steps:
        pl.semaphore_signal(barrier, inc=1, device_id={fsdp_axis: peer(f, step)}, device_id_type=mesh_id)
    for k in range(1, 4):
        pl.semaphore_signal(barrier, inc=1, device_id={"ctx": peer(c, k)}, device_id_type=mesh_id)
    pl.semaphore_wait(barrier, len(steps) + 3)
    total = value_ref[...]
    for index, step in enumerate(steps):
        held_ref[index] = total
        copy = pltpu.make_async_remote_copy(
            src_ref=held_ref.at[index],
            dst_ref=fsdp_refs[index],
            send_sem=send_sem.at[index],
            recv_sem=recv_sem.at[index],
            device_id={fsdp_axis: peer(f, step)},
            device_id_type=mesh_id,
        )
        copy.start()
        copy.wait()
        total = total + fsdp_refs[index][...]
    held_ref[len(steps)] = total
    copies = []
    for k in range(1, 4):
        copy = pltpu.make_async_remote_copy(
            src_ref=held_ref.at[len(steps)],
            dst_ref=ctx_refs[k - 1],
            send_sem=send_sem.at[len(steps) + k - 1],
            recv_sem=recv_sem.at[len(steps) + k - 1],
            device_id={"ctx": peer(c, k)},
            device_id_type=mesh_id,
        )
        copy.start()
        copies.append(copy)
    for copy in copies:
        copy.wait()
    near = total + ctx_refs[0][...]
    out_ref[...] = near + (ctx_refs[1][...] + ctx_refs[2][...])


def small_sum(values, steps):
    dma = pltpu.SemaphoreType.DMA
    return pl.pallas_call(
        functools.partial(small_sum_kernel, tuple(steps), "fsdp"),
        out_shape=jax.ShapeDtypeStruct(values.shape, values.dtype),
        in_specs=[spec(pltpu.VMEM)],
        out_specs=spec(pltpu.VMEM),
        scratch_shapes=[pltpu.VMEM((len(steps) + 1,) + values.shape, values.dtype)]
        + [pltpu.VMEM(values.shape, values.dtype)] * (len(steps) + 3)
        + [dma((len(steps) + 3,))] * 2,
        compiler_params=pltpu.CompilerParams(collective_id=3, has_side_effects=True),
        name="small_sum",
    )(values)


def norm_back(grad_normed, values, factor, gain_row):
    unit_rows = values * factor
    grad_gain = jnp.sum(grad_normed * unit_rows, axis=0)
    grad_unit = grad_normed * gain_row.astype(F32)
    inner_mean = jnp.mean(grad_unit * unit_rows, axis=-1, keepdims=True)
    return (factor * (grad_unit - unit_rows * inner_mean), grad_gain)


def swap(values, axis, size, step):
    return lax.ppermute(values, axis, [(i, i ^ step) for i in range(size)])


def halving(size):
    steps = []
    while size > 1:
        size //= 2
        steps.append(size)
    return steps


def shards(
    sizes,
    tokens,
    cotangent,
    seq_lengths,
    deal,
    norm_gains,
    query_key_value,
    forget_weight,
    forget_bias,
    out_weight,
    gate_up_weight,
    down_weight,
):
    fsdp, ctx, tp = sizes
    layer_count = query_key_value.shape[0]
    row_count, model_width = tokens.shape
    heads_here = forget_weight.shape[2]
    head_size = query_key_value.shape[3] // heads_here
    block_rows = row_count // 2
    piece = model_width // fsdp
    half_width = model_width // 2
    hp = -(-heads_here // ctx)
    heads_padded = hp * ctx
    width = heads_padded * head_size
    more_columns = (heads_padded - heads_here) * head_size
    qkv_columns = 3 * width + 128
    units = gate_up_weight.shape[3]
    unit_block = min(512, units)
    pack = Pack(hp, head_size)
    tiles = pack.tiles
    everything = (row_count, model_width)
    f_index = lax.axis_index("fsdp")
    c_index = lax.axis_index("ctx")
    t_index = lax.axis_index("tp")
    fsdp_steps = halving(fsdp)
    tp_steps = list(reversed(halving(tp)))
    offsets = [0]
    for step in fsdp_steps:
        offsets = offsets + [item ^ step for item in offsets]
    vmem, any_space = pltpu.VMEM, pltpu.HBM

    def add_low(left, right):
        return (left.astype(F32) + right.astype(F32)).astype(BF16)

    grads = {}
    tasks = {}
    pending = {}

    def gather_pieces(values):
        pieces = [values]
        for step in fsdp_steps[:-1]:
            for item in list(pieces):
                pieces.append((yield swap(item, "fsdp", fsdp, step)))
        return pieces

    def reduce_grad(near, far, axis, until):
        for step in reversed(fsdp_steps):
            near = add_low(near, (yield swap(far, "fsdp", fsdp, step)))
            if step != fsdp_steps[0]:
                size = near.shape[axis] // 2
                near, far = (
                    lax.slice_in_dim(near, 0, size, axis=axis),
                    lax.slice_in_dim(near, size, 2 * size, axis=axis),
                )
                if until == "core" and size == piece:
                    return near, far
        return near

    def begin(name, *args):
        tasks[name] = reduce_grad(*args)
        pending[name] = next(tasks[name])

    own_first = {}

    def begin_gather(name, values):
        tasks[name] = gather_pieces(values)
        own_first[name] = swap(values, "fsdp", fsdp, fsdp_steps[-1])
        pending[name] = next(tasks[name])

    def tick(values, names):
        names = [name for name in names if name in tasks]
        if not names:
            return values
        values, got = lax.optimization_barrier((values, [pending.pop(name) for name in names]))
        for name, item in zip(names, got):
            try:
                pending[name] = tasks[name].send(item)
            except StopIteration as end:
                grads[name] = end.value
                del tasks[name]
        return values

    def finished(name):
        while name in tasks:
            tick((), [name])
        return grads[name]

    def weight_pieces(name):
        pieces = finished(name)
        last = [own_first[name]] + [swap(item, "fsdp", fsdp, fsdp_steps[-1]) for item in pieces[1:]]
        return pieces + last

    def exchange(sends):
        return [sends[0]] + [swap(sends[k], "ctx", ctx, k) for k in range(1, ctx)]

    def to_local(values):
        return jnp.concatenate(
            [
                lax.dynamic_slice_in_dim(values, (f_index ^ item) * piece, piece, axis=1)
                for item in offsets
            ],
            axis=1,
        )

    def from_local(values):
        places = jnp.asarray([offsets.index(item) for item in range(fsdp)], jnp.int32)
        return jnp.concatenate(
            [
                lax.dynamic_slice_in_dim(values, places[f_index ^ item] * piece, piece, axis=1)
                for item in range(fsdp)
            ],
            axis=1,
        )

    def pick(items, index):
        out = items[0]
        for entry in range(1, len(items)):
            out = jnp.where(index == entry, items[entry], out)
        return out

    deal_order = deal[0]
    inverse = (
        jnp.zeros((2 * ctx,), jnp.int32).at[deal_order].set(jnp.arange(2 * ctx, dtype=jnp.int32))
    )
    seq_ends = jnp.cumsum(seq_lengths[0]).astype(jnp.int32)
    peers = jnp.bitwise_xor(jnp.arange(ctx, dtype=jnp.int32), c_index)
    blk = jnp.take(deal_order.reshape(ctx, 2), peers, axis=0).reshape(2 * ctx)
    place = 2 * jnp.bitwise_xor(inverse // 2, c_index) + inverse % 2

    def own_qkv(layer):
        parts = [jnp.pad(query_key_value[layer, j], ((0, 0), (0, more_columns))) for j in range(3)]
        last = jnp.concatenate(
            [
                jnp.pad(forget_weight[layer], ((0, 0), (0, heads_padded - heads_here))),
                norm_gains[layer].T,
                jnp.zeros((piece, 128 - heads_padded - 2), BF16),
            ],
            axis=1,
        )
        return with_layout_constraint(jnp.concatenate(parts + [last], axis=1), Layout((0, 1)))

    def gathered_gains(pieces):
        rows = jnp.concatenate(
            [item[:, 3 * width + heads_padded : 3 * width + heads_padded + 2] for item in pieces]
        )
        return [item[None] for item in rows.T.astype(F32)]

    share = model_width // tp

    def own_columns(values):
        values = lax.dynamic_slice_in_dim(values, t_index * share, share, axis=1).astype(BF16)
        return values.reshape(2, block_rows, share)

    def column_pieces(values):
        step = 1
        pieces = [values]
        while step < tp:
            pieces = pieces + [swap(item, "tp", tp, step) for item in pieces]
            step *= 2
        return pieces

    def all_columns(pieces):
        order = [0]
        step = 1
        while step < tp:
            order = order + [item ^ step for item in order]
            step *= 2
        stacked = jnp.concatenate(pieces, axis=1)
        places = jnp.asarray([order.index(item) for item in range(tp)], jnp.int32)
        return jnp.concatenate(
            [
                lax.dynamic_slice_in_dim(stacked, places[t_index ^ item] * share, share, axis=1)
                for item in range(tp)
            ],
            axis=1,
        )

    shard = own_qkv(0)
    begin_gather(("w_qkv", 0), shard)
    cot_blocks = own_columns(cotangent)
    late_side = (c_index >= ctx // 2).astype(jnp.int32)
    cot_sends = []
    for k in range(ctx):
        wanted = deal_order[2 * (c_index ^ k) + late_side]
        cot_sends.append(lax.dynamic_index_in_dim(cot_blocks, wanted % 2, 0, keepdims=False))
    cot_got = exchange(cot_sends)

    bias_all = jnp.pad(forget_bias.astype(F32), ((0, 0), (0, 128 - heads_here)))[:, None, :]
    own_weights = [
        {
            "w_units": gate_up_weight[layer],
            "w_back": jnp.concatenate(
                [jnp.pad(out_weight[layer], ((0, more_columns), (0, 0))), down_weight[layer]], axis=0
            ),
        }
        for layer in range(layer_count)
    ]
    for layer in range(1, layer_count):
        own_weights[layer]["w_qkv"] = own_qkv(layer)

    residual = to_local(tokens)
    own_weights, residual, cot_got = tick((own_weights, residual, cot_got), [("w_qkv", 0)])
    for name in ("w_back", "w_units"):
        begin_gather((name, 0), own_weights[0][name])
    cot_mine = jnp.concatenate(
        [pick(cot_got, (deal_order[2 * c_index + half] // 2) ^ c_index) for half in range(2)], axis=0
    )
    weights = [{"w_qkv": weight_pieces(("w_qkv", 0))}]
    gains = gathered_gains(weights[0]["w_qkv"])

    def piece_inputs(layer, *names):
        return {
            f"{name}_{index}": (item, any_space)
            for name in names
            for index, item in enumerate(weights[layer][name])
        }

    def packed_out():
        return ((ctx, tiles, 2, block_rows, 128), BF16, vmem)

    dma = pltpu.SemaphoreType.DMA
    mix = pltpu.VMEM((model_width, max(units, qkv_columns)), BF16)

    def project(layer, residual):
        out = named_call(
            functools.partial(first_kernel, pack, ctx, width),
            "project",
            {
                "residual": (residual, vmem),
                "gain": (gains[2 * layer], vmem),
                "bias": (bias_all[layer], vmem),
                **piece_inputs(layer, "w_qkv"),
            },
            {
                "normed": (everything, BF16, vmem),
                "packed": packed_out(),
                "logits": ((row_count, 128), F32, vmem),
                "stat": ((8, model_width), F32, vmem),
            },
            {"w_mix": pltpu.VMEM((model_width, qkv_columns), BF16), "sems": dma((fsdp,))},
            None,
        )
        stat_terms[layer][0] = jnp.sum(out["stat"][0])
        return out["normed"], out["packed"], out["logits"]

    stat_terms = [[None] * 3 for _ in range(layer_count)]
    normed_one, packed, logits = project(0, residual)
    kept = []
    for layer in range(layer_count):
        later = layer + 1
        last = later == layer_count
        rest = [(name, layer) for name in ("w_back", "w_units")]
        if layer == 0:
            packed, cot_mine = lax.optimization_barrier((packed, cot_mine))
        if last:
            cot_pieces = column_pieces(cot_mine)
        att, received, lse, att_turned = attend(pack, place, blk, seq_ends, packed)
        if last:
            att, cot_pieces = lax.optimization_barrier((att, cot_pieces))
            att = tick(att, rest)
        else:
            att, own_weights[later] = tick((att, own_weights[later]), rest)
            begin_gather(("w_qkv", later), own_weights[later]["w_qkv"])
            begin_gather(("w_back", later), own_weights[later]["w_back"])
        for item in rest:
            weights[layer][item[0]] = weight_pieces(item)
        inputs = {
            "att": (att, vmem),
            "residual": (residual, any_space),
            "gain_two": (gains[2 * layer + 1], vmem),
            **piece_inputs(layer, "w_back", "w_units"),
        }
        outputs = {
            "attended": ((row_count, width), BF16, vmem),
            "middle": (everything, F32, any_space),
            "normed_two": (everything, BF16, any_space),
            "gate": ((row_count, units), BF16, any_space),
            "up": ((row_count, units), BF16, any_space),
            "hidden": ((row_count, units), BF16, any_space),
            "after": (everything, F32, any_space),
            "stat": ((8, model_width), F32, vmem),
        }
        out = named_call(
            functools.partial(middle_kernel, pack, ctx, units, unit_block, tp_steps),
            "middle",
            inputs,
            outputs,
            {
                "w_o": pltpu.VMEM((width, model_width), BF16),
                "w_g": pltpu.VMEM((model_width, units), BF16),
                "w_mix": pltpu.VMEM((model_width, units), BF16),
                "w_d": pltpu.VMEM((units, model_width), BF16),
                "base": pltpu.VMEM(everything, F32),
                "after_keep": pltpu.VMEM(everything, F32),
                "normed_keep": pltpu.VMEM(everything, BF16),
                "gate_keep": pltpu.VMEM((row_count, units), BF16),
                "up_keep": pltpu.VMEM((row_count, units), BF16),
                "hidden_keep": pltpu.VMEM((row_count, units), BF16),
                "total": pltpu.VMEM((block_rows, model_width), F32),
                "sems": dma((5 * fsdp + 16,)),
                **pair_scratch(4, tp_steps, block_rows, model_width),
            },
            4,
        )
        kept.append(
            dict(
                residual=residual,
                normed_one=normed_one,
                logits=logits,
                received=received,
                lse=lse,
                att_turned=att_turned,
                **{
                    name: out[name] for name in ("attended", "middle", "normed_two", "gate", "up", "hidden")
                },
            )
        )
        stat_terms[layer][1] = jnp.sum(out["stat"][0])
        stat_terms[layer][2] = jnp.sum(out["stat"][1])
        residual = out["after"]
        if not last:
            residual, own_weights[later] = tick((residual, own_weights[later]), [("w_qkv", later)])
            begin_gather(("w_units", later), own_weights[later]["w_units"])
            weights.append({"w_qkv": weight_pieces(("w_qkv", later))})
            gains += gathered_gains(weights[later]["w_qkv"])
            normed_one, packed, logits = project(later, residual)

    final_blocks = own_columns(residual)
    out_got = exchange(
        [
            lax.dynamic_index_in_dim(
                final_blocks, ((c_index ^ k) >= ctx // 2).astype(jnp.int32), 0, keepdims=False
            )
            for k in range(ctx)
        ]
    )

    def halves(values):
        return values[:, :half_width], values[:, half_width:]

    def weight_grad(left, right):
        return lax.dot_general(left, right, (((0,), (0,)), ((), ())), preferred_element_type=F32).astype(BF16)

    gain_grads = [None] * (2 * layer_count)
    bias_grads = [None] * layer_count

    def back_call(layer, upper, grad_base, back_got):
        inputs, outputs, scratch = {}, {}, {"w_mix": mix, "sems": dma((5 * fsdp + 20,))}
        scratch["total"] = pltpu.VMEM((block_rows, model_width), F32)
        if upper is not None:
            inputs.update(
                back=(back_got, vmem), logits=(kept[upper]["logits"], vmem), **piece_inputs(upper, "w_qkv")
            )
            outputs.update(
                grads=((row_count, qkv_columns), BF16, any_space), bias_grad=((8, 128), F32, vmem)
            )
            scratch.update(grads_keep=pltpu.VMEM((row_count, qkv_columns), BF16))
            if layer is None:
                outputs.update(one_part=(everything, BF16, vmem))
            else:
                inputs.update(
                    residual=(kept[upper]["residual"], any_space), gain_one=(gains[2 * upper], vmem)
                )
        if layer is not None:
            state = kept[layer]
            inputs.update(
                base_in=(grad_base, any_space),
                middle=(state["middle"], any_space),
                gate=(state["gate"], any_space),
                up=(state["up"], any_space),
                gain_two=(gains[2 * layer + 1], vmem),
                **piece_inputs(layer, "w_back", "w_units"),
            )
            outputs.update(
                low=(everything, BF16, any_space),
                grad_gate=((row_count, units), BF16, any_space),
                grad_up=((row_count, units), BF16, any_space),
                grad=(everything, F32, any_space),
                branch=(everything, BF16, vmem),
                sends=((ctx, hp, block_rows, 128), BF16, vmem),
                gain_grad=((8, model_width), F32, vmem),
            )
            scratch.update(
                base=pltpu.VMEM(everything, grad_base.dtype),
                values=pltpu.VMEM(everything, F32),
                grad_keep=pltpu.VMEM(everything, F32),
                low_keep=pltpu.VMEM(everything, BF16),
                gate_keep=pltpu.VMEM((row_count, units), BF16),
                up_keep=pltpu.VMEM((row_count, units), BF16),
                turned=pltpu.VMEM((row_count, width), BF16),
                w_o=pltpu.VMEM((width, model_width), BF16),
                w_g=pltpu.VMEM((model_width, units), BF16),
                w_d=pltpu.VMEM((units, model_width), BF16),
                **pair_scratch(2 if upper is None else 4, tp_steps, block_rows, model_width),
            )
        return named_call(
            functools.partial(
                back_kernel,
                pack,
                ctx,
                width,
                units,
                unit_block,
                tp_steps,
                upper is not None,
                layer is not None,
            ),
            "back_top" if upper is None else "back_end" if layer is None else "back",
            inputs,
            outputs,
            scratch,
            None if layer is None else 6 if upper is None else 7,
        )

    def begin_qkv(layer, out):
        bias_grads[layer] = out["bias_grad"][0, :heads_here]
        begin(
            ("qkv", layer),
            *[weight_grad(part, out["grads"]) for part in halves(kept[layer]["normed_one"])],
            0,
            "core",
        )

    ffn = ("down", "gate", "up", "out")
    grad_base = to_local(all_columns(cot_pieces))
    back_got, upper = None, None
    for layer in reversed(range(layer_count)):
        state = kept[layer]
        out = back_call(layer, upper, grad_base, back_got)
        if upper is None:
            out, out_got = lax.optimization_barrier((out, out_got))
        else:
            out, (grads["down", upper],) = lax.optimization_barrier((out, background_down))
            background_gate = lax.psum([grads["gate", upper]], "ctx")
        if upper is not None:
            gain_grads[2 * upper] = out["gain_grad"][0]
            begin_qkv(upper, out)
        gain_grads[2 * layer + 1] = out["gain_grad"][1]
        grad_base = out["grad"]
        lefts = [state["hidden"], state["normed_two"], state["normed_two"], state["attended"]]
        rights = [out["low"], out["grad_gate"], out["grad_up"], out["branch"]]
        for name, left, right in zip(ffn, lefts, rights):
            if name in ("down", "out"):
                pairs = [weight_grad(left, part) for part in halves(right)]
            else:
                pairs = [weight_grad(part, right) for part in halves(left)]
            reach = "fsdp" if name in ("down", "gate") else "core"
            begin((name, layer), *pairs, 1 if name in ("down", "out") else 0, reach)
        sends = tick(out["sends"], [(name, layer) for name in ffn] + [("qkv", layer + 1)])
        if upper is None:
            mixed = jnp.concatenate(
                [pick(out_got, (inverse[2 * c_index + half] // 2) ^ c_index) for half in range(2)], axis=0
            )
            mixed_pieces = column_pieces(mixed)
        else:
            sends, (grads["gate", upper],) = lax.optimization_barrier((sends, background_gate))
        back_got = attend_back(
            pack, place, blk, seq_ends, state["received"], state["lse"], state["att_turned"], sends
        )
        back_got = tick(back_got, [(name, layer) for name in ffn] + [("qkv", layer + 1)])
        if upper is None:
            back_got, mixed_pieces = lax.optimization_barrier((back_got, mixed_pieces))
            mixed_out = from_local(all_columns(mixed_pieces)).astype(F32)
        if layer:
            background_down = lax.psum([grads["down", layer]], "ctx")
        upper = layer
    out = back_call(None, 0, None, back_got)
    begin_qkv(0, out)
    one_pairs = []
    for half in range(2):
        part = out["one_part"][half * block_rows : (half + 1) * block_rows]
        for step in tp_steps[:-1]:
            part = add_low(part, swap(part, "tp", tp, step))
        one_pairs.append((part, swap(part, "tp", tp, tp_steps[-1])))
    names = [(name, 0) for name in ("down", "gate")]
    arrays = [grads[name] for name in names]
    far_units = {}
    for name in [("up", 0), ("out", 0)] + [
        (name, layer) for layer in range(1, layer_count) for name in ("up", "out", "qkv")
    ] + [("qkv", 0)]:
        near, far = finished(name)
        far_units[len(arrays)] = far
        arrays.append(near)
        names.append(name)
    reduced = tail(arrays, far_units, fsdp_steps[0])
    one_pairs, reduced = lax.optimization_barrier((one_pairs, reduced))
    for name, item in zip(names, reduced):
        grads[name] = item
    grad_normed_one = jnp.concatenate(
        [left.astype(F32) + right.astype(F32) for left, right in one_pairs], axis=0
    )
    first = kept[0]["residual"]
    grad_from_one, gain_grads[0] = norm_back(grad_normed_one, first, unit_factor(first), gains[0])
    grad_tokens = from_local(grad_base + grad_from_one)

    small = jnp.concatenate(
        [from_local(jnp.stack(gain_grads)).reshape(-1), jnp.stack([item for row in stat_terms for item in row])]
        + bias_grads
    )
    used = small.shape[0]
    small = jnp.pad(small, (0, -used % 2048)).reshape(-1, 128)
    small = small_sum(small, list(reversed(fsdp_steps))).reshape(-1)
    gain_size = 2 * layer_count * model_width
    grad_gains = lax.dynamic_slice_in_dim(
        small[:gain_size].reshape(layer_count, 2, model_width), f_index * piece, piece, axis=2
    )
    stat_sums = small[gain_size : gain_size + 3 * layer_count].reshape(layer_count, 3)
    bias_sums = small[gain_size + 3 * layer_count : used].reshape(layer_count, heads_here)
    rms_values = jnp.sqrt(stat_sums / (row_count * model_width * fsdp * ctx))

    def both(pick_one):
        return jnp.stack([pick_one(layer).astype(F32) for layer in range(layer_count)])

    kept_columns = heads_here * head_size
    return (
        mixed_out,
        grad_tokens,
        grad_gains,
        both(
            lambda layer: jnp.stack(
                [grads["qkv", layer][:, j * width : j * width + kept_columns] for j in range(3)]
            )
        ),
        both(lambda layer: grads["qkv", layer][:, 3 * width : 3 * width + heads_here]),
        bias_sums,
        both(lambda layer: grads["out", layer][:kept_columns]),
        both(lambda layer: jnp.stack([grads["gate", layer], grads["up", layer]])),
        both(lambda layer: grads["down", layer]),
        rms_values,
    )


def solution(mesh):
    in_specs = (
        P(("fsdp", "ctx"), None),
        P(("fsdp", "ctx"), None),
        P("fsdp", None),
        P("fsdp", None),
        P(None, None, "fsdp"),
        P(None, None, "fsdp", "tp"),
        P(None, "fsdp", "tp"),
        P(None, "tp"),
        P(None, "tp", "fsdp"),
        P(None, None, "fsdp", "tp"),
        P(None, "tp", "fsdp"),
    )
    out_specs = (
        P(("fsdp", "ctx"), None),
        P(("fsdp", "ctx"), None),
        P(None, None, "fsdp"),
        P(None, None, "fsdp", "tp"),
        P(None, "fsdp", "tp"),
        P(None, "tp"),
        P(None, "tp", "fsdp"),
        P(None, None, "fsdp", "tp"),
        P(None, "tp", "fsdp"),
        P(),
    )
    sizes = (mesh.shape["fsdp"], mesh.shape["ctx"], mesh.shape["tp"])
    return jax.shard_map(
        functools.partial(shards, sizes),
        mesh=mesh,
        in_specs=in_specs,
        out_specs=out_specs,
        check_vma=False,
    )
```

```python
import functools
import math

import jax
import jax.numpy as jnp
from jax import lax
from jax.experimental import pallas as pl
from jax.experimental.layout import Layout, with_layout_constraint
from jax.experimental.pallas import tpu as pltpu
from jax.sharding import PartitionSpec as P

EPSILON = 1e-06
NEG_BIG = -1e30
FIRST_LENGTH = 1280
BF16 = jnp.bfloat16
F32 = jnp.float32


def matmul(left, right):
    return jnp.dot(left, right, preferred_element_type=F32)


def split_three(values):
    high = values.astype(BF16).astype(F32)
    rest = values - high
    middle = rest.astype(BF16).astype(F32)
    return high, middle, rest - middle


def iota(shape, dim):
    return lax.broadcasted_iota(jnp.int32, shape, dim)


def with_lanes(base, first, columns):
    lane = iota(base.shape, 1)
    for offset, column in enumerate(columns):
        base = jnp.where(lane == first + offset, column, base)
    return base


def with_rows(base, first, rows):
    row = iota(base.shape, 0)
    for offset, item in enumerate(rows):
        base = jnp.where(row == first + offset, item, base)
    return base


def first_lanes(values, lanes):
    return jnp.where(iota(values.shape, 1) < lanes, values, 0.0)


def widen(values, width=128):
    rows, lanes = values.shape
    return jnp.concatenate([values, jnp.zeros((rows, width - lanes), values.dtype)], axis=1)


class Pack:
    def __init__(self, hp, head_size):
        self.hp, self.head_size = hp, head_size
        self.value_tiles = (hp + 2) // 2
        self.tiles = hp + self.value_tiles

    def value_place(self, head):
        return self.hp + head // 2, (head % 2) * self.head_size


def peer(c, k):
    out, bit = c, 1
    while bit <= k:
        if k & bit:
            out = out + bit * (1 - 2 * ((c // bit) % 2))
        bit *= 2
    return out


def key_range(block, block_rows):
    first_blocks = FIRST_LENGTH // block_rows
    return (0 if block < first_blocks else first_blocks), block + 1


def score_tiles(block, block_rows, ends_ref):
    first, last = key_range(block, block_rows)
    if (block + 1) * block_rows <= FIRST_LENGTH:
        shape = (block_rows, block_rows)
        diagonal = (slice(block * block_rows, last * block_rows), iota(shape, 0) <= iota(shape, 1))
        if first == block:
            return [diagonal]
        return [(slice(first * block_rows, block * block_rows), None), diagonal]
    rows = (last - first) * block_rows
    key_pos = first * block_rows + iota((rows, 1), 0)
    query_pos = block * block_rows + iota((1, block_rows), 1)
    key_seq = jnp.zeros((rows, 1), jnp.int32)
    query_seq = jnp.zeros((1, block_rows), jnp.int32)
    for entry in range(ends_ref.shape[0]):
        key_seq = key_seq + (key_pos >= ends_ref[entry]).astype(jnp.int32)
        query_seq = query_seq + (query_pos >= ends_ref[entry]).astype(jnp.int32)
    mask = (key_pos <= query_pos) & (key_seq == query_seq)
    return [(slice(first * block_rows, last * block_rows), mask)]


def decay_blocks(load, block_count, block_rows):
    shape = (block_rows, block_rows)
    lower = (iota(shape, 0) >= iota(shape, 1)).astype(BF16)
    carry = None
    out = []
    for block in range(block_count):
        sums = matmul(lower, load(block))
        if carry is not None:
            sums = sums + carry
        carry = sums[block_rows - 1 : block_rows, :]
        out.append(sums)
    return out


def greet(count):
    c = lax.axis_index("ctx")
    barrier = pltpu.get_barrier_semaphore()
    for k in range(1, count):
        pl.semaphore_signal(
            barrier, inc=1, device_id={"ctx": peer(c, k)}, device_id_type=pl.DeviceIdType.MESH
        )
    pl.semaphore_wait(barrier, count - 1)
    return c


def move(k, c, source, target, send_sem, recv_sem):
    if k == 0:
        copy = pltpu.make_async_copy(source, target, recv_sem)
    else:
        copy = pltpu.make_async_remote_copy(
            src_ref=source,
            dst_ref=target,
            send_sem=send_sem,
            recv_sem=recv_sem,
            device_id={"ctx": peer(c, k)},
            device_id_type=pl.DeviceIdType.MESH,
        )
    copy.start()
    return copy


def arrive(k, copy):
    if k == 0:
        copy.wait()
    else:
        copy.wait_recv()


def attend_kernel(
    pack,
    place_ref,
    blk_ref,
    ends_ref,
    send_ref,
    out_ref,
    kept_ref,
    lse_ref,
    att_ref,
    key_ref,
    value_ref,
    block_ref,
    back_ref,
    in_send,
    in_recv,
    out_send,
    out_recv,
    keep_sem,
    *recv_refs,
):
    count = send_ref.shape[0]
    block_rows = send_ref.shape[3]
    block_count = 2 * count
    hp, head_size = pack.hp, pack.head_size
    scale = 1.0 / math.sqrt(head_size)
    c = greet(count)
    copies = {}
    order = [pack.value_place(hp)[0]]
    for head in range(hp):
        order += [item for item in (head, pack.value_place(head)[0]) if item not in order]
    for tile in order:
        for k in reversed(range(count)):
            copies[tile, k] = move(
                k,
                c,
                send_ref.at[k, tile],
                recv_refs[tile].at[pl.ds(2 * k, 2)],
                in_send.at[tile, k],
                in_recv.at[tile, k],
            )
    keeps = []
    here = set()

    def need(tile):
        if tile not in here:
            here.add(tile)
            for k in range(count):
                arrive(k, copies[tile, k])
            keep = pltpu.make_async_copy(recv_refs[tile], kept_ref.at[tile], keep_sem.at[tile])
            keep.start()
            keeps.append(keep)

    tile, lane = pack.value_place(hp)
    need(tile)
    decays = decay_blocks(
        lambda block: recv_refs[tile][place_ref[block]][:, lane : lane + head_size], block_count, block_rows
    )
    returns = []
    for head in range(hp):
        need(head)
        value_tile, value_lane = pack.value_place(head)
        need(value_tile)
        query_tiles = []
        for block in range(block_count):
            rows = slice(block * block_rows, (block + 1) * block_rows)
            pair = recv_refs[head][place_ref[block]].astype(F32)
            value = recv_refs[value_tile][place_ref[block]].astype(F32)
            value = value[:, value_lane : value_lane + head_size]
            high, middle, low = split_three(decays[block][:, head : head + 1])
            key_ref[rows, :] = with_lanes(
                widen(pair[:, head_size:]), head_size, (-high, -middle, -low, 1.0, 1.0, 1.0)
            ).astype(BF16)
            value_ref[:, rows] = with_lanes(widen(value), head_size, (1.0,)).T.astype(BF16)
            query_tiles.append(
                with_lanes(first_lanes(pair * scale, head_size), head_size, (1.0, 1.0, 1.0, high, middle, low))
                .T.astype(BF16)
            )
        for block in range(block_count):
            rows = slice(block * block_rows, (block + 1) * block_rows)
            tiles = []
            peak = None
            for key_rows, mask in score_tiles(block, block_rows, ends_ref):
                scores = matmul(key_ref[key_rows, :], query_tiles[block])
                if mask is not None:
                    scores = jnp.where(mask, scores, NEG_BIG)
                top = jnp.max(scores, axis=0, keepdims=True)
                peak = top if peak is None else jnp.maximum(peak, top)
                tiles.append((key_rows, scores))
            total = jnp.zeros((128, block_rows), F32)
            for key_rows, scores in tiles:
                total = total + matmul(value_ref[:, key_rows], jnp.exp(scores - peak).astype(BF16))
            exp_total = total[head_size : head_size + 1, :]
            attended = total * (1.0 / exp_total)
            att_ref[head, :, rows] = attended[:head_size, :]
            lse_ref[head, :, rows] = peak + jnp.log(exp_total)
            block_ref[head, block] = attended.T.astype(BF16)
        for k in range(count):
            back_ref[k, head] = jnp.concatenate(
                [
                    block_ref[head, blk_ref[2 * k]][:, :head_size],
                    block_ref[head, blk_ref[2 * k + 1]][:, :head_size],
                ],
                axis=1,
            )
        for k in reversed(range(count)):
            returns.append(
                (
                    k,
                    move(
                        k,
                        c,
                        back_ref.at[k, head],
                        out_ref.at[k, head],
                        out_send.at[k, head],
                        out_recv.at[k, head],
                    ),
                )
            )
    for k, copy in returns:
        copy.wait()
    for (tile, k), copy in copies.items():
        if k:
            copy.wait_send()
    for keep in keeps:
        keep.wait()


def attend_back_kernel(
    pack,
    place_ref,
    blk_ref,
    ends_ref,
    kept_ref,
    lse_ref,
    att_ref,
    send_ref,
    out_ref,
    key_ref,
    value_ref,
    turned_ref,
    plain_ref,
    grad_key_ref,
    grad_value_ref,
    decay_ref,
    block_ref,
    back_ref,
    in_send,
    in_recv,
    out_send,
    out_recv,
    *grad_refs,
):
    count = send_ref.shape[0]
    block_rows = send_ref.shape[2]
    block_count = 2 * count
    hp, head_size = pack.hp, pack.head_size
    scale = 1.0 / math.sqrt(head_size)
    c = greet(count)
    copies = {}
    for head in range(hp):
        for k in reversed(range(count)):
            copies[head, k] = move(
                k,
                c,
                send_ref.at[k, head],
                grad_refs[head].at[k],
                in_send.at[head, k],
                in_recv.at[head, k],
            )
    tile, lane = pack.value_place(hp)
    decays = decay_blocks(
        lambda block: kept_ref[tile, place_ref[block]][:, lane : lane + head_size], block_count, block_rows
    )
    returns = []

    def give(tile):
        for k in range(count):
            for half in range(2):
                back_ref[tile, k, half] = block_ref[tile, blk_ref[2 * k + half]]
        for k in reversed(range(count)):
            returns.append(
                move(
                    k,
                    c,
                    back_ref.at[tile, k],
                    out_ref.at[k, tile],
                    out_send.at[tile, k],
                    out_recv.at[tile, k],
                )
            )

    for head in range(hp):
        value_tile, value_lane = pack.value_place(head)
        query_tiles = []
        for block in range(block_count):
            rows = slice(block * block_rows, (block + 1) * block_rows)
            pair = kept_ref[head, place_ref[block]].astype(F32)
            value = kept_ref[value_tile, place_ref[block]].astype(F32)
            value = value[:, value_lane : value_lane + head_size]
            key = pair[:, head_size:]
            query = first_lanes(pair * scale, head_size)
            high, middle, low = split_three(decays[block][:, head : head + 1])
            key_ref[rows, :] = with_lanes(
                widen(key), head_size, (-high, -middle, -low, 1.0, 1.0, 1.0, 1.0, 1.0, 1.0)
            ).astype(BF16)
            turned_ref[:, rows] = with_lanes(widen(key), head_size, (1.0,)).T.astype(BF16)
            value_ref[rows, :] = with_lanes(widen(value), head_size, (1.0, 1.0, 1.0)).astype(BF16)
            plain_ref[rows, :] = with_lanes(query, head_size, (1.0,)).astype(BF16)
            query_wide = with_lanes(query, head_size, (1.0, 1.0, 1.0, high, middle, low)).T
            log_parts = [-part for part in split_three(lse_ref[head, :, rows])]
            query_tiles.append(with_rows(query_wide, head_size + 6, log_parts).astype(BF16))
        for k in range(count):
            arrive(k, copies[head, k])
        grad_plain = []
        grad_tiles = []
        for block in range(block_count):
            rows = slice(block * block_rows, (block + 1) * block_rows)
            place = place_ref[block]
            both = grad_refs[head][place // 2].astype(F32)
            grad = jnp.where(place % 2 == 0, both[:, :head_size], both[:, head_size:])
            grad_plain.append(grad.astype(BF16))
            grad_turned = widen(grad).T
            inner = jnp.sum(grad_turned[:head_size, :] * att_ref[head, :, rows], axis=0, keepdims=True)
            inner_parts = [-part for part in split_three(inner)]
            grad_tiles.append(with_rows(grad_turned, head_size, inner_parts).astype(BF16))
        query_grads = []
        for block in range(block_count):
            rows = slice(block * block_rows, (block + 1) * block_rows)
            grad_query = jnp.zeros((128, block_rows), F32)
            for key_rows, mask in score_tiles(block, block_rows, ends_ref):
                scores = matmul(key_ref[key_rows, :], query_tiles[block])
                if mask is not None:
                    scores = jnp.where(mask, scores, NEG_BIG)
                probs = jnp.exp(scores)
                grad_scores = (probs * matmul(value_ref[key_rows, :], grad_tiles[block])).astype(BF16)
                grad_query = grad_query + matmul(turned_ref[:, key_rows], grad_scores)
                add_key = matmul(grad_scores, plain_ref[rows, :])
                add_value = matmul(probs.astype(BF16), grad_plain[block])
                old = slice(key_rows.start, max(key_rows.start, rows.start))
                split = old.stop - old.start
                if split:
                    grad_key_ref[old, :] += add_key[:split]
                    grad_value_ref[old, :] += add_value[:split]
                if key_rows.stop == rows.stop:
                    grad_key_ref[rows, :] = add_key[split:]
                    grad_value_ref[rows, :] = add_value[split:]
            turned = grad_query.T
            query_grads.append((turned[:, :head_size] * scale).astype(BF16))
            decay_ref[rows, head : head + 1] = turned[:, head_size : head_size + 1]
        for block in range(block_count):
            rows = slice(block * block_rows, (block + 1) * block_rows)
            key_wide = grad_key_ref[rows, :]
            block_ref[head, block] = jnp.concatenate(
                [query_grads[block], key_wide[:, :head_size].astype(BF16)], axis=1
            )
            block_ref[value_tile, block, :, value_lane : value_lane + head_size] = grad_value_ref[
                rows, :
            ].astype(BF16)
            decay_ref[rows, head : head + 1] -= key_wide[:, head_size : head_size + 1]
        give(head)
        if value_lane and value_tile != tile:
            give(value_tile)
    shape = (block_rows, block_rows)
    upper = (iota(shape, 0) <= iota(shape, 1)).astype(BF16)
    carry = None
    for block in reversed(range(block_count)):
        rows = slice(block * block_rows, (block + 1) * block_rows)
        sums = jnp.zeros((block_rows, 128), F32)
        values = jnp.where(iota((block_rows, 128), 1) < hp, decay_ref[rows, :], 0.0)
        for part in split_three(values):
            sums = sums + matmul(upper, part.astype(BF16))
        if carry is not None:
            sums = sums + carry
        carry = sums[0:1, :]
        if lane == 0:
            block_ref[tile, block] = sums.astype(BF16)
        else:
            block_ref[tile, block, :, lane : lane + head_size] = sums[:, :head_size].astype(BF16)
    give(tile)
    for copy in returns:
        copy.wait()
    for (head, k), copy in copies.items():
        if k:
            copy.wait_send()


def spec(space):
    return pl.BlockSpec(memory_space=space)


def attend(pack, place, blk, ends, sends):
    count, tiles, _, block_rows, _ = sends.shape
    hp, head_size = pack.hp, pack.head_size
    pack_rows = 2 * count * block_rows
    dma = pltpu.SemaphoreType.DMA
    return pl.pallas_call(
        functools.partial(attend_kernel, pack),
        out_shape=[
            jax.ShapeDtypeStruct((count, hp, block_rows, 128), BF16),
            jax.ShapeDtypeStruct((tiles, 2 * count, block_rows, 128), BF16),
            jax.ShapeDtypeStruct((hp, 1, pack_rows), F32),
            jax.ShapeDtypeStruct((hp, head_size, pack_rows), F32),
        ],
        in_specs=[spec(pltpu.SMEM)] * 3 + [spec(pl.ANY)],
        out_specs=[spec(pl.ANY), spec(pl.ANY), spec(pltpu.VMEM), spec(pltpu.VMEM)],
        scratch_shapes=[
            pltpu.VMEM((pack_rows, 128), BF16),
            pltpu.VMEM((128, pack_rows), BF16),
            pltpu.VMEM((hp, 2 * count, block_rows, 128), BF16),
            pltpu.VMEM((count, hp, block_rows, 128), BF16),
            dma((tiles, count)),
            dma((tiles, count)),
            dma((count, hp)),
            dma((count, hp)),
            dma((tiles,)),
        ]
        + [pltpu.VMEM((2 * count, block_rows, 128), BF16)] * tiles,
        compiler_params=pltpu.CompilerParams(
            vmem_limit_bytes=40 << 20, collective_id=0, has_side_effects=True
        ),
        name="attend",
    )(place, blk, ends, sends)


def attend_back(pack, place, blk, ends, kept, lse, att, sends):
    count, hp, block_rows, _ = sends.shape
    tiles = kept.shape[0]
    head_size = pack.head_size
    pack_rows = 2 * count * block_rows
    dma = pltpu.SemaphoreType.DMA
    return pl.pallas_call(
        functools.partial(attend_back_kernel, pack),
        out_shape=jax.ShapeDtypeStruct((count, tiles, 2, block_rows, 128), BF16),
        in_specs=[spec(pltpu.SMEM)] * 3 + [spec(pltpu.VMEM)] * 3 + [spec(pl.ANY)],
        out_specs=spec(pl.ANY),
        scratch_shapes=[
            pltpu.VMEM((pack_rows, 128), BF16),
            pltpu.VMEM((pack_rows, 128), BF16),
            pltpu.VMEM((128, pack_rows), BF16),
            pltpu.VMEM((pack_rows, 128), BF16),
            pltpu.VMEM((pack_rows, 128), F32),
            pltpu.VMEM((pack_rows, head_size), F32),
            pltpu.VMEM((pack_rows, 128), F32),
            pltpu.VMEM((tiles, 2 * count, block_rows, 128), BF16),
            pltpu.VMEM((tiles, count, 2, block_rows, 128), BF16),
            dma((hp, count)),
            dma((hp, count)),
            dma((tiles, count)),
            dma((tiles, count)),
        ]
        + [pltpu.VMEM((count, block_rows, 128), BF16)] * hp,
        compiler_params=pltpu.CompilerParams(
            vmem_limit_bytes=40 << 20, collective_id=1, has_side_effects=True
        ),
        name="attend_back",
    )(place, blk, ends, kept, lse, att, sends)


VMEM_BYTES = 60 << 20


def turned_matmul(left, right):
    return lax.dot_general(left, right, (((1,), (1,)), ((), ())), preferred_element_type=F32)


def column_sums(values):
    return jnp.sum(values, axis=0, keepdims=True)


def unit_factor(values):
    return lax.rsqrt(jnp.mean(values * values, axis=-1, keepdims=True) + EPSILON)


def norm_rows_back(grad_normed, values, gain):
    factor = unit_factor(values)
    unit = values * factor
    grad_unit = grad_normed * gain
    inner = jnp.mean(grad_unit * unit, axis=-1, keepdims=True)
    return factor * (grad_unit - unit * inner), column_sums(grad_normed * unit)


class Refs:
    def __init__(self, names, refs):
        for name, ref in zip(names, refs, strict=True):
            setattr(self, name, ref)

    def pieces(self, name):
        out = []
        while hasattr(self, f"{name}_{len(out)}"):
            out.append(getattr(self, f"{name}_{len(out)}"))
        return out


def named_call(kernel, name, inputs, outputs, scratch, collective_id):
    names = list(inputs) + list(outputs) + list(scratch)

    def body(*refs):
        kernel(Refs(names, refs))

    params = dict(vmem_limit_bytes=VMEM_BYTES)
    if collective_id is not None:
        params.update(collective_id=collective_id, has_side_effects=True)
    out = pl.pallas_call(
        body,
        out_shape=[jax.ShapeDtypeStruct(shape, kind) for shape, kind, _ in outputs.values()],
        in_specs=[spec(space) for _, space in inputs.values()],
        out_specs=[spec(space) for _, _, space in outputs.values()],
        scratch_shapes=list(scratch.values()),
        compiler_params=pltpu.CompilerParams(**params),
        name=name,
    )(*[array for array, _ in inputs.values()])
    return dict(zip(outputs, out))


class Copies:
    def __init__(self, sems):
        self.sems, self.used, self.saves = sems, 0, []

    def load(self, source, target):
        copy = pltpu.make_async_copy(source, target, self.sems.at[self.used])
        self.used += 1
        copy.start()
        return copy

    def load_down(self, pieces, target, columns=None):
        rows = pieces[0].shape[0]
        out = []
        for index, item in enumerate(pieces):
            place = target.at[pl.ds(index * rows, rows)]
            if columns is not None:
                place = target.at[pl.ds(index * rows, rows), pl.ds(0, columns)]
            out.append(self.load(item, place))
        return out

    def load_beside(self, pieces, target):
        columns = pieces[0].shape[1]
        return [
            self.load(item, target.at[:, pl.ds(index * columns, columns)])
            for index, item in enumerate(pieces)
        ]

    def save(self, source, target):
        self.saves.append(self.load(source, target))

    def finish(self):
        for copy in self.saves:
            copy.wait()


class PairSums:
    def __init__(self, steps, send_refs, recv_refs, send_sem, recv_sem):
        self.steps, self.send_refs, self.recv_refs = steps, send_refs, recv_refs
        self.send_sem, self.recv_sem = send_sem, recv_sem
        self.t = lax.axis_index("tp")
        self.started = []

    def greet(self, also=()):
        barrier = pltpu.get_barrier_semaphore()
        for place in also:
            pl.semaphore_signal(barrier, inc=1, device_id=place, device_id_type=pl.DeviceIdType.MESH)
        for step in self.steps:
            pl.semaphore_signal(
                barrier, inc=1, device_id={"tp": peer(self.t, step)}, device_id_type=pl.DeviceIdType.MESH
            )
        pl.semaphore_wait(barrier, len(self.steps) + len(also))

    def copy(self, index):
        copy = pltpu.make_async_remote_copy(
            src_ref=self.send_refs[index],
            dst_ref=self.recv_refs[index],
            send_sem=self.send_sem.at[index],
            recv_sem=self.recv_sem.at[index],
            device_id={"tp": peer(self.t, self.steps[index % len(self.steps)])},
            device_id_type=pl.DeviceIdType.MESH,
        )
        copy.start()
        self.started.append(copy)
        return copy

    def start(self, place):
        self.first = getattr(self, "first", {})
        self.first[place] = self.copy(place * len(self.steps))

    def finish(self, place):
        copy = self.first[place]
        base = place * len(self.steps)
        for offset in range(len(self.steps)):
            if offset:
                self.send_refs[base + offset][...] = total.astype(BF16)
                copy = self.copy(base + offset)
            copy.wait_recv()
            total = self.send_refs[base + offset][...].astype(F32) + self.recv_refs[base + offset][
                ...
            ].astype(F32)
        return total

    def end(self):
        for copy in self.started:
            copy.wait_send()


def pair_scratch(places, steps, rows, columns):
    count = places * len(steps)
    buffers = {f"send{index}": pltpu.VMEM((rows, columns), BF16) for index in range(count)}
    buffers.update({f"recv{index}": pltpu.VMEM((rows, columns), BF16) for index in range(count)})
    buffers["pair_send"] = pltpu.SemaphoreType.DMA((count,))
    buffers["pair_recv"] = pltpu.SemaphoreType.DMA((count,))
    return buffers


def pair_sums(r, places, steps):
    count = places * len(steps)
    return PairSums(
        steps,
        [getattr(r, f"send{index}") for index in range(count)],
        [getattr(r, f"recv{index}") for index in range(count)],
        r.pair_send,
        r.pair_recv,
    )


def over_units(units, block, body):
    def step(index, carry):
        body(pl.ds(pl.multiple_of(index * block, block), block))
        return carry

    lax.fori_loop(0, units // block, step, 0)


def tile_columns(pack, item, head):
    first = (item * pack.hp + head) * pack.head_size
    return slice(first, first + pack.head_size)


def write_tiles(pack, count, packed_ref, half, query, key, value, forget):
    size = pack.head_size
    forget_tile, forget_lane = pack.value_place(pack.hp)
    lane = iota(forget.shape, 1)
    for item in range(count):
        target = peer(lax.axis_index("ctx"), item)
        for head in range(pack.hp):
            columns = tile_columns(pack, item, head)
            packed_ref[target, head, half] = jnp.concatenate([query[:, columns], key[:, columns]], axis=1)
        shift = (forget_lane - item * pack.hp) % 128
        moved = pltpu.roll(forget, shift, 1) if shift else forget
        moved = jnp.where((lane >= forget_lane) & (lane < forget_lane + pack.hp), moved, 0.0)
        for tile in range(pack.hp, pack.tiles):
            parts = []
            for slot in range(2):
                head = 2 * (tile - pack.hp) + slot
                if head < pack.hp:
                    parts.append(value[:, tile_columns(pack, item, head)])
                else:
                    parts.append(moved[:, slot * size : (slot + 1) * size].astype(BF16))
            packed_ref[target, tile, half] = jnp.concatenate(parts, axis=1)


def project_rows(pack, r, count, width, half, rows, normed):
    def part(first, size):
        return matmul(normed, r.w_mix[:, first : first + size])

    query, key, value = [part(index * width, width).astype(BF16) for index in range(3)]
    logits = part(3 * width, 128) + r.bias[...]
    r.logits[rows, :] = logits
    forget = jnp.minimum(logits, 0.0) - jnp.log1p(jnp.exp(-jnp.abs(logits)))
    forget = forget.astype(BF16).astype(F32)
    write_tiles(pack, count, r.packed, half, query, key, value, forget)


def first_kernel(pack, count, width, r):
    copies = Copies(r.sems)
    c = lax.axis_index("ctx")
    block_rows = r.packed.shape[3]
    for copy in copies.load_down(r.pieces("w_qkv"), r.w_mix):
        copy.wait()
    turned = r.w_mix[:, 3 * width :].astype(F32).T
    first = count * pack.hp
    r.gains[0:2, :] = turned[first : first + 2, :]
    for half in range(2):
        rows = slice(half * block_rows, (half + 1) * block_rows)
        residual = r.residual[rows, :]
        normed = (residual * unit_factor(residual) * r.gains[0:1, :]).astype(BF16)
        r.normed[rows, :] = normed
        add = column_sums(residual * residual)
        r.stat[...] = jnp.broadcast_to(add if half == 0 else add + r.stat[0:1, :], r.stat.shape)
        project_rows(pack, r, count, width, half, rows, normed)


def middle_kernel(pack, count, units, unit_block, steps, fsdp, r):
    copies = Copies(r.sems)
    c = lax.axis_index("ctx")
    sums = pair_sums(r, 4, steps)
    block_rows = r.attended.shape[0] // 2
    f = lax.axis_index("fsdp")
    other = {"fsdp": peer(f, 1)}
    width = r.w_o.shape[0]
    back, ffn = r.pieces("w_back"), r.pieces("w_units")
    load_out = copies.load_beside([item.at[pl.ds(0, width)] for item in back], r.w_o)
    load_base = copies.load(r.residual, r.base)
    load_units = copies.load_down([item.at[0] for item in ffn], r.w_g)
    load_units += copies.load_down([item.at[1] for item in ffn], r.w_mix)
    load_units += copies.load_beside([item.at[pl.ds(width, units)] for item in back], r.w_d)
    sums.greet([other])
    piece = back[0].shape[1]
    crossing = []
    for index in range(1, fsdp // 2):
        place = pl.ds((fsdp // 2 + index) * piece, piece)
        pairs = [
            (back[index].at[pl.ds(0, width)], r.w_o.at[:, place]),
            (ffn[index].at[0], r.w_g.at[place]),
            (ffn[index].at[1], r.w_mix.at[place]),
            (back[index].at[pl.ds(width, units)], r.w_d.at[:, place]),
        ]
        for source, target in pairs:
            copy = pltpu.make_async_remote_copy(
                src_ref=source,
                dst_ref=target,
                send_sem=r.core_send.at[len(crossing)],
                recv_sem=r.core_recv.at[len(crossing)],
                device_id=other,
                device_id_type=pl.DeviceIdType.MESH,
            )
            copy.start()
            crossing.append(copy)
    for copy in load_out:
        copy.wait()
    for copy in crossing[::4]:
        copy.wait_recv()
    halves = [slice(half * block_rows, (half + 1) * block_rows) for half in range(2)]
    size = pack.head_size
    for half, rows in enumerate(halves):
        columns = []
        for item in range(count):
            for head in range(pack.hp):
                columns.append(r.att[peer(c, item), head][:, half * size : (half + 1) * size])
        attended = jnp.concatenate(columns, axis=1)
        r.attended[rows, :] = attended
        sums.send_refs[half * len(steps)][...] = matmul(attended, r.w_o[...]).astype(BF16)
        sums.start(half)
    load_base.wait()
    for copy in load_units:
        copy.wait()
    for index, copy in enumerate(crossing):
        if index % 4:
            copy.wait_recv()
    for half, rows in enumerate(halves):
        branch = sums.finish(half)
        add = column_sums(branch * branch)
        r.stat[0:1, :] = add if half == 0 else r.stat[0:1, :] + add
        middle = r.base[rows, :] + branch
        r.base[rows, :] = middle
        copies.save(r.base.at[rows], r.middle.at[rows])
        normed = (middle * unit_factor(middle) * r.gains[1:2, :]).astype(BF16)
        r.normed_keep[rows, :] = normed
        copies.save(r.normed_keep.at[rows], r.normed_two.at[rows])
        r.total[...] = jnp.zeros(r.total.shape, F32)

        def block(columns, rows=rows):
            gate = matmul(r.normed_keep[rows, :], r.w_g[:, columns])
            up = matmul(r.normed_keep[rows, :], r.w_mix[:, columns])
            hidden = (gate * jax.nn.sigmoid(gate) * up).astype(BF16)
            r.gate_keep[rows, columns] = gate.astype(BF16)
            r.up_keep[rows, columns] = up.astype(BF16)
            r.hidden_keep[rows, columns] = hidden
            r.total[...] += matmul(hidden, r.w_d[columns, :])

        over_units(units, unit_block, block)
        sums.send_refs[(2 + half) * len(steps)][...] = r.total[...].astype(BF16)
        sums.start(2 + half)
        copies.save(r.gate_keep.at[rows], r.gate.at[rows])
        copies.save(r.up_keep.at[rows], r.up.at[rows])
        copies.save(r.hidden_keep.at[rows], r.hidden.at[rows])
    for half, rows in enumerate(halves):
        branch = sums.finish(2 + half)
        add = column_sums(branch * branch)
        r.stat[1:2, :] = add if half == 0 else r.stat[1:2, :] + add
        residual = r.base[rows, :] + branch
        r.after_keep[rows, :] = residual
        copies.save(r.after_keep.at[rows], r.after.at[rows])
    copies.finish()
    sums.end()
    for copy in crossing:
        copy.wait_send()


def back_kernel(pack, count, width, units, unit_block, steps, upper, feed, r):
    copies = Copies(r.sems)
    c = lax.axis_index("ctx")
    size = pack.head_size
    forget_tile, forget_lane = pack.value_place(pack.hp)
    if feed:
        sums = pair_sums(r, 4 if upper else 2, steps)
        second = 2 if upper else 0
    block_rows = r.total.shape[0]
    halves = [slice(half * block_rows, (half + 1) * block_rows) for half in range(2)]
    if upper:
        load_qkv = copies.load_down(r.pieces("w_qkv"), r.w_mix, 3 * width + 128)
    if feed:
        if upper:
            load_value = [copies.load(r.residual.at[rows], r.values.at[rows]) for rows in halves]
        load_base = copies.load(r.base_in, r.base)
        waits = [copies.load(r.gate, r.gate_keep), copies.load(r.up, r.up_keep)]
        waits += copies.load_beside(
        [item.at[pl.ds(r.w_o.shape[0], units)] for item in r.pieces("w_back")], r.w_d
    )
        waits += copies.load_down([item.at[0] for item in r.pieces("w_units")], r.w_g)
        load_out = copies.load_beside([item.at[pl.ds(0, r.w_o.shape[0])] for item in r.pieces("w_back")], r.w_o)
        sums.greet()

    if upper:
        for copy in load_qkv:
            copy.wait()
        for half, rows in enumerate(halves):
            columns = [[], [], []]
            forget = jnp.zeros((block_rows, 128), F32)
            lane = iota(forget.shape, 1)
            for item in range(count):
                source = peer(c, item)
                for head in range(pack.hp):
                    pair = r.back[source, head, half]
                    columns[0].append(pair[:, :size])
                    columns[1].append(pair[:, size:])
                    value_tile, value_lane = pack.value_place(head)
                    columns[2].append(r.back[source, value_tile, half][:, value_lane : value_lane + size])
                wide = r.back[source, forget_tile, half].astype(F32)
                shift = (item * pack.hp - forget_lane) % 128
                moved = pltpu.roll(wide, shift, 1) if shift else wide
                first = item * pack.hp
                forget = jnp.where((lane >= first) & (lane < first + pack.hp), moved, forget)
            grad_logits = (forget * jax.nn.sigmoid(-r.logits[rows, :])).astype(BF16)
            add = column_sums(grad_logits.astype(F32))
            r.bias_grad[...] = jnp.broadcast_to(
                add if half == 0 else add + r.bias_grad[0:1, :], r.bias_grad.shape
            )
            for index in range(3):
                r.grads_keep[rows, index * width : (index + 1) * width] = jnp.concatenate(
                    columns[index], axis=1
                )
            r.grads_keep[rows, 3 * width :] = grad_logits
            copies.save(r.grads_keep.at[rows], r.grads.at[rows])
            grads = r.grads_keep[rows, :]
            part = turned_matmul(grads, r.w_mix[:, : 3 * width + 128]).astype(BF16)
            if feed:
                sums.send_refs[half * len(steps)][...] = part
                sums.start(half)
            else:
                r.one_part[rows, :] = part
    if feed:
        waits += copies.load_down([item.at[1] for item in r.pieces("w_units")], r.w_mix, units)
        load_base.wait()
        load_middle = []
        for half, rows in enumerate(halves):
            grad = r.base[rows, :].astype(F32)
            if upper:
                load_value[half].wait()
                back, add = norm_rows_back(sums.finish(half), r.values[rows, :], r.upper_gains[0:1, :])
                r.gain_grad[0:1, :] = add if half == 0 else r.gain_grad[0:1, :] + add
                grad = grad + back
            load_middle.append(copies.load(r.middle.at[rows], r.values.at[rows]))
            r.grad_keep[rows, :] = grad
            r.low_keep[rows, :] = grad.astype(BF16)
            copies.save(r.low_keep.at[rows], r.low.at[rows])
            for copy in waits:
                copy.wait()
            waits = []
            r.total[...] = jnp.zeros(r.total.shape, F32)

            def block(columns, rows=rows):
                grad_hidden = turned_matmul(r.low_keep[rows, :], r.w_d[columns, :])
                gate = r.gate_keep[rows, columns].astype(F32)
                up = r.up_keep[rows, columns].astype(F32)
                sigmoid = jax.nn.sigmoid(gate)
                grad_gate = (grad_hidden * up * sigmoid * (1.0 + gate * (1.0 - sigmoid))).astype(BF16)
                grad_up = (grad_hidden * gate * sigmoid).astype(BF16)
                r.gate_keep[rows, columns] = grad_gate
                r.up_keep[rows, columns] = grad_up
                r.total[...] += turned_matmul(grad_gate, r.w_g[:, columns]) + turned_matmul(
                    grad_up, r.w_mix[:, columns]
                )

            over_units(units, unit_block, block)
            sums.send_refs[(second + half) * len(steps)][...] = r.total[...].astype(BF16)
            sums.start(second + half)
            copies.save(r.gate_keep.at[rows], r.grad_gate.at[rows])
            copies.save(r.up_keep.at[rows], r.grad_up.at[rows])
        for copy in load_out:
            copy.wait()
        for half, rows in enumerate(halves):
            load_middle[half].wait()
            back, add = norm_rows_back(sums.finish(second + half), r.values[rows, :], r.gains[1:2, :])
            r.gain_grad[1:2, :] = add if half == 0 else r.gain_grad[1:2, :] + add
            grad = r.grad_keep[rows, :] + back
            r.grad_keep[rows, :] = grad
            copies.save(r.grad_keep.at[rows], r.grad.at[rows])
            low = grad.astype(BF16)
            r.branch[rows, :] = low
            r.turned[rows, :] = turned_matmul(low, r.w_o[...]).astype(BF16)
        for item in range(count):
            for head in range(pack.hp):
                columns = tile_columns(pack, item, head)
                r.sends[peer(c, item), head] = jnp.concatenate(
                    [r.turned[rows, columns] for rows in halves], axis=1
                )
    copies.finish()
    if feed:
        sums.end()


def tail_kernel(chunks, given, halved, fsdp_step, fsdp_axis, units, *refs):
    own, rest = refs[:units], refs[units:]
    arrived, rest = rest[: len(given)], rest[len(given) :]
    apart = [unit for unit, place in halved.items() if place is not None]
    far, rest = rest[: len(apart)], rest[len(apart) :]
    outs, rest = rest[:units], rest[units:]
    inward, rest = rest[:units], rest[units:]
    held, rest = rest[:units], rest[units:]
    total_refs, rest = rest[:units], rest[units:]
    first_refs, rest = rest[: len(given) + len(halved)], rest[len(given) + len(halved) :]
    load_sem, save_sem, x_send, x_recv, a_send, a_recv, b_send, b_recv, c_send, c_recv = rest
    extra = {unit: first_refs[place] for place, unit in enumerate(list(given) + list(halved))}
    c = lax.axis_index("ctx")
    f = lax.axis_index(fsdp_axis)
    mesh_id = pl.DeviceIdType.MESH
    loads = {}
    for unit in range(units):
        rows = held[unit].shape[0]
        loads[unit] = [
            pltpu.make_async_copy(own[unit].at[pl.ds(0, rows)], held[unit], load_sem.at[unit])
        ]
        if unit in given:
            place = given.index(unit)
            loads[unit].append(
                pltpu.make_async_copy(arrived[place], extra[unit], load_sem.at[units + place])
            )
        for copy in loads[unit]:
            copy.start()
    barrier = pltpu.get_barrier_semaphore()
    pl.semaphore_signal(
        barrier, inc=1, device_id={fsdp_axis: peer(f, fsdp_step)}, device_id_type=mesh_id
    )
    for k in range(1, 4):
        pl.semaphore_signal(barrier, inc=1, device_id={"ctx": peer(c, k)}, device_id_type=mesh_id)
    pl.semaphore_wait(barrier, 4)
    is_end = c * (3 - c) == 0
    is_middle = c * (3 - c) != 0

    def remote(source, target, send, recv, where):
        return pltpu.make_async_remote_copy(
            src_ref=source,
            dst_ref=target,
            send_sem=send,
            recv_sem=recv,
            device_id=where,
            device_id_type=mesh_id,
        )

    def rows_of(index):
        unit, first, count = chunks[index]
        return unit, pl.ds(first, count)

    def x_copy(index):
        unit, first, count = chunks[index]
        if unit in apart:
            source = far[apart.index(unit)].at[pl.ds(first, count)]
        else:
            source = own[unit].at[pl.ds(held[unit].shape[0] + first, count)]
        return remote(
            source,
            extra[unit].at[pl.ds(first, count)],
            x_send.at[index],
            x_recv.at[index],
            {fsdp_axis: peer(f, fsdp_step)},
        )

    def a_copy(index):
        unit, rows = rows_of(index)
        return remote(
            held[unit].at[rows], inward[unit].at[rows], a_send.at[index], a_recv.at[index], {"ctx": 1 + c // 2}
        )

    def b_copy(index):
        unit, rows = rows_of(index)
        return remote(
            inward[unit].at[rows], total_refs[unit].at[rows], b_send.at[index], b_recv.at[index], {"ctx": 3 - c}
        )

    def c_copy(index):
        unit, rows = rows_of(index)
        return remote(
            total_refs[unit].at[rows],
            total_refs[unit].at[rows],
            c_send.at[index],
            c_recv.at[index],
            {"ctx": 3 * (c - 1)},
        )

    def add(left, right, kind):
        return (left.astype(F32) + right.astype(F32)).astype(kind)

    def is_first(index):
        return chunks[index][1] == 0

    def is_last(index):
        return index + 1 == total or chunks[index + 1][0] != chunks[index][0]

    def save(unit):
        return pltpu.make_async_copy(total_refs[unit], outs[unit], save_sem.at[unit])

    total = len(chunks)
    for index in range(total):
        if chunks[index][0] in halved:
            x_copy(index).start()

    def ready(index):
        unit, rows = rows_of(index)
        if is_first(index):
            for copy in loads[unit]:
                copy.wait()
        if unit in halved:
            x_copy(index).wait_recv()
        if unit in extra:
            held[unit][rows, :] = add(held[unit][rows, :], extra[unit][rows, :], held[unit].dtype)

    @pl.when(is_end)
    def _():
        for index in range(total):
            ready(index)
            a_copy(index).start()
        for index in range(total):
            c_copy(index).wait_recv()
            if is_last(index):
                save(chunks[index][0]).start()
        for index in range(total):
            a_copy(index).wait_send()

    @pl.when(is_middle)
    def _():
        lag = 2
        for index in range(total + lag):
            if index < total:
                unit, rows = rows_of(index)
                ready(index)
                a_copy(index).wait_recv()
                inward[unit][rows, :] = add(held[unit][rows, :], inward[unit][rows, :], held[unit].dtype)
                b_copy(index).start()
            if index >= lag:
                late = index - lag
                unit, rows = rows_of(late)
                b_copy(late).wait_recv()
                total_refs[unit][rows, :] = add(
                    inward[unit][rows, :], total_refs[unit][rows, :], held[unit].dtype
                )
                c_copy(late).start()
                if is_last(late):
                    save(unit).start()
        for index in range(total):
            b_copy(index).wait_send()
            c_copy(index).wait_send()

    for unit in range(units):
        save(unit).wait()
    for index in range(total):
        if chunks[index][0] in halved:
            x_copy(index).wait_send()


def tail(arrays, given, far, fsdp_step, chunk_bytes=128 << 10):
    ready = tuple(sorted(given))
    apart = [unit for unit in sorted(far) if far[unit] is not None]
    halved = {unit: (apart.index(unit) if unit in apart else None) for unit in sorted(far)}
    shapes = [
        (item.shape[0] // (2 if unit in halved and unit not in apart else 1), item.shape[1])
        for unit, item in enumerate(arrays)
    ]
    chunks = []
    for unit, (rows, columns) in enumerate(shapes):
        row_bytes = columns * arrays[unit].dtype.itemsize
        pieces = 1
        while rows % (2 * pieces) == 0 and (rows // (2 * pieces)) % 16 == 0 and (
            rows // pieces * row_bytes > chunk_bytes
        ):
            pieces *= 2
        chunks += [(unit, step * (rows // pieces), rows // pieces) for step in range(pieces)]
    dma = pltpu.SemaphoreType.DMA
    buffers = [pltpu.VMEM(shape, item.dtype) for shape, item in zip(shapes, arrays)]
    inputs = list(arrays) + [given[unit] for unit in ready] + [far[unit] for unit in apart]
    return pl.pallas_call(
        functools.partial(tail_kernel, tuple(chunks), ready, halved, fsdp_step, "fsdp", len(arrays)),
        out_shape=[jax.ShapeDtypeStruct(shape, item.dtype) for shape, item in zip(shapes, arrays)],
        in_specs=[spec(pltpu.HBM)] * len(inputs),
        out_specs=[spec(pltpu.HBM)] * len(arrays),
        scratch_shapes=buffers * 3
        + [buffers[unit] for unit in list(ready) + list(halved)]
        + [dma((len(arrays) + len(ready),)), dma((len(arrays),))]
        + [dma((len(chunks),))] * 8,
        compiler_params=pltpu.CompilerParams(
            vmem_limit_bytes=60 << 20, collective_id=2, has_side_effects=True
        ),
        name="tail",
    )(*inputs)


def small_sum_kernel(steps, fsdp_axis, value_ref, out_ref, held_ref, *refs):
    fsdp_refs, ctx_refs = refs[: len(steps)], refs[len(steps) : len(steps) + 3]
    send_sem, recv_sem = refs[len(steps) + 3 :]
    c = lax.axis_index("ctx")
    f = lax.axis_index(fsdp_axis)
    mesh_id = pl.DeviceIdType.MESH
    barrier = pltpu.get_barrier_semaphore()
    for step in steps:
        pl.semaphore_signal(barrier, inc=1, device_id={fsdp_axis: peer(f, step)}, device_id_type=mesh_id)
    for k in range(1, 4):
        pl.semaphore_signal(barrier, inc=1, device_id={"ctx": peer(c, k)}, device_id_type=mesh_id)
    pl.semaphore_wait(barrier, len(steps) + 3)
    total = value_ref[...]
    for index, step in enumerate(steps):
        held_ref[index] = total
        copy = pltpu.make_async_remote_copy(
            src_ref=held_ref.at[index],
            dst_ref=fsdp_refs[index],
            send_sem=send_sem.at[index],
            recv_sem=recv_sem.at[index],
            device_id={fsdp_axis: peer(f, step)},
            device_id_type=mesh_id,
        )
        copy.start()
        copy.wait()
        total = total + fsdp_refs[index][...]
    held_ref[len(steps)] = total
    copies = []
    for k in range(1, 4):
        copy = pltpu.make_async_remote_copy(
            src_ref=held_ref.at[len(steps)],
            dst_ref=ctx_refs[k - 1],
            send_sem=send_sem.at[len(steps) + k - 1],
            recv_sem=recv_sem.at[len(steps) + k - 1],
            device_id={"ctx": peer(c, k)},
            device_id_type=mesh_id,
        )
        copy.start()
        copies.append(copy)
    for copy in copies:
        copy.wait()
    near = total + ctx_refs[0][...]
    out_ref[...] = near + (ctx_refs[1][...] + ctx_refs[2][...])


def small_sum(values, steps):
    dma = pltpu.SemaphoreType.DMA
    return pl.pallas_call(
        functools.partial(small_sum_kernel, tuple(steps), "fsdp"),
        out_shape=jax.ShapeDtypeStruct(values.shape, values.dtype),
        in_specs=[spec(pltpu.VMEM)],
        out_specs=spec(pltpu.VMEM),
        scratch_shapes=[pltpu.VMEM((len(steps) + 1,) + values.shape, values.dtype)]
        + [pltpu.VMEM(values.shape, values.dtype)] * (len(steps) + 3)
        + [dma((len(steps) + 3,))] * 2,
        compiler_params=pltpu.CompilerParams(collective_id=3, has_side_effects=True),
        name="small_sum",
    )(values)


def norm_back(grad_normed, values, factor, gain_row):
    unit_rows = values * factor
    grad_gain = jnp.sum(grad_normed * unit_rows, axis=0)
    grad_unit = grad_normed * gain_row.astype(F32)
    inner_mean = jnp.mean(grad_unit * unit_rows, axis=-1, keepdims=True)
    return (factor * (grad_unit - unit_rows * inner_mean), grad_gain)


def swap(values, axis, size, step):
    return lax.ppermute(values, axis, [(i, i ^ step) for i in range(size)])


def halving(size):
    steps = []
    while size > 1:
        size //= 2
        steps.append(size)
    return steps


def shards(
    sizes,
    tokens,
    cotangent,
    seq_lengths,
    deal,
    norm_gains,
    query_key_value,
    forget_weight,
    forget_bias,
    out_weight,
    gate_up_weight,
    down_weight,
):
    fsdp, ctx, tp = sizes
    layer_count = query_key_value.shape[0]
    row_count, model_width = tokens.shape
    heads_here = forget_weight.shape[2]
    head_size = query_key_value.shape[3] // heads_here
    block_rows = row_count // 2
    piece = model_width // fsdp
    half_width = model_width // 2
    hp = -(-heads_here // ctx)
    heads_padded = hp * ctx
    width = heads_padded * head_size
    more_columns = (heads_padded - heads_here) * head_size
    qkv_columns = 3 * width + 128
    units = gate_up_weight.shape[3]
    unit_block = min(512, units)
    pack = Pack(hp, head_size)
    tiles = pack.tiles
    everything = (row_count, model_width)
    f_index = lax.axis_index("fsdp")
    c_index = lax.axis_index("ctx")
    t_index = lax.axis_index("tp")
    fsdp_steps = halving(fsdp)
    tp_steps = list(reversed(halving(tp)))
    offsets = [0]
    for step in fsdp_steps:
        offsets = offsets + [item ^ step for item in offsets]
    vmem, any_space = pltpu.VMEM, pltpu.HBM

    def add_low(left, right):
        return (left.astype(F32) + right.astype(F32)).astype(BF16)

    grads = {}
    tasks = {}
    pending = {}

    def row_major(values):
        return with_layout_constraint(values, Layout(tuple(range(values.ndim))))

    def gather_pieces(values):
        pieces = [values]
        for step in fsdp_steps[:-1]:
            for item in list(pieces):
                pieces.append(row_major((yield swap(item, "fsdp", fsdp, step))))
        return pieces

    def reduce_grad(near, far, axis, until):
        for step in reversed(fsdp_steps):
            near = add_low(near, (yield swap(far, "fsdp", fsdp, step)))
            if step != fsdp_steps[0]:
                size = near.shape[axis] // 2
                if until == "core" and size == piece and axis == 0:
                    return near, None
                near, far = (
                    lax.slice_in_dim(near, 0, size, axis=axis),
                    lax.slice_in_dim(near, size, 2 * size, axis=axis),
                )
                if until == "core" and size == piece:
                    return near, far
                if until == "pair" and size == piece:
                    return near, (yield swap(far, "fsdp", fsdp, fsdp_steps[0]))
        return near

    def begin(name, *args):
        tasks[name] = reduce_grad(*args)
        pending[name] = next(tasks[name])

    own_first = {}

    def begin_gather(name, values):
        values = row_major(values)
        tasks[name] = gather_pieces(values)
        own_first[name] = swap(values, "fsdp", fsdp, fsdp_steps[-1])
        pending[name] = next(tasks[name])

    def tick(values, names):
        names = [name for name in names if name in tasks]
        if not names:
            return values
        values, got = lax.optimization_barrier((values, [pending.pop(name) for name in names]))
        for name, item in zip(names, got):
            try:
                pending[name] = tasks[name].send(item)
            except StopIteration as end:
                grads[name] = end.value
                del tasks[name]
        return values

    def finished(name):
        while name in tasks:
            tick((), [name])
        return grads[name]

    def weight_pieces(name):
        pieces = finished(name)
        last = [own_first[name]] + [swap(item, "fsdp", fsdp, fsdp_steps[-1]) for item in pieces[1:]]
        last = [row_major(item) for item in last]
        return pieces + last

    def exchange(sends):
        return [sends[0]] + [swap(sends[k], "ctx", ctx, k) for k in range(1, ctx)]

    def to_local(values):
        return jnp.concatenate(
            [
                lax.dynamic_slice_in_dim(values, (f_index ^ item) * piece, piece, axis=1)
                for item in offsets
            ],
            axis=1,
        )

    def from_local(values):
        places = jnp.asarray([offsets.index(item) for item in range(fsdp)], jnp.int32)
        return jnp.concatenate(
            [
                lax.dynamic_slice_in_dim(values, places[f_index ^ item] * piece, piece, axis=1)
                for item in range(fsdp)
            ],
            axis=1,
        )

    def pick(items, index):
        out = items[0]
        for entry in range(1, len(items)):
            out = jnp.where(index == entry, items[entry], out)
        return out

    deal_order = deal[0]
    inverse = (
        jnp.zeros((2 * ctx,), jnp.int32).at[deal_order].set(jnp.arange(2 * ctx, dtype=jnp.int32))
    )
    seq_ends = jnp.cumsum(seq_lengths[0]).astype(jnp.int32)
    peers = jnp.bitwise_xor(jnp.arange(ctx, dtype=jnp.int32), c_index)
    blk = jnp.take(deal_order.reshape(ctx, 2), peers, axis=0).reshape(2 * ctx)
    place = 2 * jnp.bitwise_xor(inverse // 2, c_index) + inverse % 2

    def own_qkv(layer):
        parts = [jnp.pad(query_key_value[layer, j], ((0, 0), (0, more_columns))) for j in range(3)]
        last = jnp.concatenate(
            [
                jnp.pad(forget_weight[layer], ((0, 0), (0, heads_padded - heads_here))),
                norm_gains[layer].T,
                jnp.zeros((piece, 128 - heads_padded - 2), BF16),
            ],
            axis=1,
        )
        return row_major(jnp.concatenate(parts + [last], axis=1))

    share = model_width // tp

    def own_columns(values):
        values = lax.dynamic_slice_in_dim(values, t_index * share, share, axis=1).astype(BF16)
        return values.reshape(2, block_rows, share)

    def column_pieces(values):
        step = 1
        pieces = [values]
        while step < tp:
            pieces = pieces + [swap(item, "tp", tp, step) for item in pieces]
            step *= 2
        return pieces

    def all_columns(pieces):
        order = [0]
        step = 1
        while step < tp:
            order = order + [item ^ step for item in order]
            step *= 2
        stacked = jnp.concatenate(pieces, axis=1)
        places = jnp.asarray([order.index(item) for item in range(tp)], jnp.int32)
        return jnp.concatenate(
            [
                lax.dynamic_slice_in_dim(stacked, places[t_index ^ item] * share, share, axis=1)
                for item in range(tp)
            ],
            axis=1,
        )

    shard, cotangent, tokens, gate_up_weight, out_weight, down_weight = lax.optimization_barrier(
        (own_qkv(0), cotangent, tokens, gate_up_weight, out_weight, down_weight)
    )
    begin_gather(("w_qkv", 0), shard)
    cot_blocks = own_columns(cotangent)
    late_side = (c_index >= ctx // 2).astype(jnp.int32)
    cot_sends = []
    for k in range(ctx):
        wanted = deal_order[2 * (c_index ^ k) + late_side]
        cot_sends.append(lax.dynamic_index_in_dim(cot_blocks, wanted % 2, 0, keepdims=False))
    cot_got = exchange(cot_sends)

    bias_all = jnp.pad(forget_bias.astype(F32), ((0, 0), (0, 128 - heads_here)))[:, None, :]
    own_weights = [
        {
            "w_units": gate_up_weight[layer],
            "w_back": jnp.concatenate(
                [jnp.pad(out_weight[layer], ((0, more_columns), (0, 0))), down_weight[layer]], axis=0
            ),
        }
        for layer in range(layer_count)
    ]
    for layer in range(1, layer_count):
        own_weights[layer]["w_qkv"] = own_qkv(layer)

    residual = to_local(tokens)
    own_weights, residual, cot_got = tick((own_weights, residual, cot_got), [("w_qkv", 0)])
    for name in ("w_back", "w_units"):
        begin_gather((name, 0), own_weights[0][name])
    cot_mine = jnp.concatenate(
        [pick(cot_got, (deal_order[2 * c_index + half] // 2) ^ c_index) for half in range(2)], axis=0
    )
    weights = [{"w_qkv": weight_pieces(("w_qkv", 0))}]
    gains = []

    def piece_inputs(layer, *names):
        return {
            f"{name}_{index}": (item, any_space)
            for name in names
            for index, item in enumerate(weights[layer][name])
        }

    def packed_out():
        return ((ctx, tiles, 2, block_rows, 128), BF16, vmem)

    dma = pltpu.SemaphoreType.DMA
    mix = pltpu.VMEM((model_width, max(units, qkv_columns)), BF16)

    def project(layer, residual):
        out = named_call(
            functools.partial(first_kernel, pack, ctx, width),
            "project",
            {
                "residual": (residual, vmem),
                "bias": (bias_all[layer], vmem),
                **piece_inputs(layer, "w_qkv"),
            },
            {
                "normed": (everything, BF16, vmem),
                "packed": packed_out(),
                "logits": ((row_count, 128), F32, vmem),
                "stat": ((8, model_width), F32, vmem),
                "gains": ((8, model_width), F32, vmem),
            },
            {"w_mix": pltpu.VMEM((model_width, qkv_columns), BF16), "sems": dma((fsdp,))},
            None,
        )
        stat_rows[layer][0] = out["stat"][0]
        gains.append(out["gains"])
        return out["normed"], out["packed"], out["logits"]

    stat_rows = [[None] * 3 for _ in range(layer_count)]
    normed_one, packed, logits = project(0, residual)
    kept = []
    for layer in range(layer_count):
        later = layer + 1
        last = later == layer_count
        rest = [(name, layer) for name in ("w_back", "w_units")]
        if layer == 0:
            packed, cot_mine = lax.optimization_barrier((packed, cot_mine))
        if last:
            cot_pieces = column_pieces(cot_mine)
        att, received, lse, att_turned = attend(pack, place, blk, seq_ends, packed)
        if last:
            att, cot_pieces = lax.optimization_barrier((att, cot_pieces))
            att = tick(att, rest)
        else:
            att, own_weights[later] = tick((att, own_weights[later]), rest)
            begin_gather(("w_qkv", later), own_weights[later]["w_qkv"])
            begin_gather(("w_back", later), own_weights[later]["w_back"])
        for item in rest:
            weights[layer][item[0]] = weight_pieces(item)
        inputs = {
            "att": (att, vmem),
            "residual": (residual, any_space),
            "gains": (gains[layer], vmem),
            **{
                key: value
                for key, value in piece_inputs(layer, "w_back", "w_units").items()
                if int(key.split("_")[-1]) <= fsdp // 2
            },
        }
        outputs = {
            "attended": ((row_count, width), BF16, vmem),
            "middle": (everything, F32, any_space),
            "normed_two": (everything, BF16, any_space),
            "gate": ((row_count, units), BF16, any_space),
            "up": ((row_count, units), BF16, any_space),
            "hidden": ((row_count, units), BF16, any_space),
            "after": (everything, F32, any_space),
            "stat": ((8, model_width), F32, vmem),
        }
        out = named_call(
            functools.partial(middle_kernel, pack, ctx, units, unit_block, tp_steps, fsdp),
            "middle",
            inputs,
            outputs,
            {
                "w_o": pltpu.VMEM((width, model_width), BF16),
                "w_g": pltpu.VMEM((model_width, units), BF16),
                "w_mix": pltpu.VMEM((model_width, units), BF16),
                "w_d": pltpu.VMEM((units, model_width), BF16),
                "base": pltpu.VMEM(everything, F32),
                "after_keep": pltpu.VMEM(everything, F32),
                "normed_keep": pltpu.VMEM(everything, BF16),
                "gate_keep": pltpu.VMEM((row_count, units), BF16),
                "up_keep": pltpu.VMEM((row_count, units), BF16),
                "hidden_keep": pltpu.VMEM((row_count, units), BF16),
                "total": pltpu.VMEM((block_rows, model_width), F32),
                "sems": dma((5 * fsdp + 16,)),
                "core_send": dma((2 * fsdp,)),
                "core_recv": dma((2 * fsdp,)),
                **pair_scratch(4, tp_steps, block_rows, model_width),
            },
            4,
        )
        kept.append(
            dict(
                residual=residual,
                normed_one=normed_one,
                logits=logits,
                received=received,
                lse=lse,
                att_turned=att_turned,
                **{
                    name: out[name] for name in ("attended", "middle", "normed_two", "gate", "up", "hidden")
                },
            )
        )
        stat_rows[layer][1] = out["stat"][0]
        stat_rows[layer][2] = out["stat"][1]
        residual = out["after"]
        if not last:
            residual, own_weights[later] = tick((residual, own_weights[later]), [("w_qkv", later)])
            begin_gather(("w_units", later), own_weights[later]["w_units"])
            weights.append({"w_qkv": weight_pieces(("w_qkv", later))})
            normed_one, packed, logits = project(later, residual)

    final_blocks = own_columns(residual)
    out_got = exchange(
        [
            lax.dynamic_index_in_dim(
                final_blocks, ((c_index ^ k) >= ctx // 2).astype(jnp.int32), 0, keepdims=False
            )
            for k in range(ctx)
        ]
    )

    def halves(values):
        return values[:, :half_width], values[:, half_width:]

    def weight_grad(left, right):
        return lax.dot_general(left, right, (((0,), (0,)), ((), ())), preferred_element_type=F32).astype(BF16)

    gain_grads = [None] * (2 * layer_count)
    bias_grads = [None] * layer_count

    def back_call(layer, upper, grad_base, back_got):
        inputs, outputs, scratch = {}, {}, {"w_mix": mix, "sems": dma((5 * fsdp + 20,))}
        scratch["total"] = pltpu.VMEM((block_rows, model_width), F32)
        if upper is not None:
            inputs.update(
                back=(back_got, vmem), logits=(kept[upper]["logits"], vmem), **piece_inputs(upper, "w_qkv")
            )
            outputs.update(
                grads=((row_count, qkv_columns), BF16, any_space), bias_grad=((8, 128), F32, vmem)
            )
            scratch.update(grads_keep=pltpu.VMEM((row_count, qkv_columns), BF16))
            if layer is None:
                outputs.update(one_part=(everything, BF16, vmem))
            else:
                inputs.update(
                    residual=(kept[upper]["residual"], any_space), upper_gains=(gains[upper], vmem)
                )
        if layer is not None:
            state = kept[layer]
            inputs.update(
                base_in=(grad_base, any_space),
                middle=(state["middle"], any_space),
                gate=(state["gate"], any_space),
                up=(state["up"], any_space),
                gains=(gains[layer], vmem),
                **piece_inputs(layer, "w_back", "w_units"),
            )
            outputs.update(
                low=(everything, BF16, any_space),
                grad_gate=((row_count, units), BF16, any_space),
                grad_up=((row_count, units), BF16, any_space),
                grad=(everything, F32, any_space),
                branch=(everything, BF16, vmem),
                sends=((ctx, hp, block_rows, 128), BF16, vmem),
                gain_grad=((8, model_width), F32, vmem),
            )
            scratch.update(
                base=pltpu.VMEM(everything, grad_base.dtype),
                values=pltpu.VMEM(everything, F32),
                grad_keep=pltpu.VMEM(everything, F32),
                low_keep=pltpu.VMEM(everything, BF16),
                gate_keep=pltpu.VMEM((row_count, units), BF16),
                up_keep=pltpu.VMEM((row_count, units), BF16),
                turned=pltpu.VMEM((row_count, width), BF16),
                w_o=pltpu.VMEM((width, model_width), BF16),
                w_g=pltpu.VMEM((model_width, units), BF16),
                w_d=pltpu.VMEM((units, model_width), BF16),
                **pair_scratch(2 if upper is None else 4, tp_steps, block_rows, model_width),
            )
        return named_call(
            functools.partial(
                back_kernel,
                pack,
                ctx,
                width,
                units,
                unit_block,
                tp_steps,
                upper is not None,
                layer is not None,
            ),
            "back_top" if upper is None else "back_end" if layer is None else "back",
            inputs,
            outputs,
            scratch,
            None if layer is None else 6 if upper is None else 7,
        )

    def begin_qkv(layer, out):
        bias_grads[layer] = out["bias_grad"][0, :heads_here]
        begin(
            ("qkv", layer),
            *[weight_grad(part, out["grads"]) for part in halves(kept[layer]["normed_one"])],
            0,
            "core",
        )

    ffn = ("down", "gate", "up", "out")
    grad_base = to_local(all_columns(cot_pieces))
    back_got, upper = None, None
    for layer in reversed(range(layer_count)):
        state = kept[layer]
        out = back_call(layer, upper, grad_base, back_got)
        if upper is None:
            out, out_got = lax.optimization_barrier((out, out_got))
        if upper is not None:
            gain_grads[2 * upper] = out["gain_grad"][0]
            begin_qkv(upper, out)
        gain_grads[2 * layer + 1] = out["gain_grad"][1]
        grad_base = out["grad"]
        lefts = [state["hidden"], state["normed_two"], state["normed_two"], state["attended"]]
        rights = [out["low"], out["grad_gate"], out["grad_up"], out["branch"]]
        for name, left, right in zip(ffn, lefts, rights):
            if name in ("down", "out"):
                pairs = [weight_grad(left, part) for part in halves(right)]
            else:
                pairs = [weight_grad(part, right) for part in halves(left)]
            reach = "core"
            if name in ("down", "gate"):
                reach = "fsdp" if layer else "pair"
            if upper is not None and name == "gate":
                pairs, background = lax.optimization_barrier((pairs, background))
                grads["down", upper], grads["gate", upper] = background
            begin((name, layer), *pairs, 1 if name in ("down", "out") else 0, reach)
        sends = tick(out["sends"], [(name, layer) for name in ffn] + [("qkv", layer + 1)])
        if upper is None:
            mixed = jnp.concatenate(
                [pick(out_got, (inverse[2 * c_index + half] // 2) ^ c_index) for half in range(2)], axis=0
            )
            mixed_pieces = column_pieces(mixed)
        back_got = attend_back(
            pack, place, blk, seq_ends, state["received"], state["lse"], state["att_turned"], sends
        )
        back_got = tick(back_got, [(name, layer) for name in ffn] + [("qkv", layer + 1)])
        if upper is None:
            back_got, mixed_pieces = lax.optimization_barrier((back_got, mixed_pieces))
            mixed_out = from_local(all_columns(mixed_pieces)).astype(F32)
        if layer:
            background = lax.psum([grads["down", layer], grads["gate", layer]], "ctx")
        upper = layer
    out = back_call(None, 0, None, back_got)
    begin_qkv(0, out)
    one_pairs = []
    for half in range(2):
        part = out["one_part"][half * block_rows : (half + 1) * block_rows]
        for step in tp_steps[:-1]:
            part = add_low(part, swap(part, "tp", tp, step))
        one_pairs.append((part, swap(part, "tp", tp, tp_steps[-1])))
    names = [(name, 0) for name in ("down", "gate")]
    arrays = [grads[name][0] for name in names]
    given = {unit: grads[name][1] for unit, name in enumerate(names)}
    far_units = {}
    for name in [("up", 0), ("out", 0)] + [
        (name, layer) for layer in range(1, layer_count) for name in ("up", "out", "qkv")
    ] + [("qkv", 0)]:
        near, far = finished(name)
        far_units[len(arrays)] = far
        arrays.append(near)
        names.append(name)
    reduced = tail(arrays, given, far_units, fsdp_steps[0])
    one_pairs, reduced = lax.optimization_barrier((one_pairs, reduced))
    for name, item in zip(names, reduced):
        grads[name] = item
    grad_normed_one = jnp.concatenate(
        [left.astype(F32) + right.astype(F32) for left, right in one_pairs], axis=0
    )
    first = kept[0]["residual"]
    grad_from_one, gain_grads[0] = norm_back(grad_normed_one, first, unit_factor(first), gains[0][0:1])
    grad_tokens = from_local(grad_base + grad_from_one)

    small = jnp.concatenate(
        [from_local(jnp.stack(gain_grads)).reshape(-1), jnp.sum(jnp.stack([item for row in stat_rows for item in row]), axis=1)]
        + bias_grads
    )
    used = small.shape[0]
    small = jnp.pad(small, (0, -used % 2048)).reshape(-1, 128)
    small = small_sum(small, list(reversed(fsdp_steps))).reshape(-1)
    gain_size = 2 * layer_count * model_width
    grad_gains = lax.dynamic_slice_in_dim(
        small[:gain_size].reshape(layer_count, 2, model_width), f_index * piece, piece, axis=2
    )
    stat_sums = small[gain_size : gain_size + 3 * layer_count].reshape(layer_count, 3)
    bias_sums = small[gain_size + 3 * layer_count : used].reshape(layer_count, heads_here)
    rms_values = jnp.sqrt(stat_sums / (row_count * model_width * fsdp * ctx))

    def both(pick_one):
        return jnp.stack([pick_one(layer).astype(F32) for layer in range(layer_count)])

    kept_columns = heads_here * head_size
    return (
        mixed_out,
        grad_tokens,
        grad_gains,
        both(
            lambda layer: jnp.stack(
                [grads["qkv", layer][:, j * width : j * width + kept_columns] for j in range(3)]
            )
        ),
        both(lambda layer: grads["qkv", layer][:, 3 * width : 3 * width + heads_here]),
        bias_sums,
        both(lambda layer: grads["out", layer][:kept_columns]),
        both(lambda layer: jnp.stack([grads["gate", layer], grads["up", layer]])),
        both(lambda layer: grads["down", layer]),
        rms_values,
    )


def solution(mesh):
    in_specs = (
        P(("fsdp", "ctx"), None),
        P(("fsdp", "ctx"), None),
        P("fsdp", None),
        P("fsdp", None),
        P(None, None, "fsdp"),
        P(None, None, "fsdp", "tp"),
        P(None, "fsdp", "tp"),
        P(None, "tp"),
        P(None, "tp", "fsdp"),
        P(None, None, "fsdp", "tp"),
        P(None, "tp", "fsdp"),
    )
    out_specs = (
        P(("fsdp", "ctx"), None),
        P(("fsdp", "ctx"), None),
        P(None, None, "fsdp"),
        P(None, None, "fsdp", "tp"),
        P(None, "fsdp", "tp"),
        P(None, "tp"),
        P(None, "tp", "fsdp"),
        P(None, None, "fsdp", "tp"),
        P(None, "tp", "fsdp"),
        P(),
    )
    sizes = (mesh.shape["fsdp"], mesh.shape["ctx"], mesh.shape["tp"])
    return jax.shard_map(
        functools.partial(shards, sizes),
        mesh=mesh,
        in_specs=in_specs,
        out_specs=out_specs,
        check_vma=False,
    )
```

```python
import functools
import math

import jax
import jax.numpy as jnp
from jax import lax
from jax.experimental import pallas as pl
from jax.experimental.layout import Layout, with_layout_constraint
from jax.experimental.pallas import tpu as pltpu
from jax.sharding import PartitionSpec as P

EPSILON = 1e-06
NEG_BIG = -1e30
FIRST_LENGTH = 1280
BF16 = jnp.bfloat16
F32 = jnp.float32


def matmul(left, right):
    return jnp.dot(left, right, preferred_element_type=F32)


def split_three(values):
    high = values.astype(BF16).astype(F32)
    rest = values - high
    middle = rest.astype(BF16).astype(F32)
    return high, middle, rest - middle


def iota(shape, dim):
    return lax.broadcasted_iota(jnp.int32, shape, dim)


def with_lanes(base, first, columns):
    lane = iota(base.shape, 1)
    for offset, column in enumerate(columns):
        base = jnp.where(lane == first + offset, column, base)
    return base


def with_rows(base, first, rows):
    row = iota(base.shape, 0)
    for offset, item in enumerate(rows):
        base = jnp.where(row == first + offset, item, base)
    return base


def first_lanes(values, lanes):
    return jnp.where(iota(values.shape, 1) < lanes, values, 0.0)


def widen(values, width=128):
    rows, lanes = values.shape
    return jnp.concatenate([values, jnp.zeros((rows, width - lanes), values.dtype)], axis=1)


class Pack:
    def __init__(self, hp, head_size):
        self.hp, self.head_size = hp, head_size
        self.value_tiles = (hp + 2) // 2
        self.tiles = hp + self.value_tiles

    def value_place(self, head):
        return self.hp + head // 2, (head % 2) * self.head_size


def peer(c, k):
    out, bit = c, 1
    while bit <= k:
        if k & bit:
            out = out + bit * (1 - 2 * ((c // bit) % 2))
        bit *= 2
    return out


def key_range(block, block_rows):
    first_blocks = FIRST_LENGTH // block_rows
    return (0 if block < first_blocks else first_blocks), block + 1


def score_tiles(block, block_rows, ends_ref):
    first, last = key_range(block, block_rows)
    if (block + 1) * block_rows <= FIRST_LENGTH:
        shape = (block_rows, block_rows)
        diagonal = (slice(block * block_rows, last * block_rows), iota(shape, 0) <= iota(shape, 1))
        if first == block:
            return [diagonal]
        return [(slice(first * block_rows, block * block_rows), None), diagonal]
    rows = (last - first) * block_rows
    key_pos = first * block_rows + iota((rows, 1), 0)
    query_pos = block * block_rows + iota((1, block_rows), 1)
    key_seq = jnp.zeros((rows, 1), jnp.int32)
    query_seq = jnp.zeros((1, block_rows), jnp.int32)
    for entry in range(ends_ref.shape[0]):
        key_seq = key_seq + (key_pos >= ends_ref[entry]).astype(jnp.int32)
        query_seq = query_seq + (query_pos >= ends_ref[entry]).astype(jnp.int32)
    mask = (key_pos <= query_pos) & (key_seq == query_seq)
    return [(slice(first * block_rows, last * block_rows), mask)]


def decay_blocks(load, block_count, block_rows):
    shape = (block_rows, block_rows)
    lower = (iota(shape, 0) >= iota(shape, 1)).astype(BF16)
    carry = None
    out = []
    for block in range(block_count):
        sums = matmul(lower, load(block))
        if carry is not None:
            sums = sums + carry
        carry = sums[block_rows - 1 : block_rows, :]
        out.append(sums)
    return out


def greet(count):
    c = lax.axis_index("ctx")
    barrier = pltpu.get_barrier_semaphore()
    for k in range(1, count):
        pl.semaphore_signal(
            barrier, inc=1, device_id={"ctx": peer(c, k)}, device_id_type=pl.DeviceIdType.MESH
        )
    pl.semaphore_wait(barrier, count - 1)
    return c


def move(k, c, source, target, send_sem, recv_sem):
    if k == 0:
        copy = pltpu.make_async_copy(source, target, recv_sem)
    else:
        copy = pltpu.make_async_remote_copy(
            src_ref=source,
            dst_ref=target,
            send_sem=send_sem,
            recv_sem=recv_sem,
            device_id={"ctx": peer(c, k)},
            device_id_type=pl.DeviceIdType.MESH,
        )
    copy.start()
    return copy


def arrive(k, copy):
    if k == 0:
        copy.wait()
    else:
        copy.wait_recv()


def attend_kernel(
    pack,
    place_ref,
    blk_ref,
    ends_ref,
    send_ref,
    out_ref,
    kept_ref,
    lse_ref,
    att_ref,
    key_ref,
    value_ref,
    block_ref,
    back_ref,
    in_send,
    in_recv,
    out_send,
    out_recv,
    keep_sem,
    *recv_refs,
):
    count = send_ref.shape[0]
    block_rows = send_ref.shape[3]
    block_count = 2 * count
    hp, head_size = pack.hp, pack.head_size
    scale = 1.0 / math.sqrt(head_size)
    c = greet(count)
    copies = {}
    order = [pack.value_place(hp)[0]]
    for head in range(hp):
        order += [item for item in (head, pack.value_place(head)[0]) if item not in order]
    for tile in order:
        for k in reversed(range(count)):
            copies[tile, k] = move(
                k,
                c,
                send_ref.at[k, tile],
                recv_refs[tile].at[pl.ds(2 * k, 2)],
                in_send.at[tile, k],
                in_recv.at[tile, k],
            )
    keeps = []
    here = set()

    def need(tile):
        if tile not in here:
            here.add(tile)
            for k in range(count):
                arrive(k, copies[tile, k])
            keep = pltpu.make_async_copy(recv_refs[tile], kept_ref.at[tile], keep_sem.at[tile])
            keep.start()
            keeps.append(keep)

    tile, lane = pack.value_place(hp)
    need(tile)
    decays = decay_blocks(
        lambda block: recv_refs[tile][place_ref[block]][:, lane : lane + head_size], block_count, block_rows
    )
    returns = []
    for head in range(hp):
        need(head)
        value_tile, value_lane = pack.value_place(head)
        need(value_tile)
        query_tiles = []
        for block in range(block_count):
            rows = slice(block * block_rows, (block + 1) * block_rows)
            pair = recv_refs[head][place_ref[block]].astype(F32)
            value = recv_refs[value_tile][place_ref[block]].astype(F32)
            value = value[:, value_lane : value_lane + head_size]
            high, middle, low = split_three(decays[block][:, head : head + 1])
            key_ref[rows, :] = with_lanes(
                widen(pair[:, head_size:]), head_size, (-high, -middle, -low, 1.0, 1.0, 1.0)
            ).astype(BF16)
            value_ref[:, rows] = with_lanes(widen(value), head_size, (1.0,)).T.astype(BF16)
            query_tiles.append(
                with_lanes(first_lanes(pair * scale, head_size), head_size, (1.0, 1.0, 1.0, high, middle, low))
                .T.astype(BF16)
            )
        for block in range(block_count):
            rows = slice(block * block_rows, (block + 1) * block_rows)
            tiles = []
            peak = None
            for key_rows, mask in score_tiles(block, block_rows, ends_ref):
                scores = matmul(key_ref[key_rows, :], query_tiles[block])
                if mask is not None:
                    scores = jnp.where(mask, scores, NEG_BIG)
                top = jnp.max(scores, axis=0, keepdims=True)
                peak = top if peak is None else jnp.maximum(peak, top)
                tiles.append((key_rows, scores))
            total = jnp.zeros((128, block_rows), F32)
            for key_rows, scores in tiles:
                total = total + matmul(value_ref[:, key_rows], jnp.exp(scores - peak).astype(BF16))
            exp_total = total[head_size : head_size + 1, :]
            attended = total * (1.0 / exp_total)
            att_ref[head, :, rows] = attended[:head_size, :]
            lse_ref[head, :, rows] = peak + jnp.log(exp_total)
            block_ref[head, block] = attended.T.astype(BF16)
        for k in range(count):
            back_ref[k, head] = jnp.concatenate(
                [
                    block_ref[head, blk_ref[2 * k]][:, :head_size],
                    block_ref[head, blk_ref[2 * k + 1]][:, :head_size],
                ],
                axis=1,
            )
        for k in reversed(range(count)):
            returns.append(
                (
                    k,
                    move(
                        k,
                        c,
                        back_ref.at[k, head],
                        out_ref.at[k, head],
                        out_send.at[k, head],
                        out_recv.at[k, head],
                    ),
                )
            )
    for k, copy in returns:
        copy.wait()
    for (tile, k), copy in copies.items():
        if k:
            copy.wait_send()
    for keep in keeps:
        keep.wait()


def attend_back_kernel(
    pack,
    place_ref,
    blk_ref,
    ends_ref,
    kept_ref,
    lse_ref,
    att_ref,
    send_ref,
    out_ref,
    key_ref,
    value_ref,
    turned_ref,
    plain_ref,
    grad_key_ref,
    grad_value_ref,
    decay_ref,
    block_ref,
    back_ref,
    in_send,
    in_recv,
    out_send,
    out_recv,
    *grad_refs,
):
    count = send_ref.shape[0]
    block_rows = send_ref.shape[2]
    block_count = 2 * count
    hp, head_size = pack.hp, pack.head_size
    scale = 1.0 / math.sqrt(head_size)
    c = greet(count)
    copies = {}
    for head in range(hp):
        for k in reversed(range(count)):
            copies[head, k] = move(
                k,
                c,
                send_ref.at[k, head],
                grad_refs[head].at[k],
                in_send.at[head, k],
                in_recv.at[head, k],
            )
    tile, lane = pack.value_place(hp)
    decays = decay_blocks(
        lambda block: kept_ref[tile, place_ref[block]][:, lane : lane + head_size], block_count, block_rows
    )
    returns = []

    def give(tile):
        for k in range(count):
            for half in range(2):
                back_ref[tile, k, half] = block_ref[tile, blk_ref[2 * k + half]]
        for k in reversed(range(count)):
            returns.append(
                move(
                    k,
                    c,
                    back_ref.at[tile, k],
                    out_ref.at[k, tile],
                    out_send.at[tile, k],
                    out_recv.at[tile, k],
                )
            )

    for head in range(hp):
        value_tile, value_lane = pack.value_place(head)
        query_tiles = []
        for block in range(block_count):
            rows = slice(block * block_rows, (block + 1) * block_rows)
            pair = kept_ref[head, place_ref[block]].astype(F32)
            value = kept_ref[value_tile, place_ref[block]].astype(F32)
            value = value[:, value_lane : value_lane + head_size]
            key = pair[:, head_size:]
            query = first_lanes(pair * scale, head_size)
            high, middle, low = split_three(decays[block][:, head : head + 1])
            key_ref[rows, :] = with_lanes(
                widen(key), head_size, (-high, -middle, -low, 1.0, 1.0, 1.0, 1.0, 1.0, 1.0)
            ).astype(BF16)
            turned_ref[:, rows] = with_lanes(widen(key), head_size, (1.0,)).T.astype(BF16)
            value_ref[rows, :] = with_lanes(widen(value), head_size, (1.0, 1.0, 1.0)).astype(BF16)
            plain_ref[rows, :] = with_lanes(query, head_size, (1.0,)).astype(BF16)
            query_wide = with_lanes(query, head_size, (1.0, 1.0, 1.0, high, middle, low)).T
            log_parts = [-part for part in split_three(lse_ref[head, :, rows])]
            query_tiles.append(with_rows(query_wide, head_size + 6, log_parts).astype(BF16))
        for k in range(count):
            arrive(k, copies[head, k])
        grad_plain = []
        grad_tiles = []
        for block in range(block_count):
            rows = slice(block * block_rows, (block + 1) * block_rows)
            place = place_ref[block]
            both = grad_refs[head][place // 2].astype(F32)
            grad = jnp.where(place % 2 == 0, both[:, :head_size], both[:, head_size:])
            grad_plain.append(grad.astype(BF16))
            grad_turned = widen(grad).T
            inner = jnp.sum(grad_turned[:head_size, :] * att_ref[head, :, rows], axis=0, keepdims=True)
            inner_parts = [-part for part in split_three(inner)]
            grad_tiles.append(with_rows(grad_turned, head_size, inner_parts).astype(BF16))
        query_grads = []
        for block in range(block_count):
            rows = slice(block * block_rows, (block + 1) * block_rows)
            grad_query = jnp.zeros((128, block_rows), F32)
            for key_rows, mask in score_tiles(block, block_rows, ends_ref):
                scores = matmul(key_ref[key_rows, :], query_tiles[block])
                if mask is not None:
                    scores = jnp.where(mask, scores, NEG_BIG)
                probs = jnp.exp(scores)
                grad_scores = (probs * matmul(value_ref[key_rows, :], grad_tiles[block])).astype(BF16)
                grad_query = grad_query + matmul(turned_ref[:, key_rows], grad_scores)
                add_key = matmul(grad_scores, plain_ref[rows, :])
                add_value = matmul(probs.astype(BF16), grad_plain[block])
                old = slice(key_rows.start, max(key_rows.start, rows.start))
                split = old.stop - old.start
                if split:
                    grad_key_ref[old, :] += add_key[:split]
                    grad_value_ref[old, :] += add_value[:split]
                if key_rows.stop == rows.stop:
                    grad_key_ref[rows, :] = add_key[split:]
                    grad_value_ref[rows, :] = add_value[split:]
            turned = grad_query.T
            query_grads.append((turned[:, :head_size] * scale).astype(BF16))
            decay_ref[rows, head : head + 1] = turned[:, head_size : head_size + 1]
        for block in range(block_count):
            rows = slice(block * block_rows, (block + 1) * block_rows)
            key_wide = grad_key_ref[rows, :]
            block_ref[head, block] = jnp.concatenate(
                [query_grads[block], key_wide[:, :head_size].astype(BF16)], axis=1
            )
            block_ref[value_tile, block, :, value_lane : value_lane + head_size] = grad_value_ref[
                rows, :
            ].astype(BF16)
            decay_ref[rows, head : head + 1] -= key_wide[:, head_size : head_size + 1]
        give(head)
        if value_lane and value_tile != tile:
            give(value_tile)
    shape = (block_rows, block_rows)
    upper = (iota(shape, 0) <= iota(shape, 1)).astype(BF16)
    carry = None
    for block in reversed(range(block_count)):
        rows = slice(block * block_rows, (block + 1) * block_rows)
        sums = jnp.zeros((block_rows, 128), F32)
        values = jnp.where(iota((block_rows, 128), 1) < hp, decay_ref[rows, :], 0.0)
        for part in split_three(values):
            sums = sums + matmul(upper, part.astype(BF16))
        if carry is not None:
            sums = sums + carry
        carry = sums[0:1, :]
        if lane == 0:
            block_ref[tile, block] = sums.astype(BF16)
        else:
            block_ref[tile, block, :, lane : lane + head_size] = sums[:, :head_size].astype(BF16)
    give(tile)
    for copy in returns:
        copy.wait()
    for (head, k), copy in copies.items():
        if k:
            copy.wait_send()


def spec(space):
    return pl.BlockSpec(memory_space=space)


def attend(pack, place, blk, ends, sends):
    count, tiles, _, block_rows, _ = sends.shape
    hp, head_size = pack.hp, pack.head_size
    pack_rows = 2 * count * block_rows
    dma = pltpu.SemaphoreType.DMA
    return pl.pallas_call(
        functools.partial(attend_kernel, pack),
        out_shape=[
            jax.ShapeDtypeStruct((count, hp, block_rows, 128), BF16),
            jax.ShapeDtypeStruct((tiles, 2 * count, block_rows, 128), BF16),
            jax.ShapeDtypeStruct((hp, 1, pack_rows), F32),
            jax.ShapeDtypeStruct((hp, head_size, pack_rows), F32),
        ],
        in_specs=[spec(pltpu.SMEM)] * 3 + [spec(pl.ANY)],
        out_specs=[spec(pl.ANY), spec(pl.ANY), spec(pltpu.VMEM), spec(pltpu.VMEM)],
        scratch_shapes=[
            pltpu.VMEM((pack_rows, 128), BF16),
            pltpu.VMEM((128, pack_rows), BF16),
            pltpu.VMEM((hp, 2 * count, block_rows, 128), BF16),
            pltpu.VMEM((count, hp, block_rows, 128), BF16),
            dma((tiles, count)),
            dma((tiles, count)),
            dma((count, hp)),
            dma((count, hp)),
            dma((tiles,)),
        ]
        + [pltpu.VMEM((2 * count, block_rows, 128), BF16)] * tiles,
        compiler_params=pltpu.CompilerParams(
            vmem_limit_bytes=40 << 20, collective_id=0, has_side_effects=True
        ),
        name="attend",
    )(place, blk, ends, sends)


def attend_back(pack, place, blk, ends, kept, lse, att, sends):
    count, hp, block_rows, _ = sends.shape
    tiles = kept.shape[0]
    head_size = pack.head_size
    pack_rows = 2 * count * block_rows
    dma = pltpu.SemaphoreType.DMA
    return pl.pallas_call(
        functools.partial(attend_back_kernel, pack),
        out_shape=jax.ShapeDtypeStruct((count, tiles, 2, block_rows, 128), BF16),
        in_specs=[spec(pltpu.SMEM)] * 3 + [spec(pltpu.VMEM)] * 3 + [spec(pl.ANY)],
        out_specs=spec(pl.ANY),
        scratch_shapes=[
            pltpu.VMEM((pack_rows, 128), BF16),
            pltpu.VMEM((pack_rows, 128), BF16),
            pltpu.VMEM((128, pack_rows), BF16),
            pltpu.VMEM((pack_rows, 128), BF16),
            pltpu.VMEM((pack_rows, 128), F32),
            pltpu.VMEM((pack_rows, head_size), F32),
            pltpu.VMEM((pack_rows, 128), F32),
            pltpu.VMEM((tiles, 2 * count, block_rows, 128), BF16),
            pltpu.VMEM((tiles, count, 2, block_rows, 128), BF16),
            dma((hp, count)),
            dma((hp, count)),
            dma((tiles, count)),
            dma((tiles, count)),
        ]
        + [pltpu.VMEM((count, block_rows, 128), BF16)] * hp,
        compiler_params=pltpu.CompilerParams(
            vmem_limit_bytes=40 << 20, collective_id=1, has_side_effects=True
        ),
        name="attend_back",
    )(place, blk, ends, kept, lse, att, sends)


VMEM_BYTES = 60 << 20


def turned_matmul(left, right):
    return lax.dot_general(left, right, (((1,), (1,)), ((), ())), preferred_element_type=F32)


def column_sums(values):
    return jnp.sum(values, axis=0, keepdims=True)


def unit_factor(values):
    return lax.rsqrt(jnp.mean(values * values, axis=-1, keepdims=True) + EPSILON)


def norm_rows_back(grad_normed, values, gain):
    factor = unit_factor(values)
    unit = values * factor
    grad_unit = grad_normed * gain
    inner = jnp.mean(grad_unit * unit, axis=-1, keepdims=True)
    return factor * (grad_unit - unit * inner), column_sums(grad_normed * unit)


class Refs:
    def __init__(self, names, refs):
        for name, ref in zip(names, refs, strict=True):
            setattr(self, name, ref)

    def pieces(self, name):
        out = []
        while hasattr(self, f"{name}_{len(out)}"):
            out.append(getattr(self, f"{name}_{len(out)}"))
        return out


def named_call(kernel, name, inputs, outputs, scratch, collective_id):
    names = list(inputs) + list(outputs) + list(scratch)

    def body(*refs):
        kernel(Refs(names, refs))

    params = dict(vmem_limit_bytes=VMEM_BYTES)
    if collective_id is not None:
        params.update(collective_id=collective_id, has_side_effects=True)
    out = pl.pallas_call(
        body,
        out_shape=[jax.ShapeDtypeStruct(shape, kind) for shape, kind, _ in outputs.values()],
        in_specs=[spec(space) for _, space in inputs.values()],
        out_specs=[spec(space) for _, _, space in outputs.values()],
        scratch_shapes=list(scratch.values()),
        compiler_params=pltpu.CompilerParams(**params),
        name=name,
    )(*[array for array, _ in inputs.values()])
    return dict(zip(outputs, out))


class Copies:
    def __init__(self, sems):
        self.sems, self.used, self.saves = sems, 0, []

    def load(self, source, target):
        copy = pltpu.make_async_copy(source, target, self.sems.at[self.used])
        self.used += 1
        copy.start()
        return copy

    def load_down(self, pieces, target, columns=None):
        rows = pieces[0].shape[0]
        out = []
        for index, item in enumerate(pieces):
            place = target.at[pl.ds(index * rows, rows)]
            if columns is not None:
                place = target.at[pl.ds(index * rows, rows), pl.ds(*columns)]
            out.append(self.load(item, place))
        return out

    def load_beside(self, pieces, target):
        columns = pieces[0].shape[1]
        return [
            self.load(item, target.at[:, pl.ds(index * columns, columns)])
            for index, item in enumerate(pieces)
        ]

    def save(self, source, target):
        self.saves.append(self.load(source, target))

    def finish(self):
        for copy in self.saves:
            copy.wait()


class PairSums:
    def __init__(self, steps, send_refs, recv_refs, send_sem, recv_sem):
        self.steps, self.send_refs, self.recv_refs = steps, send_refs, recv_refs
        self.send_sem, self.recv_sem = send_sem, recv_sem
        self.t = lax.axis_index("tp")
        self.started = []

    def greet(self, also=()):
        barrier = pltpu.get_barrier_semaphore()
        for place in also:
            pl.semaphore_signal(barrier, inc=1, device_id=place, device_id_type=pl.DeviceIdType.MESH)
        for step in self.steps:
            pl.semaphore_signal(
                barrier, inc=1, device_id={"tp": peer(self.t, step)}, device_id_type=pl.DeviceIdType.MESH
            )
        pl.semaphore_wait(barrier, len(self.steps) + len(also))

    def copy(self, index):
        copy = pltpu.make_async_remote_copy(
            src_ref=self.send_refs[index],
            dst_ref=self.recv_refs[index],
            send_sem=self.send_sem.at[index],
            recv_sem=self.recv_sem.at[index],
            device_id={"tp": peer(self.t, self.steps[index % len(self.steps)])},
            device_id_type=pl.DeviceIdType.MESH,
        )
        copy.start()
        self.started.append(copy)
        return copy

    def start(self, place):
        self.first = getattr(self, "first", {})
        self.first[place] = self.copy(place * len(self.steps))

    def finish(self, place):
        copy = self.first[place]
        base = place * len(self.steps)
        for offset in range(len(self.steps)):
            if offset:
                self.send_refs[base + offset][...] = total.astype(BF16)
                copy = self.copy(base + offset)
            copy.wait_recv()
            total = self.send_refs[base + offset][...].astype(F32) + self.recv_refs[base + offset][
                ...
            ].astype(F32)
        return total

    def end(self):
        for copy in self.started:
            copy.wait_send()


def pair_scratch(places, steps, rows, columns):
    count = places * len(steps)
    buffers = {f"send{index}": pltpu.VMEM((rows, columns), BF16) for index in range(count)}
    buffers.update({f"recv{index}": pltpu.VMEM((rows, columns), BF16) for index in range(count)})
    buffers["pair_send"] = pltpu.SemaphoreType.DMA((count,))
    buffers["pair_recv"] = pltpu.SemaphoreType.DMA((count,))
    return buffers


def pair_sums(r, places, steps):
    count = places * len(steps)
    return PairSums(
        steps,
        [getattr(r, f"send{index}") for index in range(count)],
        [getattr(r, f"recv{index}") for index in range(count)],
        r.pair_send,
        r.pair_recv,
    )


def over_units(units, block, body):
    def step(index, carry):
        body(pl.ds(pl.multiple_of(index * block, block), block))
        return carry

    lax.fori_loop(0, units // block, step, 0)


def tile_columns(pack, item, head):
    first = (item * pack.hp + head) * pack.head_size
    return slice(first, first + pack.head_size)


def write_tiles(pack, count, packed_ref, half, query, key, value, forget):
    size = pack.head_size
    forget_tile, forget_lane = pack.value_place(pack.hp)
    lane = iota(forget.shape, 1)
    for item in range(count):
        target = peer(lax.axis_index("ctx"), item)
        for head in range(pack.hp):
            columns = tile_columns(pack, item, head)
            packed_ref[target, head, half] = jnp.concatenate([query[:, columns], key[:, columns]], axis=1)
        shift = (forget_lane - item * pack.hp) % 128
        moved = pltpu.roll(forget, shift, 1) if shift else forget
        moved = jnp.where((lane >= forget_lane) & (lane < forget_lane + pack.hp), moved, 0.0)
        for tile in range(pack.hp, pack.tiles):
            parts = []
            for slot in range(2):
                head = 2 * (tile - pack.hp) + slot
                if head < pack.hp:
                    parts.append(value[:, tile_columns(pack, item, head)])
                else:
                    parts.append(moved[:, slot * size : (slot + 1) * size].astype(BF16))
            packed_ref[target, tile, half] = jnp.concatenate(parts, axis=1)


def project_rows(pack, r, count, width, half, rows, normed):
    def part(first, size):
        return matmul(normed, r.w_mix[:, first : first + size])

    query, key, value = [part(index * width, width).astype(BF16) for index in range(3)]
    logits = part(3 * width, 128) + r.bias[...]
    r.logits[rows, :] = logits
    forget = jnp.minimum(logits, 0.0) - jnp.log1p(jnp.exp(-jnp.abs(logits)))
    forget = forget.astype(BF16).astype(F32)
    write_tiles(pack, count, r.packed, half, query, key, value, forget)


def load_projections(copies, r, width, layer):
    out = []
    for j in range(3):
        out += copies.load_down([item.at[j] for item in r.pieces("w_qkv")], r.w_mix, (j * width, width))
    last = [item.at[:, pl.ds(128 * layer, 128)] for item in r.pieces("w_last")]
    return out + copies.load_down(last, r.w_mix, (3 * width, 128))


def first_kernel(pack, count, width, layer, r):
    copies = Copies(r.sems)
    c = lax.axis_index("ctx")
    block_rows = r.packed.shape[3]
    for copy in load_projections(copies, r, width, layer):
        copy.wait()
    turned = r.w_mix[:, 3 * width :].astype(F32).T
    first = count * pack.hp
    r.gains[0:2, :] = turned[first : first + 2, :]
    for half in range(2):
        rows = slice(half * block_rows, (half + 1) * block_rows)
        residual = r.residual[rows, :]
        normed = (residual * unit_factor(residual) * r.gains[0:1, :]).astype(BF16)
        r.normed[rows, :] = normed
        add = column_sums(residual * residual)
        r.stat[...] = jnp.broadcast_to(add if half == 0 else add + r.stat[0:1, :], r.stat.shape)
        project_rows(pack, r, count, width, half, rows, normed)


def middle_kernel(pack, count, units, unit_block, steps, fsdp, r):
    copies = Copies(r.sems)
    c = lax.axis_index("ctx")
    sums = pair_sums(r, 4, steps)
    block_rows = r.attended.shape[0] // 2
    f = lax.axis_index("fsdp")
    other = {"fsdp": peer(f, 1)}
    width = r.w_o.shape[0]
    back, ffn = r.pieces("w_back"), r.pieces("w_units")
    load_out = copies.load_beside([item.at[pl.ds(0, width)] for item in back], r.w_o)
    load_base = copies.load(r.residual, r.base)
    load_units = copies.load_down([item.at[0] for item in ffn], r.w_g)
    load_units += copies.load_down([item.at[1] for item in ffn], r.w_mix)
    load_units += copies.load_beside([item.at[pl.ds(width, units)] for item in back], r.w_d)
    sums.greet([other])
    piece = back[0].shape[1]
    crossing = []
    for index in range(1, fsdp // 2):
        place = pl.ds((fsdp // 2 + index) * piece, piece)
        pairs = [
            (back[index].at[pl.ds(0, width)], r.w_o.at[:, place]),
            (ffn[index].at[0], r.w_g.at[place]),
            (ffn[index].at[1], r.w_mix.at[place]),
            (back[index].at[pl.ds(width, units)], r.w_d.at[:, place]),
        ]
        for source, target in pairs:
            copy = pltpu.make_async_remote_copy(
                src_ref=source,
                dst_ref=target,
                send_sem=r.core_send.at[len(crossing)],
                recv_sem=r.core_recv.at[len(crossing)],
                device_id=other,
                device_id_type=pl.DeviceIdType.MESH,
            )
            copy.start()
            crossing.append(copy)
    for copy in load_out:
        copy.wait()
    for copy in crossing[::4]:
        copy.wait_recv()
    halves = [slice(half * block_rows, (half + 1) * block_rows) for half in range(2)]
    size = pack.head_size
    for half, rows in enumerate(halves):
        columns = []
        for item in range(count):
            for head in range(pack.hp):
                columns.append(r.att[peer(c, item), head][:, half * size : (half + 1) * size])
        attended = jnp.concatenate(columns, axis=1)
        r.attended[rows, :] = attended
        sums.send_refs[half * len(steps)][...] = matmul(attended, r.w_o[...]).astype(BF16)
        sums.start(half)
    load_base.wait()
    for copy in load_units:
        copy.wait()
    for index, copy in enumerate(crossing):
        if index % 4:
            copy.wait_recv()
    for half, rows in enumerate(halves):
        branch = sums.finish(half)
        add = column_sums(branch * branch)
        r.stat[0:1, :] = add if half == 0 else r.stat[0:1, :] + add
        middle = r.base[rows, :] + branch
        r.base[rows, :] = middle
        copies.save(r.base.at[rows], r.middle.at[rows])
        normed = (middle * unit_factor(middle) * r.gains[1:2, :]).astype(BF16)
        r.normed_keep[rows, :] = normed
        copies.save(r.normed_keep.at[rows], r.normed_two.at[rows])
        r.total[...] = jnp.zeros(r.total.shape, F32)

        def block(columns, rows=rows):
            gate = matmul(r.normed_keep[rows, :], r.w_g[:, columns])
            up = matmul(r.normed_keep[rows, :], r.w_mix[:, columns])
            hidden = (gate * jax.nn.sigmoid(gate) * up).astype(BF16)
            r.gate_keep[rows, columns] = gate.astype(BF16)
            r.up_keep[rows, columns] = up.astype(BF16)
            r.hidden_keep[rows, columns] = hidden
            r.total[...] += matmul(hidden, r.w_d[columns, :])

        over_units(units, unit_block, block)
        sums.send_refs[(2 + half) * len(steps)][...] = r.total[...].astype(BF16)
        sums.start(2 + half)
        copies.save(r.gate_keep.at[rows], r.gate.at[rows])
        copies.save(r.up_keep.at[rows], r.up.at[rows])
        copies.save(r.hidden_keep.at[rows], r.hidden.at[rows])
    for half, rows in enumerate(halves):
        branch = sums.finish(2 + half)
        add = column_sums(branch * branch)
        r.stat[1:2, :] = add if half == 0 else r.stat[1:2, :] + add
        residual = r.base[rows, :] + branch
        r.after_keep[rows, :] = residual
        copies.save(r.after_keep.at[rows], r.after.at[rows])
    copies.finish()
    sums.end()
    for copy in crossing:
        copy.wait_send()


def back_kernel(pack, count, width, units, unit_block, steps, upper_layer, feed, r):
    copies = Copies(r.sems)
    c = lax.axis_index("ctx")
    size = pack.head_size
    upper = upper_layer is not None
    forget_tile, forget_lane = pack.value_place(pack.hp)
    if feed:
        sums = pair_sums(r, 4 if upper else 2, steps)
        second = 2 if upper else 0
    block_rows = r.total.shape[0]
    halves = [slice(half * block_rows, (half + 1) * block_rows) for half in range(2)]
    if upper:
        load_qkv = load_projections(copies, r, width, upper_layer)
    if feed:
        if upper:
            load_value = [copies.load(r.residual.at[rows], r.values.at[rows]) for rows in halves]
        load_base = copies.load(r.base_in, r.base)
        waits = [copies.load(r.gate, r.gate_keep), copies.load(r.up, r.up_keep)]
        waits += copies.load_beside(
        [item.at[pl.ds(r.w_o.shape[0], units)] for item in r.pieces("w_back")], r.w_d
    )
        waits += copies.load_down([item.at[0] for item in r.pieces("w_units")], r.w_g)
        load_out = copies.load_beside([item.at[pl.ds(0, r.w_o.shape[0])] for item in r.pieces("w_back")], r.w_o)
        sums.greet()

    if upper:
        for copy in load_qkv:
            copy.wait()
        for half, rows in enumerate(halves):
            columns = [[], [], []]
            forget = jnp.zeros((block_rows, 128), F32)
            lane = iota(forget.shape, 1)
            for item in range(count):
                source = peer(c, item)
                for head in range(pack.hp):
                    pair = r.back[source, head, half]
                    columns[0].append(pair[:, :size])
                    columns[1].append(pair[:, size:])
                    value_tile, value_lane = pack.value_place(head)
                    columns[2].append(r.back[source, value_tile, half][:, value_lane : value_lane + size])
                wide = r.back[source, forget_tile, half].astype(F32)
                shift = (item * pack.hp - forget_lane) % 128
                moved = pltpu.roll(wide, shift, 1) if shift else wide
                first = item * pack.hp
                forget = jnp.where((lane >= first) & (lane < first + pack.hp), moved, forget)
            grad_logits = (forget * jax.nn.sigmoid(-r.logits[rows, :])).astype(BF16)
            add = column_sums(grad_logits.astype(F32))
            r.bias_grad[...] = jnp.broadcast_to(
                add if half == 0 else add + r.bias_grad[0:1, :], r.bias_grad.shape
            )
            for index in range(3):
                r.grads_keep[rows, index * width : (index + 1) * width] = jnp.concatenate(
                    columns[index], axis=1
                )
            r.grads_keep[rows, 3 * width :] = grad_logits
            copies.save(r.grads_keep.at[rows], r.grads.at[rows])
            grads = r.grads_keep[rows, :]
            part = turned_matmul(grads, r.w_mix[:, : 3 * width + 128]).astype(BF16)
            if feed:
                sums.send_refs[half * len(steps)][...] = part
                sums.start(half)
            else:
                r.one_part[rows, :] = part
    if feed:
        waits += copies.load_down([item.at[1] for item in r.pieces("w_units")], r.w_mix, (0, units))
        load_base.wait()
        load_middle = []
        for half, rows in enumerate(halves):
            grad = r.base[rows, :].astype(F32)
            if upper:
                load_value[half].wait()
                back, add = norm_rows_back(sums.finish(half), r.values[rows, :], r.upper_gains[0:1, :])
                r.gain_grad[0:1, :] = add if half == 0 else r.gain_grad[0:1, :] + add
                grad = grad + back
            load_middle.append(copies.load(r.middle.at[rows], r.values.at[rows]))
            r.grad_keep[rows, :] = grad
            r.low_keep[rows, :] = grad.astype(BF16)
            copies.save(r.low_keep.at[rows], r.low.at[rows])
            for copy in waits:
                copy.wait()
            waits = []
            r.total[...] = jnp.zeros(r.total.shape, F32)

            def block(columns, rows=rows):
                grad_hidden = turned_matmul(r.low_keep[rows, :], r.w_d[columns, :])
                gate = r.gate_keep[rows, columns].astype(F32)
                up = r.up_keep[rows, columns].astype(F32)
                sigmoid = jax.nn.sigmoid(gate)
                grad_gate = (grad_hidden * up * sigmoid * (1.0 + gate * (1.0 - sigmoid))).astype(BF16)
                grad_up = (grad_hidden * gate * sigmoid).astype(BF16)
                r.gate_keep[rows, columns] = grad_gate
                r.up_keep[rows, columns] = grad_up
                r.total[...] += turned_matmul(grad_gate, r.w_g[:, columns]) + turned_matmul(
                    grad_up, r.w_mix[:, columns]
                )

            over_units(units, unit_block, block)
            sums.send_refs[(second + half) * len(steps)][...] = r.total[...].astype(BF16)
            sums.start(second + half)
            copies.save(r.gate_keep.at[rows], r.grad_gate.at[rows])
            copies.save(r.up_keep.at[rows], r.grad_up.at[rows])
        for copy in load_out:
            copy.wait()
        for half, rows in enumerate(halves):
            load_middle[half].wait()
            back, add = norm_rows_back(sums.finish(second + half), r.values[rows, :], r.gains[1:2, :])
            r.gain_grad[1:2, :] = add if half == 0 else r.gain_grad[1:2, :] + add
            grad = r.grad_keep[rows, :] + back
            r.grad_keep[rows, :] = grad
            copies.save(r.grad_keep.at[rows], r.grad.at[rows])
            low = grad.astype(BF16)
            r.branch[rows, :] = low
            r.turned[rows, :] = turned_matmul(low, r.w_o[...]).astype(BF16)
        for item in range(count):
            for head in range(pack.hp):
                columns = tile_columns(pack, item, head)
                r.sends[peer(c, item), head] = jnp.concatenate(
                    [r.turned[rows, columns] for rows in halves], axis=1
                )
    copies.finish()
    if feed:
        sums.end()


def tail_kernel(chunks, given, halved, fsdp_step, fsdp_axis, units, *refs):
    own, rest = refs[:units], refs[units:]
    arrived, rest = rest[: len(given)], rest[len(given) :]
    apart = [unit for unit, place in halved.items() if place is not None]
    far, rest = rest[: len(apart)], rest[len(apart) :]
    outs, rest = rest[:units], rest[units:]
    inward, rest = rest[:units], rest[units:]
    held, rest = rest[:units], rest[units:]
    total_refs, rest = rest[:units], rest[units:]
    first_refs, rest = rest[: len(given) + len(halved)], rest[len(given) + len(halved) :]
    load_sem, save_sem, x_send, x_recv, a_send, a_recv, b_send, b_recv, c_send, c_recv = rest
    extra = {unit: first_refs[place] for place, unit in enumerate(list(given) + list(halved))}
    c = lax.axis_index("ctx")
    f = lax.axis_index(fsdp_axis)
    mesh_id = pl.DeviceIdType.MESH
    loads = {}
    for unit in range(units):
        rows = held[unit].shape[0]
        loads[unit] = [
            pltpu.make_async_copy(own[unit].at[pl.ds(0, rows)], held[unit], load_sem.at[unit])
        ]
        if unit in given:
            place = given.index(unit)
            loads[unit].append(
                pltpu.make_async_copy(arrived[place], extra[unit], load_sem.at[units + place])
            )
        for copy in loads[unit]:
            copy.start()
    barrier = pltpu.get_barrier_semaphore()
    pl.semaphore_signal(
        barrier, inc=1, device_id={fsdp_axis: peer(f, fsdp_step)}, device_id_type=mesh_id
    )
    for k in range(1, 4):
        pl.semaphore_signal(barrier, inc=1, device_id={"ctx": peer(c, k)}, device_id_type=mesh_id)
    pl.semaphore_wait(barrier, 4)
    is_end = c * (3 - c) == 0
    is_middle = c * (3 - c) != 0

    def remote(source, target, send, recv, where):
        return pltpu.make_async_remote_copy(
            src_ref=source,
            dst_ref=target,
            send_sem=send,
            recv_sem=recv,
            device_id=where,
            device_id_type=mesh_id,
        )

    def rows_of(index):
        unit, first, count = chunks[index]
        return unit, pl.ds(first, count)

    def x_copy(index):
        unit, first, count = chunks[index]
        if unit in apart:
            source = far[apart.index(unit)].at[pl.ds(first, count)]
        else:
            source = own[unit].at[pl.ds(held[unit].shape[0] + first, count)]
        return remote(
            source,
            extra[unit].at[pl.ds(first, count)],
            x_send.at[index],
            x_recv.at[index],
            {fsdp_axis: peer(f, fsdp_step)},
        )

    def a_copy(index):
        unit, rows = rows_of(index)
        return remote(
            held[unit].at[rows], inward[unit].at[rows], a_send.at[index], a_recv.at[index], {"ctx": 1 + c // 2}
        )

    def b_copy(index):
        unit, rows = rows_of(index)
        return remote(
            inward[unit].at[rows], total_refs[unit].at[rows], b_send.at[index], b_recv.at[index], {"ctx": 3 - c}
        )

    def c_copy(index):
        unit, rows = rows_of(index)
        return remote(
            total_refs[unit].at[rows],
            total_refs[unit].at[rows],
            c_send.at[index],
            c_recv.at[index],
            {"ctx": 3 * (c - 1)},
        )

    def add(left, right, kind):
        return (left.astype(F32) + right.astype(F32)).astype(kind)

    def is_first(index):
        return chunks[index][1] == 0

    def is_last(index):
        return index + 1 == total or chunks[index + 1][0] != chunks[index][0]

    def save(unit):
        return pltpu.make_async_copy(total_refs[unit], outs[unit], save_sem.at[unit])

    total = len(chunks)
    for index in range(total):
        if chunks[index][0] in halved:
            x_copy(index).start()

    def ready(index):
        unit, rows = rows_of(index)
        if is_first(index):
            for copy in loads[unit]:
                copy.wait()
        if unit in halved:
            x_copy(index).wait_recv()
        if unit in extra:
            held[unit][rows, :] = add(held[unit][rows, :], extra[unit][rows, :], held[unit].dtype)

    @pl.when(is_end)
    def _():
        for index in range(total):
            ready(index)
            a_copy(index).start()
        for index in range(total):
            c_copy(index).wait_recv()
            if is_last(index):
                save(chunks[index][0]).start()
        for index in range(total):
            a_copy(index).wait_send()

    @pl.when(is_middle)
    def _():
        lag = 2
        for index in range(total + lag):
            if index < total:
                unit, rows = rows_of(index)
                ready(index)
                a_copy(index).wait_recv()
                inward[unit][rows, :] = add(held[unit][rows, :], inward[unit][rows, :], held[unit].dtype)
                b_copy(index).start()
            if index >= lag:
                late = index - lag
                unit, rows = rows_of(late)
                b_copy(late).wait_recv()
                total_refs[unit][rows, :] = add(
                    inward[unit][rows, :], total_refs[unit][rows, :], held[unit].dtype
                )
                c_copy(late).start()
                if is_last(late):
                    save(unit).start()
        for index in range(total):
            b_copy(index).wait_send()
            c_copy(index).wait_send()

    for unit in range(units):
        save(unit).wait()
    for index in range(total):
        if chunks[index][0] in halved:
            x_copy(index).wait_send()


def tail(arrays, given, far, fsdp_step, chunk_bytes=128 << 10):
    ready = tuple(sorted(given))
    apart = [unit for unit in sorted(far) if far[unit] is not None]
    halved = {unit: (apart.index(unit) if unit in apart else None) for unit in sorted(far)}
    shapes = [
        (item.shape[0] // (2 if unit in halved and unit not in apart else 1), item.shape[1])
        for unit, item in enumerate(arrays)
    ]
    chunks = []
    for unit, (rows, columns) in enumerate(shapes):
        row_bytes = columns * arrays[unit].dtype.itemsize
        pieces = 1
        while rows % (2 * pieces) == 0 and (rows // (2 * pieces)) % 16 == 0 and (
            rows // pieces * row_bytes > chunk_bytes
        ):
            pieces *= 2
        chunks += [(unit, step * (rows // pieces), rows // pieces) for step in range(pieces)]
    dma = pltpu.SemaphoreType.DMA
    buffers = [pltpu.VMEM(shape, item.dtype) for shape, item in zip(shapes, arrays)]
    inputs = list(arrays) + [given[unit] for unit in ready] + [far[unit] for unit in apart]
    return pl.pallas_call(
        functools.partial(tail_kernel, tuple(chunks), ready, halved, fsdp_step, "fsdp", len(arrays)),
        out_shape=[jax.ShapeDtypeStruct(shape, item.dtype) for shape, item in zip(shapes, arrays)],
        in_specs=[spec(pltpu.HBM)] * len(inputs),
        out_specs=[spec(pltpu.HBM)] * len(arrays),
        scratch_shapes=buffers * 3
        + [buffers[unit] for unit in list(ready) + list(halved)]
        + [dma((len(arrays) + len(ready),)), dma((len(arrays),))]
        + [dma((len(chunks),))] * 8,
        compiler_params=pltpu.CompilerParams(
            vmem_limit_bytes=60 << 20, collective_id=2, has_side_effects=True
        ),
        name="tail",
    )(*inputs)


def small_sum_kernel(steps, fsdp_axis, value_ref, out_ref, held_ref, *refs):
    fsdp_refs, ctx_refs = refs[: len(steps)], refs[len(steps) : len(steps) + 3]
    send_sem, recv_sem = refs[len(steps) + 3 :]
    c = lax.axis_index("ctx")
    f = lax.axis_index(fsdp_axis)
    mesh_id = pl.DeviceIdType.MESH
    barrier = pltpu.get_barrier_semaphore()
    for step in steps:
        pl.semaphore_signal(barrier, inc=1, device_id={fsdp_axis: peer(f, step)}, device_id_type=mesh_id)
    for k in range(1, 4):
        pl.semaphore_signal(barrier, inc=1, device_id={"ctx": peer(c, k)}, device_id_type=mesh_id)
    pl.semaphore_wait(barrier, len(steps) + 3)
    total = value_ref[...]
    for index, step in enumerate(steps):
        held_ref[index] = total
        copy = pltpu.make_async_remote_copy(
            src_ref=held_ref.at[index],
            dst_ref=fsdp_refs[index],
            send_sem=send_sem.at[index],
            recv_sem=recv_sem.at[index],
            device_id={fsdp_axis: peer(f, step)},
            device_id_type=mesh_id,
        )
        copy.start()
        copy.wait()
        total = total + fsdp_refs[index][...]
    held_ref[len(steps)] = total
    copies = []
    for k in range(1, 4):
        copy = pltpu.make_async_remote_copy(
            src_ref=held_ref.at[len(steps)],
            dst_ref=ctx_refs[k - 1],
            send_sem=send_sem.at[len(steps) + k - 1],
            recv_sem=recv_sem.at[len(steps) + k - 1],
            device_id={"ctx": peer(c, k)},
            device_id_type=mesh_id,
        )
        copy.start()
        copies.append(copy)
    for copy in copies:
        copy.wait()
    near = total + ctx_refs[0][...]
    out_ref[...] = near + (ctx_refs[1][...] + ctx_refs[2][...])


def small_sum(values, steps):
    dma = pltpu.SemaphoreType.DMA
    return pl.pallas_call(
        functools.partial(small_sum_kernel, tuple(steps), "fsdp"),
        out_shape=jax.ShapeDtypeStruct(values.shape, values.dtype),
        in_specs=[spec(pltpu.VMEM)],
        out_specs=spec(pltpu.VMEM),
        scratch_shapes=[pltpu.VMEM((len(steps) + 1,) + values.shape, values.dtype)]
        + [pltpu.VMEM(values.shape, values.dtype)] * (len(steps) + 3)
        + [dma((len(steps) + 3,))] * 2,
        compiler_params=pltpu.CompilerParams(collective_id=3, has_side_effects=True),
        name="small_sum",
    )(values)


def norm_back(grad_normed, values, factor, gain_row):
    unit_rows = values * factor
    grad_gain = jnp.sum(grad_normed * unit_rows, axis=0)
    grad_unit = grad_normed * gain_row.astype(F32)
    inner_mean = jnp.mean(grad_unit * unit_rows, axis=-1, keepdims=True)
    return (factor * (grad_unit - unit_rows * inner_mean), grad_gain)


def swap(values, axis, size, step):
    return lax.ppermute(values, axis, [(i, i ^ step) for i in range(size)])


def halving(size):
    steps = []
    while size > 1:
        size //= 2
        steps.append(size)
    return steps


def shards(
    sizes,
    tokens,
    cotangent,
    seq_lengths,
    deal,
    norm_gains,
    query_key_value,
    forget_weight,
    forget_bias,
    out_weight,
    gate_up_weight,
    down_weight,
):
    fsdp, ctx, tp = sizes
    layer_count = query_key_value.shape[0]
    row_count, model_width = tokens.shape
    heads_here = forget_weight.shape[2]
    head_size = query_key_value.shape[3] // heads_here
    block_rows = row_count // 2
    piece = model_width // fsdp
    half_width = model_width // 2
    hp = -(-heads_here // ctx)
    heads_padded = hp * ctx
    width = heads_padded * head_size
    more_columns = (heads_padded - heads_here) * head_size
    qkv_columns = 3 * width + 128
    units = gate_up_weight.shape[3]
    unit_block = min(512, units)
    pack = Pack(hp, head_size)
    tiles = pack.tiles
    everything = (row_count, model_width)
    f_index = lax.axis_index("fsdp")
    c_index = lax.axis_index("ctx")
    t_index = lax.axis_index("tp")
    fsdp_steps = halving(fsdp)
    tp_steps = list(reversed(halving(tp)))
    offsets = [0]
    for step in fsdp_steps:
        offsets = offsets + [item ^ step for item in offsets]
    vmem, any_space = pltpu.VMEM, pltpu.HBM

    def add_low(left, right):
        return (left.astype(F32) + right.astype(F32)).astype(BF16)

    grads = {}
    tasks = {}
    pending = {}

    def row_major(values):
        return with_layout_constraint(values, Layout(tuple(range(values.ndim))))

    def gather_pieces(values):
        pieces = [values]
        for step in fsdp_steps[:-1]:
            for item in list(pieces):
                pieces.append(row_major((yield swap(item, "fsdp", fsdp, step))))
        return pieces

    def reduce_grad(near, far, axis, until):
        for step in reversed(fsdp_steps):
            near = add_low(near, (yield swap(far, "fsdp", fsdp, step)))
            if step != fsdp_steps[0]:
                size = near.shape[axis] // 2
                if until == "core" and size == piece and axis == 0:
                    return near, None
                near, far = (
                    lax.slice_in_dim(near, 0, size, axis=axis),
                    lax.slice_in_dim(near, size, 2 * size, axis=axis),
                )
                if until == "core" and size == piece:
                    return near, far
                if until == "pair" and size == piece:
                    return near, (yield swap(far, "fsdp", fsdp, fsdp_steps[0]))
        return near

    def begin(name, *args):
        tasks[name] = reduce_grad(*args)
        pending[name] = next(tasks[name])

    own_first = {}

    def begin_gather(name, values):
        values = row_major(values)
        tasks[name] = gather_pieces(values)
        own_first[name] = swap(values, "fsdp", fsdp, fsdp_steps[-1])
        pending[name] = next(tasks[name])

    def tick(values, names):
        names = [name for name in names if name in tasks]
        if not names:
            return values
        values, got = lax.optimization_barrier((values, [pending.pop(name) for name in names]))
        for name, item in zip(names, got):
            try:
                pending[name] = tasks[name].send(item)
            except StopIteration as end:
                grads[name] = end.value
                del tasks[name]
        return values

    def finished(name):
        while name in tasks:
            tick((), [name])
        return grads[name]

    def weight_pieces(name):
        pieces = finished(name)
        last = [own_first[name]] + [swap(item, "fsdp", fsdp, fsdp_steps[-1]) for item in pieces[1:]]
        last = [row_major(item) for item in last]
        return pieces + last

    def exchange(sends):
        return [sends[0]] + [swap(sends[k], "ctx", ctx, k) for k in range(1, ctx)]

    def to_local(values):
        return jnp.concatenate(
            [
                lax.dynamic_slice_in_dim(values, (f_index ^ item) * piece, piece, axis=1)
                for item in offsets
            ],
            axis=1,
        )

    def from_local(values):
        places = jnp.asarray([offsets.index(item) for item in range(fsdp)], jnp.int32)
        return jnp.concatenate(
            [
                lax.dynamic_slice_in_dim(values, places[f_index ^ item] * piece, piece, axis=1)
                for item in range(fsdp)
            ],
            axis=1,
        )

    def pick(items, index):
        out = items[0]
        for entry in range(1, len(items)):
            out = jnp.where(index == entry, items[entry], out)
        return out

    deal_order = deal[0]
    inverse = (
        jnp.zeros((2 * ctx,), jnp.int32).at[deal_order].set(jnp.arange(2 * ctx, dtype=jnp.int32))
    )
    seq_ends = jnp.cumsum(seq_lengths[0]).astype(jnp.int32)
    peers = jnp.bitwise_xor(jnp.arange(ctx, dtype=jnp.int32), c_index)
    blk = jnp.take(deal_order.reshape(ctx, 2), peers, axis=0).reshape(2 * ctx)
    place = 2 * jnp.bitwise_xor(inverse // 2, c_index) + inverse % 2

    def own_qkv(layer):
        return jnp.pad(query_key_value[layer], ((0, 0), (0, 0), (0, more_columns)))

    def own_last():
        parts = []
        for layer in range(layer_count):
            parts += [
                jnp.pad(forget_weight[layer], ((0, 0), (0, heads_padded - heads_here))),
                norm_gains[layer].T,
                jnp.zeros((piece, 128 - heads_padded - 2), BF16),
            ]
        return jnp.concatenate(parts, axis=1)

    share = model_width // tp

    def own_columns(values):
        values = lax.dynamic_slice_in_dim(values, t_index * share, share, axis=1).astype(BF16)
        return values.reshape(2, block_rows, share)

    def column_pieces(values):
        step = 1
        pieces = [values]
        while step < tp:
            pieces = pieces + [swap(item, "tp", tp, step) for item in pieces]
            step *= 2
        return pieces

    def all_columns(pieces):
        order = [0]
        step = 1
        while step < tp:
            order = order + [item ^ step for item in order]
            step *= 2
        stacked = jnp.concatenate(pieces, axis=1)
        places = jnp.asarray([order.index(item) for item in range(tp)], jnp.int32)
        return jnp.concatenate(
            [
                lax.dynamic_slice_in_dim(stacked, places[t_index ^ item] * share, share, axis=1)
                for item in range(tp)
            ],
            axis=1,
        )

    shard, cotangent, tokens, gate_up_weight, out_weight, down_weight = lax.optimization_barrier(
        (own_qkv(0), cotangent, tokens, gate_up_weight, out_weight, down_weight)
    )
    begin_gather(("w_qkv", 0), shard)
    begin_gather(("w_last", 0), own_last())
    output_places = [(inverse[2 * c_index + half] // 2) ^ c_index for half in range(2)]
    cot_places = [(deal_order[2 * c_index + half] // 2) ^ c_index for half in range(2)]
    cot_blocks = own_columns(cotangent)
    late_side = (c_index >= ctx // 2).astype(jnp.int32)
    cot_sends = []
    for k in range(ctx):
        wanted = deal_order[2 * (c_index ^ k) + late_side]
        cot_sends.append(lax.dynamic_index_in_dim(cot_blocks, wanted % 2, 0, keepdims=False))
    cot_got = exchange(cot_sends)

    bias_all = jnp.pad(forget_bias.astype(F32), ((0, 0), (0, 128 - heads_here)))[:, None, :]
    own_weights = [
        {
            "w_units": gate_up_weight[layer],
            "w_back": jnp.concatenate(
                [jnp.pad(out_weight[layer], ((0, more_columns), (0, 0))), down_weight[layer]], axis=0
            ),
        }
        for layer in range(layer_count)
    ]
    for layer in range(1, layer_count):
        own_weights[layer]["w_qkv"] = own_qkv(layer)

    residual = to_local(tokens)
    own_weights, residual, cot_got, output_places, cot_places = tick(
        (own_weights, residual, cot_got, output_places, cot_places), [("w_qkv", 0), ("w_last", 0)]
    )
    for name in ("w_back", "w_units"):
        begin_gather((name, 0), own_weights[0][name])
    cot_mine = jnp.concatenate(
        [pick(cot_got, cot_places[half]) for half in range(2)], axis=0
    )
    weights = [{"w_qkv": weight_pieces(("w_qkv", 0)), "w_last": weight_pieces(("w_last", 0))}]
    gains = []

    def piece_inputs(layer, *names):
        return {
            f"{name}_{index}": (item, any_space)
            for name in names
            for index, item in enumerate(weights[layer][name])
        }

    def packed_out():
        return ((ctx, tiles, 2, block_rows, 128), BF16, vmem)

    dma = pltpu.SemaphoreType.DMA
    mix = pltpu.VMEM((model_width, max(units, qkv_columns)), BF16)

    def project(layer, residual):
        out = named_call(
            functools.partial(first_kernel, pack, ctx, width, layer),
            "project",
            {
                "residual": (residual, vmem),
                "bias": (bias_all[layer], vmem),
                **piece_inputs(layer, "w_qkv", "w_last"),
            },
            {
                "normed": (everything, BF16, vmem),
                "packed": packed_out(),
                "logits": ((row_count, 128), F32, vmem),
                "stat": ((8, model_width), F32, vmem),
                "gains": ((8, model_width), F32, vmem),
            },
            {"w_mix": pltpu.VMEM((model_width, qkv_columns), BF16), "sems": dma((4 * fsdp,))},
            None,
        )
        stat_rows[layer][0] = out["stat"][0]
        gains.append(out["gains"])
        return out["normed"], out["packed"], out["logits"]

    stat_rows = [[None] * 3 for _ in range(layer_count)]
    normed_one, packed, logits = project(0, residual)
    kept = []
    for layer in range(layer_count):
        later = layer + 1
        last = later == layer_count
        rest = [(name, layer) for name in ("w_back", "w_units")]
        if layer == 0:
            packed, cot_mine = lax.optimization_barrier((packed, cot_mine))
        if last:
            cot_pieces = column_pieces(cot_mine)
        att, received, lse, att_turned = attend(pack, place, blk, seq_ends, packed)
        if last:
            att, cot_pieces = lax.optimization_barrier((att, cot_pieces))
            att = tick(att, rest)
        else:
            att, own_weights[later] = tick((att, own_weights[later]), rest)
            begin_gather(("w_qkv", later), own_weights[later]["w_qkv"])
            begin_gather(("w_back", later), own_weights[later]["w_back"])
        for item in rest:
            weights[layer][item[0]] = weight_pieces(item)
        inputs = {
            "att": (att, vmem),
            "residual": (residual, any_space),
            "gains": (gains[layer], vmem),
            **{
                key: value
                for key, value in piece_inputs(layer, "w_back", "w_units").items()
                if int(key.split("_")[-1]) <= fsdp // 2
            },
        }
        outputs = {
            "attended": ((row_count, width), BF16, vmem),
            "middle": (everything, F32, any_space),
            "normed_two": (everything, BF16, any_space),
            "gate": ((row_count, units), BF16, any_space),
            "up": ((row_count, units), BF16, any_space),
            "hidden": ((row_count, units), BF16, any_space),
            "after": (everything, F32, any_space),
            "stat": ((8, model_width), F32, vmem),
        }
        out = named_call(
            functools.partial(middle_kernel, pack, ctx, units, unit_block, tp_steps, fsdp),
            "middle",
            inputs,
            outputs,
            {
                "w_o": pltpu.VMEM((width, model_width), BF16),
                "w_g": pltpu.VMEM((model_width, units), BF16),
                "w_mix": pltpu.VMEM((model_width, units), BF16),
                "w_d": pltpu.VMEM((units, model_width), BF16),
                "base": pltpu.VMEM(everything, F32),
                "after_keep": pltpu.VMEM(everything, F32),
                "normed_keep": pltpu.VMEM(everything, BF16),
                "gate_keep": pltpu.VMEM((row_count, units), BF16),
                "up_keep": pltpu.VMEM((row_count, units), BF16),
                "hidden_keep": pltpu.VMEM((row_count, units), BF16),
                "total": pltpu.VMEM((block_rows, model_width), F32),
                "sems": dma((5 * fsdp + 16,)),
                "core_send": dma((2 * fsdp,)),
                "core_recv": dma((2 * fsdp,)),
                **pair_scratch(4, tp_steps, block_rows, model_width),
            },
            4,
        )
        kept.append(
            dict(
                residual=residual,
                normed_one=normed_one,
                logits=logits,
                received=received,
                lse=lse,
                att_turned=att_turned,
                **{
                    name: out[name] for name in ("attended", "middle", "normed_two", "gate", "up", "hidden")
                },
            )
        )
        stat_rows[layer][1] = out["stat"][0]
        stat_rows[layer][2] = out["stat"][1]
        residual = out["after"]
        if not last:
            residual, own_weights[later] = tick(
                (residual, own_weights[later]), [("w_qkv", later), ("w_back", later)]
            )
            begin_gather(("w_units", later), own_weights[later]["w_units"])
            weights.append(
                {"w_qkv": weight_pieces(("w_qkv", later)), "w_last": weights[0]["w_last"]}
            )
            normed_one, packed, logits = project(later, residual)

    final_blocks = own_columns(residual)
    out_got = exchange(
        [
            lax.dynamic_index_in_dim(
                final_blocks, ((c_index ^ k) >= ctx // 2).astype(jnp.int32), 0, keepdims=False
            )
            for k in range(ctx)
        ]
    )

    def halves(values):
        return values[:, :half_width], values[:, half_width:]

    def weight_grad(left, right):
        return lax.dot_general(left, right, (((0,), (0,)), ((), ())), preferred_element_type=F32).astype(BF16)

    gain_grads = [None] * (2 * layer_count)
    bias_grads = [None] * layer_count

    def back_call(layer, upper, grad_base, back_got):
        inputs, outputs, scratch = {}, {}, {"w_mix": mix, "sems": dma((8 * fsdp + 24,))}
        scratch["total"] = pltpu.VMEM((block_rows, model_width), F32)
        if upper is not None:
            inputs.update(
                back=(back_got, vmem), logits=(kept[upper]["logits"], vmem), **piece_inputs(upper, "w_qkv", "w_last")
            )
            outputs.update(
                grads=((row_count, qkv_columns), BF16, any_space), bias_grad=((8, 128), F32, vmem)
            )
            scratch.update(grads_keep=pltpu.VMEM((row_count, qkv_columns), BF16))
            if layer is None:
                outputs.update(one_part=(everything, BF16, vmem))
            else:
                inputs.update(
                    residual=(kept[upper]["residual"], any_space), upper_gains=(gains[upper], vmem)
                )
        if layer is not None:
            state = kept[layer]
            inputs.update(
                base_in=(grad_base, any_space),
                middle=(state["middle"], any_space),
                gate=(state["gate"], any_space),
                up=(state["up"], any_space),
                gains=(gains[layer], vmem),
                **piece_inputs(layer, "w_back", "w_units"),
            )
            outputs.update(
                low=(everything, BF16, any_space),
                grad_gate=((row_count, units), BF16, any_space),
                grad_up=((row_count, units), BF16, any_space),
                grad=(everything, F32, any_space),
                branch=(everything, BF16, vmem),
                sends=((ctx, hp, block_rows, 128), BF16, vmem),
                gain_grad=((8, model_width), F32, vmem),
            )
            scratch.update(
                base=pltpu.VMEM(everything, grad_base.dtype),
                values=pltpu.VMEM(everything, F32),
                grad_keep=pltpu.VMEM(everything, F32),
                low_keep=pltpu.VMEM(everything, BF16),
                gate_keep=pltpu.VMEM((row_count, units), BF16),
                up_keep=pltpu.VMEM((row_count, units), BF16),
                turned=pltpu.VMEM((row_count, width), BF16),
                w_o=pltpu.VMEM((width, model_width), BF16),
                w_g=pltpu.VMEM((model_width, units), BF16),
                w_d=pltpu.VMEM((units, model_width), BF16),
                **pair_scratch(2 if upper is None else 4, tp_steps, block_rows, model_width),
            )
        return named_call(
            functools.partial(
                back_kernel,
                pack,
                ctx,
                width,
                units,
                unit_block,
                tp_steps,
                upper,
                layer is not None,
            ),
            "back_top" if upper is None else "back_end" if layer is None else "back",
            inputs,
            outputs,
            scratch,
            None if layer is None else 6 if upper is None else 7,
        )

    def begin_qkv(layer, out):
        bias_grads[layer] = out["bias_grad"][0, :heads_here]
        begin(
            ("qkv", layer),
            *[weight_grad(part, out["grads"]) for part in halves(kept[layer]["normed_one"])],
            0,
            "core",
        )

    ffn = ("down", "gate", "up", "out")
    grad_base = to_local(all_columns(cot_pieces))
    back_got, upper = None, None
    for layer in reversed(range(layer_count)):
        state = kept[layer]
        out = back_call(layer, upper, grad_base, back_got)
        if upper is None:
            out, out_got = lax.optimization_barrier((out, out_got))
        if upper is not None:
            gain_grads[2 * upper] = out["gain_grad"][0]
            begin_qkv(upper, out)
        gain_grads[2 * layer + 1] = out["gain_grad"][1]
        grad_base = out["grad"]
        lefts = [state["hidden"], state["normed_two"], state["normed_two"], state["attended"]]
        rights = [out["low"], out["grad_gate"], out["grad_up"], out["branch"]]
        for name, left, right in zip(ffn, lefts, rights):
            if name in ("down", "out"):
                pairs = [weight_grad(left, part) for part in halves(right)]
            else:
                pairs = [weight_grad(part, right) for part in halves(left)]
            reach = "core"
            if name in ("down", "gate"):
                reach = "fsdp" if layer else "pair"
            if upper is not None and name == "gate":
                pairs, background = lax.optimization_barrier((pairs, background))
                grads["down", upper], grads["gate", upper] = background
            begin((name, layer), *pairs, 1 if name in ("down", "out") else 0, reach)
        sends = tick(out["sends"], [(name, layer) for name in ("down", "gate")])
        if upper is None:
            mixed = jnp.concatenate(
                [pick(out_got, output_places[half]) for half in range(2)], axis=0
            )
        if layer == 0:
            sends, mixed = lax.optimization_barrier((sends, mixed))
            mixed_pieces = column_pieces(mixed)
        back_got = attend_back(
            pack, place, blk, seq_ends, state["received"], state["lse"], state["att_turned"], sends
        )
        back_got = tick(back_got, [(name, layer) for name in ffn] + [("qkv", layer + 1)])
        if layer == 0:
            back_got, mixed_pieces = lax.optimization_barrier((back_got, mixed_pieces))
            mixed_out = from_local(all_columns(mixed_pieces)).astype(F32)
        if layer:
            background = lax.psum([grads["down", layer], grads["gate", layer]], "ctx")
        upper = layer
    out = back_call(None, 0, None, back_got)
    begin_qkv(0, out)
    one_pairs = []
    for half in range(2):
        part = out["one_part"][half * block_rows : (half + 1) * block_rows]
        for step in tp_steps[:-1]:
            part = add_low(part, swap(part, "tp", tp, step))
        one_pairs.append((part, swap(part, "tp", tp, tp_steps[-1])))
    names = [(name, 0) for name in ("down", "gate")]
    arrays = [grads[name][0] for name in names]
    given = {unit: grads[name][1] for unit, name in enumerate(names)}
    far_units = {}
    for name in [("up", 0), ("out", 0)] + [
        (name, layer) for layer in range(1, layer_count) for name in ("up", "out", "qkv")
    ] + [("qkv", 0)]:
        near, far = finished(name)
        far_units[len(arrays)] = far
        arrays.append(near)
        names.append(name)
    reduced = tail(arrays, given, far_units, fsdp_steps[0])
    one_pairs, reduced = lax.optimization_barrier((one_pairs, reduced))
    for name, item in zip(names, reduced):
        grads[name] = item
    grad_normed_one = jnp.concatenate(
        [left.astype(F32) + right.astype(F32) for left, right in one_pairs], axis=0
    )
    first = kept[0]["residual"]
    grad_from_one, gain_grads[0] = norm_back(grad_normed_one, first, unit_factor(first), gains[0][0:1])
    grad_tokens = from_local(grad_base + grad_from_one)

    small = jnp.concatenate(
        [from_local(jnp.stack(gain_grads)).reshape(-1), jnp.sum(jnp.stack([item for row in stat_rows for item in row]), axis=1)]
        + bias_grads
    )
    used = small.shape[0]
    small = jnp.pad(small, (0, -used % 2048)).reshape(-1, 128)
    small = small_sum(small, list(reversed(fsdp_steps))).reshape(-1)
    gain_size = 2 * layer_count * model_width
    grad_gains = lax.dynamic_slice_in_dim(
        small[:gain_size].reshape(layer_count, 2, model_width), f_index * piece, piece, axis=2
    )
    stat_sums = small[gain_size : gain_size + 3 * layer_count].reshape(layer_count, 3)
    bias_sums = small[gain_size + 3 * layer_count : used].reshape(layer_count, heads_here)
    rms_values = jnp.sqrt(stat_sums / (row_count * model_width * fsdp * ctx))

    def both(pick_one):
        return jnp.stack([pick_one(layer).astype(F32) for layer in range(layer_count)])

    kept_columns = heads_here * head_size
    return (
        mixed_out,
        grad_tokens,
        grad_gains,
        both(
            lambda layer: jnp.stack(
                [grads["qkv", layer][:, j * width : j * width + kept_columns] for j in range(3)]
            )
        ),
        both(lambda layer: grads["qkv", layer][:, 3 * width : 3 * width + heads_here]),
        bias_sums,
        both(lambda layer: grads["out", layer][:kept_columns]),
        both(lambda layer: jnp.stack([grads["gate", layer], grads["up", layer]])),
        both(lambda layer: grads["down", layer]),
        rms_values,
    )


def solution(mesh):
    in_specs = (
        P(("fsdp", "ctx"), None),
        P(("fsdp", "ctx"), None),
        P("fsdp", None),
        P("fsdp", None),
        P(None, None, "fsdp"),
        P(None, None, "fsdp", "tp"),
        P(None, "fsdp", "tp"),
        P(None, "tp"),
        P(None, "tp", "fsdp"),
        P(None, None, "fsdp", "tp"),
        P(None, "tp", "fsdp"),
    )
    out_specs = (
        P(("fsdp", "ctx"), None),
        P(("fsdp", "ctx"), None),
        P(None, None, "fsdp"),
        P(None, None, "fsdp", "tp"),
        P(None, "fsdp", "tp"),
        P(None, "tp"),
        P(None, "tp", "fsdp"),
        P(None, None, "fsdp", "tp"),
        P(None, "tp", "fsdp"),
        P(),
    )
    sizes = (mesh.shape["fsdp"], mesh.shape["ctx"], mesh.shape["tp"])
    return jax.shard_map(
        functools.partial(shards, sizes),
        mesh=mesh,
        in_specs=in_specs,
        out_specs=out_specs,
        check_vma=False,
    )
```

```python
import functools
import math

import jax
import jax.numpy as jnp
from jax import lax
from jax.experimental import pallas as pl
from jax.experimental.layout import Layout, with_layout_constraint
from jax.experimental.pallas import tpu as pltpu
from jax.sharding import PartitionSpec as P

EPSILON = 1e-06
NEG_BIG = -1e30
FIRST_LENGTH = 1280
BF16 = jnp.bfloat16
F32 = jnp.float32


def matmul(left, right):
    return jnp.dot(left, right, preferred_element_type=F32)


def split_three(values):
    high = values.astype(BF16).astype(F32)
    rest = values - high
    middle = rest.astype(BF16).astype(F32)
    return high, middle, rest - middle


def iota(shape, dim):
    return lax.broadcasted_iota(jnp.int32, shape, dim)


def with_lanes(base, first, columns):
    lane = iota(base.shape, 1)
    for offset, column in enumerate(columns):
        base = jnp.where(lane == first + offset, column, base)
    return base


def with_rows(base, first, rows):
    row = iota(base.shape, 0)
    for offset, item in enumerate(rows):
        base = jnp.where(row == first + offset, item, base)
    return base


def first_lanes(values, lanes):
    return jnp.where(iota(values.shape, 1) < lanes, values, 0.0)


def widen(values, width=128):
    rows, lanes = values.shape
    return jnp.concatenate([values, jnp.zeros((rows, width - lanes), values.dtype)], axis=1)


class Pack:
    def __init__(self, hp, head_size):
        self.hp, self.head_size = hp, head_size
        self.value_tiles = (hp + 2) // 2
        self.tiles = hp + self.value_tiles

    def value_place(self, head):
        return self.hp + head // 2, (head % 2) * self.head_size


def peer(c, k):
    out, bit = c, 1
    while bit <= k:
        if k & bit:
            out = out + bit * (1 - 2 * ((c // bit) % 2))
        bit *= 2
    return out


def key_range(block, block_rows):
    first_blocks = FIRST_LENGTH // block_rows
    return (0 if block < first_blocks else first_blocks), block + 1


def score_tiles(block, block_rows, ends_ref):
    first, last = key_range(block, block_rows)
    if (block + 1) * block_rows <= FIRST_LENGTH:
        shape = (block_rows, block_rows)
        diagonal = (slice(block * block_rows, last * block_rows), iota(shape, 0) <= iota(shape, 1))
        if first == block:
            return [diagonal]
        return [(slice(first * block_rows, block * block_rows), None), diagonal]
    rows = (last - first) * block_rows
    key_pos = first * block_rows + iota((rows, 1), 0)
    query_pos = block * block_rows + iota((1, block_rows), 1)
    key_seq = jnp.zeros((rows, 1), jnp.int32)
    query_seq = jnp.zeros((1, block_rows), jnp.int32)
    for entry in range(ends_ref.shape[0]):
        key_seq = key_seq + (key_pos >= ends_ref[entry]).astype(jnp.int32)
        query_seq = query_seq + (query_pos >= ends_ref[entry]).astype(jnp.int32)
    mask = (key_pos <= query_pos) & (key_seq == query_seq)
    return [(slice(first * block_rows, last * block_rows), mask)]


def decay_blocks(load, block_count, block_rows):
    shape = (block_rows, block_rows)
    lower = (iota(shape, 0) >= iota(shape, 1)).astype(BF16)
    carry = None
    out = []
    for block in range(block_count):
        sums = matmul(lower, load(block))
        if carry is not None:
            sums = sums + carry
        carry = sums[block_rows - 1 : block_rows, :]
        out.append(sums)
    return out


def greet(count):
    c = lax.axis_index("ctx")
    barrier = pltpu.get_barrier_semaphore()
    for k in range(1, count):
        pl.semaphore_signal(
            barrier, inc=1, device_id={"ctx": peer(c, k)}, device_id_type=pl.DeviceIdType.MESH
        )
    pl.semaphore_wait(barrier, count - 1)
    return c


def move(k, c, source, target, send_sem, recv_sem):
    if k == 0:
        copy = pltpu.make_async_copy(source, target, recv_sem)
    else:
        copy = pltpu.make_async_remote_copy(
            src_ref=source,
            dst_ref=target,
            send_sem=send_sem,
            recv_sem=recv_sem,
            device_id={"ctx": peer(c, k)},
            device_id_type=pl.DeviceIdType.MESH,
        )
    copy.start()
    return copy


def arrive(k, copy):
    if k == 0:
        copy.wait()
    else:
        copy.wait_recv()


def attend_kernel(
    pack,
    place_ref,
    blk_ref,
    ends_ref,
    send_ref,
    out_ref,
    kept_ref,
    lse_ref,
    att_ref,
    key_ref,
    value_ref,
    block_ref,
    back_ref,
    in_send,
    in_recv,
    out_send,
    out_recv,
    keep_sem,
    *recv_refs,
):
    count = send_ref.shape[0]
    block_rows = send_ref.shape[3]
    block_count = 2 * count
    hp, head_size = pack.hp, pack.head_size
    scale = 1.0 / math.sqrt(head_size)
    c = greet(count)
    copies = {}
    order = [pack.value_place(hp)[0]]
    for head in range(hp):
        order += [item for item in (head, pack.value_place(head)[0]) if item not in order]
    for tile in order:
        for k in reversed(range(count)):
            copies[tile, k] = move(
                k,
                c,
                send_ref.at[k, tile],
                recv_refs[tile].at[pl.ds(2 * k, 2)],
                in_send.at[tile, k],
                in_recv.at[tile, k],
            )
    keeps = []
    here = set()

    def need(tile):
        if tile not in here:
            here.add(tile)
            for k in range(count):
                arrive(k, copies[tile, k])
            keep = pltpu.make_async_copy(recv_refs[tile], kept_ref.at[tile], keep_sem.at[tile])
            keep.start()
            keeps.append(keep)

    tile, lane = pack.value_place(hp)
    need(tile)
    decays = decay_blocks(
        lambda block: recv_refs[tile][place_ref[block]][:, lane : lane + head_size], block_count, block_rows
    )
    returns = []
    for head in range(hp):
        need(head)
        value_tile, value_lane = pack.value_place(head)
        need(value_tile)
        query_tiles = []
        for block in range(block_count):
            rows = slice(block * block_rows, (block + 1) * block_rows)
            pair = recv_refs[head][place_ref[block]].astype(F32)
            value = recv_refs[value_tile][place_ref[block]].astype(F32)
            value = value[:, value_lane : value_lane + head_size]
            high, middle, low = split_three(decays[block][:, head : head + 1])
            key_ref[rows, :] = with_lanes(
                widen(pair[:, head_size:]), head_size, (-high, -middle, -low, 1.0, 1.0, 1.0)
            ).astype(BF16)
            value_ref[:, rows] = with_lanes(widen(value), head_size, (1.0,)).T.astype(BF16)
            query_tiles.append(
                with_lanes(first_lanes(pair * scale, head_size), head_size, (1.0, 1.0, 1.0, high, middle, low))
                .T.astype(BF16)
            )
        for block in range(block_count):
            rows = slice(block * block_rows, (block + 1) * block_rows)
            tiles = []
            peak = None
            for key_rows, mask in score_tiles(block, block_rows, ends_ref):
                scores = matmul(key_ref[key_rows, :], query_tiles[block])
                if mask is not None:
                    scores = jnp.where(mask, scores, NEG_BIG)
                top = jnp.max(scores, axis=0, keepdims=True)
                peak = top if peak is None else jnp.maximum(peak, top)
                tiles.append((key_rows, scores))
            total = jnp.zeros((128, block_rows), F32)
            for key_rows, scores in tiles:
                total = total + matmul(value_ref[:, key_rows], jnp.exp(scores - peak).astype(BF16))
            exp_total = total[head_size : head_size + 1, :]
            attended = total * (1.0 / exp_total)
            att_ref[head, :, rows] = attended[:head_size, :]
            lse_ref[head, :, rows] = peak + jnp.log(exp_total)
            block_ref[head, block] = attended.T.astype(BF16)
        for k in range(count):
            back_ref[k, head] = jnp.concatenate(
                [
                    block_ref[head, blk_ref[2 * k]][:, :head_size],
                    block_ref[head, blk_ref[2 * k + 1]][:, :head_size],
                ],
                axis=1,
            )
        for k in reversed(range(count)):
            returns.append(
                (
                    k,
                    move(
                        k,
                        c,
                        back_ref.at[k, head],
                        out_ref.at[k, head],
                        out_send.at[k, head],
                        out_recv.at[k, head],
                    ),
                )
            )
    for k, copy in returns:
        copy.wait()
    for (tile, k), copy in copies.items():
        if k:
            copy.wait_send()
    for keep in keeps:
        keep.wait()


def attend_back_kernel(
    pack,
    place_ref,
    blk_ref,
    ends_ref,
    kept_ref,
    lse_ref,
    att_ref,
    send_ref,
    out_ref,
    key_ref,
    value_ref,
    turned_ref,
    plain_ref,
    grad_key_ref,
    grad_value_ref,
    decay_ref,
    block_ref,
    back_ref,
    in_send,
    in_recv,
    out_send,
    out_recv,
    *grad_refs,
):
    count = send_ref.shape[0]
    block_rows = send_ref.shape[2]
    block_count = 2 * count
    hp, head_size = pack.hp, pack.head_size
    scale = 1.0 / math.sqrt(head_size)
    c = greet(count)
    copies = {}
    for head in range(hp):
        for k in reversed(range(count)):
            copies[head, k] = move(
                k,
                c,
                send_ref.at[k, head],
                grad_refs[head].at[k],
                in_send.at[head, k],
                in_recv.at[head, k],
            )
    tile, lane = pack.value_place(hp)
    decays = decay_blocks(
        lambda block: kept_ref[tile, place_ref[block]][:, lane : lane + head_size], block_count, block_rows
    )
    returns = []

    def give(tile):
        for k in range(count):
            for half in range(2):
                back_ref[tile, k, half] = block_ref[tile, blk_ref[2 * k + half]]
        for k in reversed(range(count)):
            returns.append(
                move(
                    k,
                    c,
                    back_ref.at[tile, k],
                    out_ref.at[k, tile],
                    out_send.at[tile, k],
                    out_recv.at[tile, k],
                )
            )

    for head in range(hp):
        value_tile, value_lane = pack.value_place(head)
        query_tiles = []
        for block in range(block_count):
            rows = slice(block * block_rows, (block + 1) * block_rows)
            pair = kept_ref[head, place_ref[block]].astype(F32)
            value = kept_ref[value_tile, place_ref[block]].astype(F32)
            value = value[:, value_lane : value_lane + head_size]
            key = pair[:, head_size:]
            query = first_lanes(pair * scale, head_size)
            high, middle, low = split_three(decays[block][:, head : head + 1])
            key_ref[rows, :] = with_lanes(
                widen(key), head_size, (-high, -middle, -low, 1.0, 1.0, 1.0, 1.0, 1.0, 1.0)
            ).astype(BF16)
            turned_ref[:, rows] = with_lanes(widen(key), head_size, (1.0,)).T.astype(BF16)
            value_ref[rows, :] = with_lanes(widen(value), head_size, (1.0, 1.0, 1.0)).astype(BF16)
            plain_ref[rows, :] = with_lanes(query, head_size, (1.0,)).astype(BF16)
            query_wide = with_lanes(query, head_size, (1.0, 1.0, 1.0, high, middle, low)).T
            log_parts = [-part for part in split_three(lse_ref[head, :, rows])]
            query_tiles.append(with_rows(query_wide, head_size + 6, log_parts).astype(BF16))
        for k in range(count):
            arrive(k, copies[head, k])
        grad_plain = []
        grad_tiles = []
        for block in range(block_count):
            rows = slice(block * block_rows, (block + 1) * block_rows)
            place = place_ref[block]
            both = grad_refs[head][place // 2].astype(F32)
            grad = jnp.where(place % 2 == 0, both[:, :head_size], both[:, head_size:])
            grad_plain.append(grad.astype(BF16))
            grad_turned = widen(grad).T
            inner = jnp.sum(grad_turned[:head_size, :] * att_ref[head, :, rows], axis=0, keepdims=True)
            inner_parts = [-part for part in split_three(inner)]
            grad_tiles.append(with_rows(grad_turned, head_size, inner_parts).astype(BF16))
        query_grads = []
        for block in range(block_count):
            rows = slice(block * block_rows, (block + 1) * block_rows)
            grad_query = jnp.zeros((128, block_rows), F32)
            for key_rows, mask in score_tiles(block, block_rows, ends_ref):
                scores = matmul(key_ref[key_rows, :], query_tiles[block])
                if mask is not None:
                    scores = jnp.where(mask, scores, NEG_BIG)
                probs = jnp.exp(scores)
                grad_scores = (probs * matmul(value_ref[key_rows, :], grad_tiles[block])).astype(BF16)
                grad_query = grad_query + matmul(turned_ref[:, key_rows], grad_scores)
                add_key = matmul(grad_scores, plain_ref[rows, :])
                add_value = matmul(probs.astype(BF16), grad_plain[block])
                old = slice(key_rows.start, max(key_rows.start, rows.start))
                split = old.stop - old.start
                if split:
                    grad_key_ref[old, :] += add_key[:split]
                    grad_value_ref[old, :] += add_value[:split]
                if key_rows.stop == rows.stop:
                    grad_key_ref[rows, :] = add_key[split:]
                    grad_value_ref[rows, :] = add_value[split:]
            turned = grad_query.T
            query_grads.append((turned[:, :head_size] * scale).astype(BF16))
            decay_ref[rows, head : head + 1] = turned[:, head_size : head_size + 1]
        for block in range(block_count):
            rows = slice(block * block_rows, (block + 1) * block_rows)
            key_wide = grad_key_ref[rows, :]
            block_ref[head, block] = jnp.concatenate(
                [query_grads[block], key_wide[:, :head_size].astype(BF16)], axis=1
            )
            block_ref[value_tile, block, :, value_lane : value_lane + head_size] = grad_value_ref[
                rows, :
            ].astype(BF16)
            decay_ref[rows, head : head + 1] -= key_wide[:, head_size : head_size + 1]
        give(head)
        if value_lane and value_tile != tile:
            give(value_tile)
    shape = (block_rows, block_rows)
    upper = (iota(shape, 0) <= iota(shape, 1)).astype(BF16)
    carry = None
    for block in reversed(range(block_count)):
        rows = slice(block * block_rows, (block + 1) * block_rows)
        sums = jnp.zeros((block_rows, 128), F32)
        values = jnp.where(iota((block_rows, 128), 1) < hp, decay_ref[rows, :], 0.0)
        for part in split_three(values):
            sums = sums + matmul(upper, part.astype(BF16))
        if carry is not None:
            sums = sums + carry
        carry = sums[0:1, :]
        if lane == 0:
            block_ref[tile, block] = sums.astype(BF16)
        else:
            block_ref[tile, block, :, lane : lane + head_size] = sums[:, :head_size].astype(BF16)
    give(tile)
    for copy in returns:
        copy.wait()
    for (head, k), copy in copies.items():
        if k:
            copy.wait_send()


def spec(space):
    return pl.BlockSpec(memory_space=space)


def attend(pack, place, blk, ends, sends):
    count, tiles, _, block_rows, _ = sends.shape
    hp, head_size = pack.hp, pack.head_size
    pack_rows = 2 * count * block_rows
    dma = pltpu.SemaphoreType.DMA
    return pl.pallas_call(
        functools.partial(attend_kernel, pack),
        out_shape=[
            jax.ShapeDtypeStruct((count, hp, block_rows, 128), BF16),
            jax.ShapeDtypeStruct((tiles, 2 * count, block_rows, 128), BF16),
            jax.ShapeDtypeStruct((hp, 1, pack_rows), F32),
            jax.ShapeDtypeStruct((hp, head_size, pack_rows), F32),
        ],
        in_specs=[spec(pltpu.SMEM)] * 3 + [spec(pl.ANY)],
        out_specs=[spec(pl.ANY), spec(pl.ANY), spec(pltpu.VMEM), spec(pltpu.VMEM)],
        scratch_shapes=[
            pltpu.VMEM((pack_rows, 128), BF16),
            pltpu.VMEM((128, pack_rows), BF16),
            pltpu.VMEM((hp, 2 * count, block_rows, 128), BF16),
            pltpu.VMEM((count, hp, block_rows, 128), BF16),
            dma((tiles, count)),
            dma((tiles, count)),
            dma((count, hp)),
            dma((count, hp)),
            dma((tiles,)),
        ]
        + [pltpu.VMEM((2 * count, block_rows, 128), BF16)] * tiles,
        compiler_params=pltpu.CompilerParams(
            vmem_limit_bytes=40 << 20, collective_id=0, has_side_effects=True
        ),
        name="attend",
    )(place, blk, ends, sends)


def attend_back(pack, place, blk, ends, kept, lse, att, sends):
    count, hp, block_rows, _ = sends.shape
    tiles = kept.shape[0]
    head_size = pack.head_size
    pack_rows = 2 * count * block_rows
    dma = pltpu.SemaphoreType.DMA
    return pl.pallas_call(
        functools.partial(attend_back_kernel, pack),
        out_shape=jax.ShapeDtypeStruct((count, tiles, 2, block_rows, 128), BF16),
        in_specs=[spec(pltpu.SMEM)] * 3 + [spec(pltpu.VMEM)] * 3 + [spec(pl.ANY)],
        out_specs=spec(pl.ANY),
        scratch_shapes=[
            pltpu.VMEM((pack_rows, 128), BF16),
            pltpu.VMEM((pack_rows, 128), BF16),
            pltpu.VMEM((128, pack_rows), BF16),
            pltpu.VMEM((pack_rows, 128), BF16),
            pltpu.VMEM((pack_rows, 128), F32),
            pltpu.VMEM((pack_rows, head_size), F32),
            pltpu.VMEM((pack_rows, 128), F32),
            pltpu.VMEM((tiles, 2 * count, block_rows, 128), BF16),
            pltpu.VMEM((tiles, count, 2, block_rows, 128), BF16),
            dma((hp, count)),
            dma((hp, count)),
            dma((tiles, count)),
            dma((tiles, count)),
        ]
        + [pltpu.VMEM((count, block_rows, 128), BF16)] * hp,
        compiler_params=pltpu.CompilerParams(
            vmem_limit_bytes=40 << 20, collective_id=1, has_side_effects=True
        ),
        name="attend_back",
    )(place, blk, ends, kept, lse, att, sends)


VMEM_BYTES = 60 << 20


def turned_matmul(left, right):
    return lax.dot_general(left, right, (((1,), (1,)), ((), ())), preferred_element_type=F32)


def column_sums(values):
    return jnp.sum(values, axis=0, keepdims=True)


def unit_factor(values):
    return lax.rsqrt(jnp.mean(values * values, axis=-1, keepdims=True) + EPSILON)


def norm_rows_back(grad_normed, values, gain):
    factor = unit_factor(values)
    unit = values * factor
    grad_unit = grad_normed * gain
    inner = jnp.mean(grad_unit * unit, axis=-1, keepdims=True)
    return factor * (grad_unit - unit * inner), column_sums(grad_normed * unit)


class Refs:
    def __init__(self, names, refs):
        for name, ref in zip(names, refs, strict=True):
            setattr(self, name, ref)

    def pieces(self, name):
        out = []
        while hasattr(self, f"{name}_{len(out)}"):
            out.append(getattr(self, f"{name}_{len(out)}"))
        return out


def named_call(kernel, name, inputs, outputs, scratch, collective_id):
    names = list(inputs) + list(outputs) + list(scratch)

    def body(*refs):
        kernel(Refs(names, refs))

    params = dict(vmem_limit_bytes=VMEM_BYTES)
    if collective_id is not None:
        params.update(collective_id=collective_id, has_side_effects=True)
    out = pl.pallas_call(
        body,
        out_shape=[jax.ShapeDtypeStruct(shape, kind) for shape, kind, _ in outputs.values()],
        in_specs=[spec(space) for _, space in inputs.values()],
        out_specs=[spec(space) for _, _, space in outputs.values()],
        scratch_shapes=list(scratch.values()),
        compiler_params=pltpu.CompilerParams(**params),
        name=name,
    )(*[array for array, _ in inputs.values()])
    return dict(zip(outputs, out))


class Copies:
    def __init__(self, sems):
        self.sems, self.used, self.saves = sems, 0, []

    def load(self, source, target):
        copy = pltpu.make_async_copy(source, target, self.sems.at[self.used])
        self.used += 1
        copy.start()
        return copy

    def load_down(self, pieces, target, columns=None):
        rows = pieces[0].shape[0]
        out = []
        for index, item in enumerate(pieces):
            place = target.at[pl.ds(index * rows, rows)]
            if columns is not None:
                place = target.at[pl.ds(index * rows, rows), pl.ds(*columns)]
            out.append(self.load(item, place))
        return out

    def load_beside(self, pieces, target):
        columns = pieces[0].shape[1]
        return [
            self.load(item, target.at[:, pl.ds(index * columns, columns)])
            for index, item in enumerate(pieces)
        ]

    def save(self, source, target):
        self.saves.append(self.load(source, target))

    def finish(self):
        for copy in self.saves:
            copy.wait()


class PairSums:
    def __init__(self, steps, send_refs, recv_refs, send_sem, recv_sem):
        self.steps, self.send_refs, self.recv_refs = steps, send_refs, recv_refs
        self.send_sem, self.recv_sem = send_sem, recv_sem
        self.t = lax.axis_index("tp")
        self.started = []

    def greet(self, also=()):
        barrier = pltpu.get_barrier_semaphore()
        for place in also:
            pl.semaphore_signal(barrier, inc=1, device_id=place, device_id_type=pl.DeviceIdType.MESH)
        for step in self.steps:
            pl.semaphore_signal(
                barrier, inc=1, device_id={"tp": peer(self.t, step)}, device_id_type=pl.DeviceIdType.MESH
            )
        pl.semaphore_wait(barrier, len(self.steps) + len(also))

    def copy(self, index):
        copy = pltpu.make_async_remote_copy(
            src_ref=self.send_refs[index],
            dst_ref=self.recv_refs[index],
            send_sem=self.send_sem.at[index],
            recv_sem=self.recv_sem.at[index],
            device_id={"tp": peer(self.t, self.steps[index % len(self.steps)])},
            device_id_type=pl.DeviceIdType.MESH,
        )
        copy.start()
        self.started.append(copy)
        return copy

    def start(self, place):
        self.first = getattr(self, "first", {})
        self.first[place] = self.copy(place * len(self.steps))

    def finish(self, place):
        copy = self.first[place]
        base = place * len(self.steps)
        for offset in range(len(self.steps)):
            if offset:
                self.send_refs[base + offset][...] = total.astype(BF16)
                copy = self.copy(base + offset)
            copy.wait_recv()
            total = self.send_refs[base + offset][...].astype(F32) + self.recv_refs[base + offset][
                ...
            ].astype(F32)
        return total

    def end(self):
        for copy in self.started:
            copy.wait_send()


def pair_scratch(places, steps, rows, columns):
    count = places * len(steps)
    buffers = {f"send{index}": pltpu.VMEM((rows, columns), BF16) for index in range(count)}
    buffers.update({f"recv{index}": pltpu.VMEM((rows, columns), BF16) for index in range(count)})
    buffers["pair_send"] = pltpu.SemaphoreType.DMA((count,))
    buffers["pair_recv"] = pltpu.SemaphoreType.DMA((count,))
    return buffers


def pair_sums(r, places, steps):
    count = places * len(steps)
    return PairSums(
        steps,
        [getattr(r, f"send{index}") for index in range(count)],
        [getattr(r, f"recv{index}") for index in range(count)],
        r.pair_send,
        r.pair_recv,
    )


def over_units(units, block, body):
    def step(index, carry):
        body(pl.ds(pl.multiple_of(index * block, block), block))
        return carry

    lax.fori_loop(0, units // block, step, 0)


def tile_columns(pack, item, head):
    first = (item * pack.hp + head) * pack.head_size
    return slice(first, first + pack.head_size)


def write_tiles(pack, count, packed_ref, half, query, key, value, forget):
    size = pack.head_size
    forget_tile, forget_lane = pack.value_place(pack.hp)
    lane = iota(forget.shape, 1)
    for item in range(count):
        target = peer(lax.axis_index("ctx"), item)
        for head in range(pack.hp):
            columns = tile_columns(pack, item, head)
            packed_ref[target, head, half] = jnp.concatenate([query[:, columns], key[:, columns]], axis=1)
        shift = (forget_lane - item * pack.hp) % 128
        moved = pltpu.roll(forget, shift, 1) if shift else forget
        moved = jnp.where((lane >= forget_lane) & (lane < forget_lane + pack.hp), moved, 0.0)
        for tile in range(pack.hp, pack.tiles):
            parts = []
            for slot in range(2):
                head = 2 * (tile - pack.hp) + slot
                if head < pack.hp:
                    parts.append(value[:, tile_columns(pack, item, head)])
                else:
                    parts.append(moved[:, slot * size : (slot + 1) * size].astype(BF16))
            packed_ref[target, tile, half] = jnp.concatenate(parts, axis=1)


def project_rows(pack, r, count, width, half, rows, normed):
    def part(first, size):
        return matmul(normed, r.w_mix[:, first : first + size])

    query, key, value = [part(index * width, width).astype(BF16) for index in range(3)]
    logits = part(3 * width, 128) + r.bias[...]
    r.logits[rows, :] = logits
    forget = jnp.minimum(logits, 0.0) - jnp.log1p(jnp.exp(-jnp.abs(logits)))
    forget = forget.astype(BF16).astype(F32)
    write_tiles(pack, count, r.packed, half, query, key, value, forget)


def load_projections(copies, r, width, layer):
    last = [item.at[:, pl.ds(128 * layer, 128)] for item in r.pieces("w_last")]
    out = copies.load_down(last, r.w_mix, (3 * width, 128))
    for j in range(3):
        out += copies.load_down([item.at[j] for item in r.pieces("w_qkv")], r.w_mix, (j * width, width))
    return out


def first_kernel(pack, count, width, layer, r):
    copies = Copies(r.sems)
    c = lax.axis_index("ctx")
    block_rows = r.packed.shape[3]
    loads = load_projections(copies, r, width, layer)
    last_count = len(r.pieces("w_last"))
    for copy in loads[:last_count]:
        copy.wait()
    turned = r.w_mix[:, 3 * width :].astype(F32).T
    first = count * pack.hp
    r.gains[0:2, :] = turned[first : first + 2, :]
    for half in range(2):
        rows = slice(half * block_rows, (half + 1) * block_rows)
        residual = r.residual[rows, :]
        normed = (residual * unit_factor(residual) * r.gains[0:1, :]).astype(BF16)
        r.normed[rows, :] = normed
        add = column_sums(residual * residual)
        r.stat[...] = jnp.broadcast_to(add if half == 0 else add + r.stat[0:1, :], r.stat.shape)
        if half == 0:
            for copy in loads[last_count:]:
                copy.wait()
        project_rows(pack, r, count, width, half, rows, normed)


def middle_kernel(pack, count, units, unit_block, steps, fsdp, r):
    copies = Copies(r.sems)
    c = lax.axis_index("ctx")
    sums = pair_sums(r, 4, steps)
    block_rows = r.attended.shape[0] // 2
    f = lax.axis_index("fsdp")
    other = {"fsdp": peer(f, 1)}
    width = r.w_o.shape[0]
    back, ffn = r.pieces("w_back"), r.pieces("w_units")
    load_out = copies.load_beside([item.at[pl.ds(0, width)] for item in back], r.w_o)
    load_base = copies.load(r.residual, r.base)
    load_units = copies.load_down([item.at[0] for item in ffn], r.w_g)
    load_units += copies.load_down([item.at[1] for item in ffn], r.w_mix)
    load_units += copies.load_beside([item.at[pl.ds(width, units)] for item in back], r.w_d)
    sums.greet([other])
    piece = back[0].shape[1]
    crossing = []
    for index in range(1, fsdp // 2):
        place = pl.ds((fsdp // 2 + index) * piece, piece)
        pairs = [
            (back[index].at[pl.ds(0, width)], r.w_o.at[:, place]),
            (ffn[index].at[0], r.w_g.at[place]),
            (ffn[index].at[1], r.w_mix.at[place]),
            (back[index].at[pl.ds(width, units)], r.w_d.at[:, place]),
        ]
        for source, target in pairs:
            copy = pltpu.make_async_remote_copy(
                src_ref=source,
                dst_ref=target,
                send_sem=r.core_send.at[len(crossing)],
                recv_sem=r.core_recv.at[len(crossing)],
                device_id=other,
                device_id_type=pl.DeviceIdType.MESH,
            )
            copy.start()
            crossing.append(copy)
    for copy in load_out:
        copy.wait()
    for copy in crossing[::4]:
        copy.wait_recv()
    halves = [slice(half * block_rows, (half + 1) * block_rows) for half in range(2)]
    size = pack.head_size
    for half, rows in enumerate(halves):
        columns = []
        for item in range(count):
            for head in range(pack.hp):
                columns.append(r.att[peer(c, item), head][:, half * size : (half + 1) * size])
        attended = jnp.concatenate(columns, axis=1)
        r.attended[rows, :] = attended
        sums.send_refs[half * len(steps)][...] = matmul(attended, r.w_o[...]).astype(BF16)
        sums.start(half)
    load_base.wait()
    for copy in load_units:
        copy.wait()
    for index, copy in enumerate(crossing):
        if index % 4:
            copy.wait_recv()
    for half, rows in enumerate(halves):
        branch = sums.finish(half)
        add = column_sums(branch * branch)
        r.stat[0:1, :] = add if half == 0 else r.stat[0:1, :] + add
        middle = r.base[rows, :] + branch
        r.base[rows, :] = middle
        copies.save(r.base.at[rows], r.middle.at[rows])
        normed = (middle * unit_factor(middle) * r.gains[1:2, :]).astype(BF16)
        r.normed_keep[rows, :] = normed
        copies.save(r.normed_keep.at[rows], r.normed_two.at[rows])
        r.total[...] = jnp.zeros(r.total.shape, F32)

        def block(columns, rows=rows):
            gate = matmul(r.normed_keep[rows, :], r.w_g[:, columns])
            up = matmul(r.normed_keep[rows, :], r.w_mix[:, columns])
            hidden = (gate * jax.nn.sigmoid(gate) * up).astype(BF16)
            r.gate_keep[rows, columns] = gate.astype(BF16)
            r.up_keep[rows, columns] = up.astype(BF16)
            r.hidden_keep[rows, columns] = hidden
            r.total[...] += matmul(hidden, r.w_d[columns, :])

        over_units(units, unit_block, block)
        sums.send_refs[(2 + half) * len(steps)][...] = r.total[...].astype(BF16)
        sums.start(2 + half)
        copies.save(r.gate_keep.at[rows], r.gate.at[rows])
        copies.save(r.up_keep.at[rows], r.up.at[rows])
        copies.save(r.hidden_keep.at[rows], r.hidden.at[rows])
    for half, rows in enumerate(halves):
        branch = sums.finish(2 + half)
        add = column_sums(branch * branch)
        r.stat[1:2, :] = add if half == 0 else r.stat[1:2, :] + add
        residual = r.base[rows, :] + branch
        r.after_keep[rows, :] = residual
        copies.save(r.after_keep.at[rows], r.after.at[rows])
    copies.finish()
    sums.end()
    for copy in crossing:
        copy.wait_send()


def back_kernel(pack, count, width, units, unit_block, steps, upper_layer, feed, r):
    copies = Copies(r.sems)
    c = lax.axis_index("ctx")
    size = pack.head_size
    upper = upper_layer is not None
    forget_tile, forget_lane = pack.value_place(pack.hp)
    if feed:
        sums = pair_sums(r, 4 if upper else 2, steps)
        second = 2 if upper else 0
    block_rows = r.total.shape[0]
    halves = [slice(half * block_rows, (half + 1) * block_rows) for half in range(2)]
    if upper:
        load_qkv = load_projections(copies, r, width, upper_layer)
    if feed:
        if upper:
            load_value = [copies.load(r.residual.at[rows], r.values.at[rows]) for rows in halves]
        load_base = copies.load(r.base_in, r.base)
        waits = [copies.load(r.gate, r.gate_keep), copies.load(r.up, r.up_keep)]
        waits += copies.load_beside(
        [item.at[pl.ds(r.w_o.shape[0], units)] for item in r.pieces("w_back")], r.w_d
    )
        waits += copies.load_down([item.at[0] for item in r.pieces("w_units")], r.w_g)
        load_out = copies.load_beside([item.at[pl.ds(0, r.w_o.shape[0])] for item in r.pieces("w_back")], r.w_o)
        sums.greet()

    if upper:
        for copy in load_qkv:
            copy.wait()
        for half, rows in enumerate(halves):
            columns = [[], [], []]
            forget = jnp.zeros((block_rows, 128), F32)
            lane = iota(forget.shape, 1)
            for item in range(count):
                source = peer(c, item)
                for head in range(pack.hp):
                    pair = r.back[source, head, half]
                    columns[0].append(pair[:, :size])
                    columns[1].append(pair[:, size:])
                    value_tile, value_lane = pack.value_place(head)
                    columns[2].append(r.back[source, value_tile, half][:, value_lane : value_lane + size])
                wide = r.back[source, forget_tile, half].astype(F32)
                shift = (item * pack.hp - forget_lane) % 128
                moved = pltpu.roll(wide, shift, 1) if shift else wide
                first = item * pack.hp
                forget = jnp.where((lane >= first) & (lane < first + pack.hp), moved, forget)
            grad_logits = (forget * jax.nn.sigmoid(-r.logits[rows, :])).astype(BF16)
            add = column_sums(grad_logits.astype(F32))
            r.bias_grad[...] = jnp.broadcast_to(
                add if half == 0 else add + r.bias_grad[0:1, :], r.bias_grad.shape
            )
            for index in range(3):
                r.grads_keep[rows, index * width : (index + 1) * width] = jnp.concatenate(
                    columns[index], axis=1
                )
            r.grads_keep[rows, 3 * width :] = grad_logits
            copies.save(r.grads_keep.at[rows], r.grads.at[rows])
            grads = r.grads_keep[rows, :]
            part = turned_matmul(grads, r.w_mix[:, : 3 * width + 128]).astype(BF16)
            if feed:
                sums.send_refs[half * len(steps)][...] = part
                sums.start(half)
            else:
                r.one_part[rows, :] = part
    if feed:
        waits += copies.load_down([item.at[1] for item in r.pieces("w_units")], r.w_mix, (0, units))
        load_base.wait()
        load_middle = []
        for half, rows in enumerate(halves):
            grad = r.base[rows, :].astype(F32)
            if upper:
                load_value[half].wait()
                back, add = norm_rows_back(sums.finish(half), r.values[rows, :], r.upper_gains[0:1, :])
                r.gain_grad[0:1, :] = add if half == 0 else r.gain_grad[0:1, :] + add
                grad = grad + back
            load_middle.append(copies.load(r.middle.at[rows], r.values.at[rows]))
            r.grad_keep[rows, :] = grad
            r.low_keep[rows, :] = grad.astype(BF16)
            copies.save(r.low_keep.at[rows], r.low.at[rows])
            for copy in waits:
                copy.wait()
            waits = []
            r.total[...] = jnp.zeros(r.total.shape, F32)

            def block(columns, rows=rows):
                grad_hidden = turned_matmul(r.low_keep[rows, :], r.w_d[columns, :])
                gate = r.gate_keep[rows, columns].astype(F32)
                up = r.up_keep[rows, columns].astype(F32)
                sigmoid = jax.nn.sigmoid(gate)
                grad_gate = (grad_hidden * up * sigmoid * (1.0 + gate * (1.0 - sigmoid))).astype(BF16)
                grad_up = (grad_hidden * gate * sigmoid).astype(BF16)
                r.gate_keep[rows, columns] = grad_gate
                r.up_keep[rows, columns] = grad_up
                r.total[...] += turned_matmul(grad_gate, r.w_g[:, columns]) + turned_matmul(
                    grad_up, r.w_mix[:, columns]
                )

            over_units(units, unit_block, block)
            sums.send_refs[(second + half) * len(steps)][...] = r.total[...].astype(BF16)
            sums.start(second + half)
            copies.save(r.gate_keep.at[rows], r.grad_gate.at[rows])
            copies.save(r.up_keep.at[rows], r.grad_up.at[rows])
        for copy in load_out:
            copy.wait()
        for half, rows in enumerate(halves):
            load_middle[half].wait()
            back, add = norm_rows_back(sums.finish(second + half), r.values[rows, :], r.gains[1:2, :])
            r.gain_grad[1:2, :] = add if half == 0 else r.gain_grad[1:2, :] + add
            grad = r.grad_keep[rows, :] + back
            r.grad_keep[rows, :] = grad
            copies.save(r.grad_keep.at[rows], r.grad.at[rows])
            low = grad.astype(BF16)
            r.branch[rows, :] = low
            r.turned[rows, :] = turned_matmul(low, r.w_o[...]).astype(BF16)
        for item in range(count):
            for head in range(pack.hp):
                columns = tile_columns(pack, item, head)
                r.sends[peer(c, item), head] = jnp.concatenate(
                    [r.turned[rows, columns] for rows in halves], axis=1
                )
    copies.finish()
    if feed:
        sums.end()


def tail_kernel(chunks, given, halved, fsdp_step, fsdp_axis, units, *refs):
    own, rest = refs[:units], refs[units:]
    arrived, rest = rest[: len(given)], rest[len(given) :]
    apart = [unit for unit, place in halved.items() if place is not None]
    far, rest = rest[: len(apart)], rest[len(apart) :]
    outs, rest = rest[:units], rest[units:]
    inward, rest = rest[:units], rest[units:]
    held, rest = rest[:units], rest[units:]
    total_refs, rest = rest[:units], rest[units:]
    first_refs, rest = rest[: len(given) + len(halved)], rest[len(given) + len(halved) :]
    load_sem, save_sem, x_send, x_recv, a_send, a_recv, b_send, b_recv, c_send, c_recv = rest
    extra = {unit: first_refs[place] for place, unit in enumerate(list(given) + list(halved))}
    c = lax.axis_index("ctx")
    f = lax.axis_index(fsdp_axis)
    mesh_id = pl.DeviceIdType.MESH
    loads = {}
    for unit in range(units):
        rows = held[unit].shape[0]
        loads[unit] = [
            pltpu.make_async_copy(own[unit].at[pl.ds(0, rows)], held[unit], load_sem.at[unit])
        ]
        if unit in given:
            place = given.index(unit)
            loads[unit].append(
                pltpu.make_async_copy(arrived[place], extra[unit], load_sem.at[units + place])
            )
        for copy in loads[unit]:
            copy.start()
    barrier = pltpu.get_barrier_semaphore()
    pl.semaphore_signal(
        barrier, inc=1, device_id={fsdp_axis: peer(f, fsdp_step)}, device_id_type=mesh_id
    )
    for k in range(1, 4):
        pl.semaphore_signal(barrier, inc=1, device_id={"ctx": peer(c, k)}, device_id_type=mesh_id)
    pl.semaphore_wait(barrier, 4)
    is_end = c * (3 - c) == 0
    is_middle = c * (3 - c) != 0

    def remote(source, target, send, recv, where):
        return pltpu.make_async_remote_copy(
            src_ref=source,
            dst_ref=target,
            send_sem=send,
            recv_sem=recv,
            device_id=where,
            device_id_type=mesh_id,
        )

    def rows_of(index):
        unit, first, count = chunks[index]
        return unit, pl.ds(first, count)

    def x_copy(index):
        unit, first, count = chunks[index]
        if unit in apart:
            source = far[apart.index(unit)].at[pl.ds(first, count)]
        else:
            source = own[unit].at[pl.ds(held[unit].shape[0] + first, count)]
        return remote(
            source,
            extra[unit].at[pl.ds(first, count)],
            x_send.at[index],
            x_recv.at[index],
            {fsdp_axis: peer(f, fsdp_step)},
        )

    def a_copy(index):
        unit, rows = rows_of(index)
        return remote(
            held[unit].at[rows], inward[unit].at[rows], a_send.at[index], a_recv.at[index], {"ctx": 1 + c // 2}
        )

    def b_copy(index):
        unit, rows = rows_of(index)
        return remote(
            inward[unit].at[rows], total_refs[unit].at[rows], b_send.at[index], b_recv.at[index], {"ctx": 3 - c}
        )

    def c_copy(index):
        unit, rows = rows_of(index)
        return remote(
            total_refs[unit].at[rows],
            total_refs[unit].at[rows],
            c_send.at[index],
            c_recv.at[index],
            {"ctx": 3 * (c - 1)},
        )

    def add(left, right, kind):
        return (left.astype(F32) + right.astype(F32)).astype(kind)

    def is_first(index):
        return chunks[index][1] == 0

    def is_last(index):
        return index + 1 == total or chunks[index + 1][0] != chunks[index][0]

    def save(unit):
        return pltpu.make_async_copy(total_refs[unit], outs[unit], save_sem.at[unit])

    total = len(chunks)
    for index in range(total):
        if chunks[index][0] in halved:
            x_copy(index).start()

    def ready(index):
        unit, rows = rows_of(index)
        if is_first(index):
            for copy in loads[unit]:
                copy.wait()
        if unit in halved:
            x_copy(index).wait_recv()
        if unit in extra:
            held[unit][rows, :] = add(held[unit][rows, :], extra[unit][rows, :], held[unit].dtype)

    @pl.when(is_end)
    def _():
        for index in range(total):
            ready(index)
            a_copy(index).start()
        for index in range(total):
            c_copy(index).wait_recv()
            if is_last(index):
                save(chunks[index][0]).start()
        for index in range(total):
            a_copy(index).wait_send()

    @pl.when(is_middle)
    def _():
        lag = 4
        for index in range(total + lag):
            if index < total:
                unit, rows = rows_of(index)
                ready(index)
                a_copy(index).wait_recv()
                inward[unit][rows, :] = add(held[unit][rows, :], inward[unit][rows, :], held[unit].dtype)
                b_copy(index).start()
            if index >= lag:
                late = index - lag
                unit, rows = rows_of(late)
                b_copy(late).wait_recv()
                total_refs[unit][rows, :] = add(
                    inward[unit][rows, :], total_refs[unit][rows, :], held[unit].dtype
                )
                c_copy(late).start()
                if is_last(late):
                    save(unit).start()
        for index in range(total):
            b_copy(index).wait_send()
            c_copy(index).wait_send()

    for unit in range(units):
        save(unit).wait()
    for index in range(total):
        if chunks[index][0] in halved:
            x_copy(index).wait_send()


def tail(arrays, given, far, fsdp_step, chunk_bytes=128 << 10):
    ready = tuple(sorted(given))
    apart = [unit for unit in sorted(far) if far[unit] is not None]
    halved = {unit: (apart.index(unit) if unit in apart else None) for unit in sorted(far)}
    shapes = [
        (item.shape[0] // (2 if unit in halved and unit not in apart else 1), item.shape[1])
        for unit, item in enumerate(arrays)
    ]
    chunks = []
    for unit, (rows, columns) in enumerate(shapes):
        row_bytes = columns * arrays[unit].dtype.itemsize
        pieces = 1
        while rows % (2 * pieces) == 0 and (rows // (2 * pieces)) % 16 == 0 and (
            rows // pieces * row_bytes > chunk_bytes
        ):
            pieces *= 2
        chunks += [(unit, step * (rows // pieces), rows // pieces) for step in range(pieces)]
    dma = pltpu.SemaphoreType.DMA
    buffers = [pltpu.VMEM(shape, item.dtype) for shape, item in zip(shapes, arrays)]
    inputs = list(arrays) + [given[unit] for unit in ready] + [far[unit] for unit in apart]
    return pl.pallas_call(
        functools.partial(tail_kernel, tuple(chunks), ready, halved, fsdp_step, "fsdp", len(arrays)),
        out_shape=[jax.ShapeDtypeStruct(shape, item.dtype) for shape, item in zip(shapes, arrays)],
        in_specs=[spec(pltpu.HBM)] * len(inputs),
        out_specs=[spec(pltpu.HBM)] * len(arrays),
        scratch_shapes=buffers * 3
        + [buffers[unit] for unit in list(ready) + list(halved)]
        + [dma((len(arrays) + len(ready),)), dma((len(arrays),))]
        + [dma((len(chunks),))] * 8,
        compiler_params=pltpu.CompilerParams(
            vmem_limit_bytes=60 << 20, collective_id=2, has_side_effects=True
        ),
        name="tail",
    )(*inputs)


def small_sum_kernel(steps, fsdp_axis, value_ref, out_ref, held_ref, *refs):
    fsdp_refs, ctx_refs = refs[: len(steps)], refs[len(steps) : len(steps) + 3]
    send_sem, recv_sem = refs[len(steps) + 3 :]
    c = lax.axis_index("ctx")
    f = lax.axis_index(fsdp_axis)
    mesh_id = pl.DeviceIdType.MESH
    barrier = pltpu.get_barrier_semaphore()
    for step in steps:
        pl.semaphore_signal(barrier, inc=1, device_id={fsdp_axis: peer(f, step)}, device_id_type=mesh_id)
    for k in range(1, 4):
        pl.semaphore_signal(barrier, inc=1, device_id={"ctx": peer(c, k)}, device_id_type=mesh_id)
    pl.semaphore_wait(barrier, len(steps) + 3)
    total = value_ref[...]
    for index, step in enumerate(steps):
        held_ref[index] = total
        copy = pltpu.make_async_remote_copy(
            src_ref=held_ref.at[index],
            dst_ref=fsdp_refs[index],
            send_sem=send_sem.at[index],
            recv_sem=recv_sem.at[index],
            device_id={fsdp_axis: peer(f, step)},
            device_id_type=mesh_id,
        )
        copy.start()
        copy.wait()
        total = total + fsdp_refs[index][...]
    held_ref[len(steps)] = total
    copies = []
    for k in range(1, 4):
        copy = pltpu.make_async_remote_copy(
            src_ref=held_ref.at[len(steps)],
            dst_ref=ctx_refs[k - 1],
            send_sem=send_sem.at[len(steps) + k - 1],
            recv_sem=recv_sem.at[len(steps) + k - 1],
            device_id={"ctx": peer(c, k)},
            device_id_type=mesh_id,
        )
        copy.start()
        copies.append(copy)
    for copy in copies:
        copy.wait()
    near = total + ctx_refs[0][...]
    out_ref[...] = near + (ctx_refs[1][...] + ctx_refs[2][...])


def small_sum(values, steps):
    dma = pltpu.SemaphoreType.DMA
    return pl.pallas_call(
        functools.partial(small_sum_kernel, tuple(steps), "fsdp"),
        out_shape=jax.ShapeDtypeStruct(values.shape, values.dtype),
        in_specs=[spec(pltpu.VMEM)],
        out_specs=spec(pltpu.VMEM),
        scratch_shapes=[pltpu.VMEM((len(steps) + 1,) + values.shape, values.dtype)]
        + [pltpu.VMEM(values.shape, values.dtype)] * (len(steps) + 3)
        + [dma((len(steps) + 3,))] * 2,
        compiler_params=pltpu.CompilerParams(collective_id=3, has_side_effects=True),
        name="small_sum",
    )(values)


def norm_back(grad_normed, values, factor, gain_row):
    unit_rows = values * factor
    grad_gain = jnp.sum(grad_normed * unit_rows, axis=0)
    grad_unit = grad_normed * gain_row.astype(F32)
    inner_mean = jnp.mean(grad_unit * unit_rows, axis=-1, keepdims=True)
    return (factor * (grad_unit - unit_rows * inner_mean), grad_gain)


def swap(values, axis, size, step):
    return lax.ppermute(values, axis, [(i, i ^ step) for i in range(size)])


def halving(size):
    steps = []
    while size > 1:
        size //= 2
        steps.append(size)
    return steps


def shards(
    sizes,
    tokens,
    cotangent,
    seq_lengths,
    deal,
    norm_gains,
    query_key_value,
    forget_weight,
    forget_bias,
    out_weight,
    gate_up_weight,
    down_weight,
):
    fsdp, ctx, tp = sizes
    layer_count = query_key_value.shape[0]
    row_count, model_width = tokens.shape
    heads_here = forget_weight.shape[2]
    head_size = query_key_value.shape[3] // heads_here
    block_rows = row_count // 2
    piece = model_width // fsdp
    half_width = model_width // 2
    hp = -(-heads_here // ctx)
    heads_padded = hp * ctx
    width = heads_padded * head_size
    more_columns = (heads_padded - heads_here) * head_size
    qkv_columns = 3 * width + 128
    units = gate_up_weight.shape[3]
    unit_block = min(512, units)
    pack = Pack(hp, head_size)
    tiles = pack.tiles
    everything = (row_count, model_width)
    f_index = lax.axis_index("fsdp")
    c_index = lax.axis_index("ctx")
    t_index = lax.axis_index("tp")
    fsdp_steps = halving(fsdp)
    tp_steps = list(reversed(halving(tp)))
    offsets = [0]
    for step in fsdp_steps:
        offsets = offsets + [item ^ step for item in offsets]
    vmem, any_space = pltpu.VMEM, pltpu.HBM

    def add_low(left, right):
        return (left.astype(F32) + right.astype(F32)).astype(BF16)

    grads = {}
    tasks = {}
    pending = {}

    def row_major(values):
        return with_layout_constraint(values, Layout(tuple(range(values.ndim))))

    def gather_pieces(values):
        pieces = [values]
        for step in fsdp_steps[:-1]:
            for item in list(pieces):
                pieces.append(row_major((yield swap(item, "fsdp", fsdp, step))))
        return pieces

    def reduce_grad(near, far, axis, until):
        for step in reversed(fsdp_steps):
            near = add_low(near, (yield swap(far, "fsdp", fsdp, step)))
            if step != fsdp_steps[0]:
                size = near.shape[axis] // 2
                if until == "core" and size == piece and axis == 0:
                    return near, None
                near, far = (
                    lax.slice_in_dim(near, 0, size, axis=axis),
                    lax.slice_in_dim(near, size, 2 * size, axis=axis),
                )
                if until == "core" and size == piece:
                    return near, far
                if until == "pair" and size == piece:
                    return near, (yield swap(far, "fsdp", fsdp, fsdp_steps[0]))
        return near

    def begin(name, *args):
        tasks[name] = reduce_grad(*args)
        pending[name] = next(tasks[name])

    own_first = {}

    def begin_gather(name, values):
        values = row_major(values)
        tasks[name] = gather_pieces(values)
        own_first[name] = swap(values, "fsdp", fsdp, fsdp_steps[-1])
        pending[name] = next(tasks[name])

    def tick(values, names):
        names = [name for name in names if name in tasks]
        if not names:
            return values
        values, got = lax.optimization_barrier((values, [pending.pop(name) for name in names]))
        for name, item in zip(names, got):
            try:
                pending[name] = tasks[name].send(item)
            except StopIteration as end:
                grads[name] = end.value
                del tasks[name]
        return values

    def finished(name):
        while name in tasks:
            tick((), [name])
        return grads[name]

    def weight_pieces(name):
        pieces = finished(name)
        last = [own_first[name]] + [swap(item, "fsdp", fsdp, fsdp_steps[-1]) for item in pieces[1:]]
        last = [row_major(item) for item in last]
        return pieces + last

    def exchange(sends):
        return [sends[0]] + [swap(sends[k], "ctx", ctx, k) for k in range(1, ctx)]

    def to_local(values):
        return jnp.concatenate(
            [
                lax.dynamic_slice_in_dim(values, (f_index ^ item) * piece, piece, axis=1)
                for item in offsets
            ],
            axis=1,
        )

    def from_local(values):
        places = jnp.asarray([offsets.index(item) for item in range(fsdp)], jnp.int32)
        return jnp.concatenate(
            [
                lax.dynamic_slice_in_dim(values, places[f_index ^ item] * piece, piece, axis=1)
                for item in range(fsdp)
            ],
            axis=1,
        )

    def pick(items, index):
        out = items[0]
        for entry in range(1, len(items)):
            out = jnp.where(index == entry, items[entry], out)
        return out

    deal_order = deal[0]
    inverse = (
        jnp.zeros((2 * ctx,), jnp.int32).at[deal_order].set(jnp.arange(2 * ctx, dtype=jnp.int32))
    )
    seq_ends = jnp.cumsum(seq_lengths[0]).astype(jnp.int32)
    peers = jnp.bitwise_xor(jnp.arange(ctx, dtype=jnp.int32), c_index)
    blk = jnp.take(deal_order.reshape(ctx, 2), peers, axis=0).reshape(2 * ctx)
    place = 2 * jnp.bitwise_xor(inverse // 2, c_index) + inverse % 2

    def own_qkv(layer):
        return jnp.pad(query_key_value[layer], ((0, 0), (0, 0), (0, more_columns)))

    def own_last():
        parts = []
        for layer in range(layer_count):
            parts += [
                jnp.pad(forget_weight[layer], ((0, 0), (0, heads_padded - heads_here))),
                norm_gains[layer].T,
                jnp.zeros((piece, 128 - heads_padded - 2), BF16),
            ]
        return jnp.concatenate(parts, axis=1)

    share = model_width // tp

    def own_columns(values):
        values = lax.dynamic_slice_in_dim(values, t_index * share, share, axis=1).astype(BF16)
        return values.reshape(2, block_rows, share)

    def column_pieces(values):
        step = 1
        pieces = [values]
        while step < tp:
            pieces = pieces + [swap(item, "tp", tp, step) for item in pieces]
            step *= 2
        return pieces

    def all_columns(pieces):
        order = [0]
        step = 1
        while step < tp:
            order = order + [item ^ step for item in order]
            step *= 2
        stacked = jnp.concatenate(pieces, axis=1)
        places = jnp.asarray([order.index(item) for item in range(tp)], jnp.int32)
        return jnp.concatenate(
            [
                lax.dynamic_slice_in_dim(stacked, places[t_index ^ item] * share, share, axis=1)
                for item in range(tp)
            ],
            axis=1,
        )

    shard, cotangent, tokens, gate_up_weight, out_weight, down_weight = lax.optimization_barrier(
        (own_qkv(0), cotangent, tokens, gate_up_weight, out_weight, down_weight)
    )
    begin_gather(("w_qkv", 0), shard)
    begin_gather(("w_last", 0), own_last())
    output_places = [(inverse[2 * c_index + half] // 2) ^ c_index for half in range(2)]
    cot_places = [(deal_order[2 * c_index + half] // 2) ^ c_index for half in range(2)]
    cot_blocks = own_columns(cotangent)
    late_side = (c_index >= ctx // 2).astype(jnp.int32)
    cot_sends = []
    for k in range(ctx):
        wanted = deal_order[2 * (c_index ^ k) + late_side]
        cot_sends.append(lax.dynamic_index_in_dim(cot_blocks, wanted % 2, 0, keepdims=False))
    cot_got = exchange(cot_sends)

    bias_all = jnp.pad(forget_bias.astype(F32), ((0, 0), (0, 128 - heads_here)))[:, None, :]
    own_weights = [
        {
            "w_units": gate_up_weight[layer],
            "w_back": jnp.concatenate(
                [jnp.pad(out_weight[layer], ((0, more_columns), (0, 0))), down_weight[layer]], axis=0
            ),
        }
        for layer in range(layer_count)
    ]
    for layer in range(1, layer_count):
        own_weights[layer]["w_qkv"] = own_qkv(layer)

    residual = to_local(tokens)
    own_weights, residual, cot_got, output_places, cot_places = tick(
        (own_weights, residual, cot_got, output_places, cot_places), [("w_qkv", 0), ("w_last", 0)]
    )
    for name in ("w_back", "w_units"):
        begin_gather((name, 0), own_weights[0][name])
    cot_mine = jnp.concatenate(
        [pick(cot_got, cot_places[half]) for half in range(2)], axis=0
    )
    weights = [{"w_qkv": weight_pieces(("w_qkv", 0)), "w_last": weight_pieces(("w_last", 0))}]
    gains = []

    def piece_inputs(layer, *names):
        return {
            f"{name}_{index}": (item, any_space)
            for name in names
            for index, item in enumerate(weights[layer][name])
        }

    def packed_out():
        return ((ctx, tiles, 2, block_rows, 128), BF16, vmem)

    dma = pltpu.SemaphoreType.DMA
    mix = pltpu.VMEM((model_width, max(units, qkv_columns)), BF16)

    def project(layer, residual):
        out = named_call(
            functools.partial(first_kernel, pack, ctx, width, layer),
            "project",
            {
                "residual": (residual, vmem),
                "bias": (bias_all[layer], vmem),
                **piece_inputs(layer, "w_qkv", "w_last"),
            },
            {
                "normed": (everything, BF16, vmem),
                "packed": packed_out(),
                "logits": ((row_count, 128), F32, vmem),
                "stat": ((8, model_width), F32, vmem),
                "gains": ((8, model_width), F32, vmem),
            },
            {"w_mix": pltpu.VMEM((model_width, qkv_columns), BF16), "sems": dma((4 * fsdp,))},
            None,
        )
        stat_rows[layer][0] = out["stat"][0]
        gains.append(out["gains"])
        return out["normed"], out["packed"], out["logits"]

    stat_rows = [[None] * 3 for _ in range(layer_count)]
    normed_one, packed, logits = project(0, residual)
    kept = []
    for layer in range(layer_count):
        later = layer + 1
        last = later == layer_count
        rest = [(name, layer) for name in ("w_back", "w_units")]
        if layer == 0:
            packed, cot_mine = lax.optimization_barrier((packed, cot_mine))
        if last:
            cot_pieces = column_pieces(cot_mine)
        att, received, lse, att_turned = attend(pack, place, blk, seq_ends, packed)
        if last:
            att, cot_pieces = lax.optimization_barrier((att, cot_pieces))
            att = tick(att, rest)
        else:
            att, own_weights[later] = tick((att, own_weights[later]), rest)
            begin_gather(("w_qkv", later), own_weights[later]["w_qkv"])
            begin_gather(("w_back", later), own_weights[later]["w_back"])
        for item in rest:
            weights[layer][item[0]] = weight_pieces(item)
        inputs = {
            "att": (att, vmem),
            "residual": (residual, any_space),
            "gains": (gains[layer], vmem),
            **{
                key: value
                for key, value in piece_inputs(layer, "w_back", "w_units").items()
                if int(key.split("_")[-1]) <= fsdp // 2
            },
        }
        outputs = {
            "attended": ((row_count, width), BF16, vmem),
            "middle": (everything, F32, any_space),
            "normed_two": (everything, BF16, any_space),
            "gate": ((row_count, units), BF16, any_space),
            "up": ((row_count, units), BF16, any_space),
            "hidden": ((row_count, units), BF16, any_space),
            "after": (everything, F32, any_space),
            "stat": ((8, model_width), F32, vmem),
        }
        out = named_call(
            functools.partial(middle_kernel, pack, ctx, units, unit_block, tp_steps, fsdp),
            "middle",
            inputs,
            outputs,
            {
                "w_o": pltpu.VMEM((width, model_width), BF16),
                "w_g": pltpu.VMEM((model_width, units), BF16),
                "w_mix": pltpu.VMEM((model_width, units), BF16),
                "w_d": pltpu.VMEM((units, model_width), BF16),
                "base": pltpu.VMEM(everything, F32),
                "after_keep": pltpu.VMEM(everything, F32),
                "normed_keep": pltpu.VMEM(everything, BF16),
                "gate_keep": pltpu.VMEM((row_count, units), BF16),
                "up_keep": pltpu.VMEM((row_count, units), BF16),
                "hidden_keep": pltpu.VMEM((row_count, units), BF16),
                "total": pltpu.VMEM((block_rows, model_width), F32),
                "sems": dma((5 * fsdp + 16,)),
                "core_send": dma((2 * fsdp,)),
                "core_recv": dma((2 * fsdp,)),
                **pair_scratch(4, tp_steps, block_rows, model_width),
            },
            4,
        )
        kept.append(
            dict(
                residual=residual,
                normed_one=normed_one,
                logits=logits,
                received=received,
                lse=lse,
                att_turned=att_turned,
                **{
                    name: out[name] for name in ("attended", "middle", "normed_two", "gate", "up", "hidden")
                },
            )
        )
        stat_rows[layer][1] = out["stat"][0]
        stat_rows[layer][2] = out["stat"][1]
        residual = out["after"]
        if not last:
            residual, own_weights[later] = tick(
                (residual, own_weights[later]), [("w_qkv", later), ("w_back", later)]
            )
            begin_gather(("w_units", later), own_weights[later]["w_units"])
            weights.append(
                {"w_qkv": weight_pieces(("w_qkv", later)), "w_last": weights[0]["w_last"]}
            )
            normed_one, packed, logits = project(later, residual)

    final_blocks = own_columns(residual)
    out_got = exchange(
        [
            lax.dynamic_index_in_dim(
                final_blocks, ((c_index ^ k) >= ctx // 2).astype(jnp.int32), 0, keepdims=False
            )
            for k in range(ctx)
        ]
    )

    def halves(values):
        return values[:, :half_width], values[:, half_width:]

    def weight_grad(left, right):
        return lax.dot_general(left, right, (((0,), (0,)), ((), ())), preferred_element_type=F32).astype(BF16)

    gain_grads = [None] * (2 * layer_count)
    bias_grads = [None] * layer_count

    def back_call(layer, upper, grad_base, back_got):
        inputs, outputs, scratch = {}, {}, {"w_mix": mix, "sems": dma((8 * fsdp + 24,))}
        scratch["total"] = pltpu.VMEM((block_rows, model_width), F32)
        if upper is not None:
            inputs.update(
                back=(back_got, vmem), logits=(kept[upper]["logits"], vmem), **piece_inputs(upper, "w_qkv", "w_last")
            )
            outputs.update(
                grads=((row_count, qkv_columns), BF16, any_space), bias_grad=((8, 128), F32, vmem)
            )
            scratch.update(grads_keep=pltpu.VMEM((row_count, qkv_columns), BF16))
            if layer is None:
                outputs.update(one_part=(everything, BF16, vmem))
            else:
                inputs.update(
                    residual=(kept[upper]["residual"], any_space), upper_gains=(gains[upper], vmem)
                )
        if layer is not None:
            state = kept[layer]
            inputs.update(
                base_in=(grad_base, any_space),
                middle=(state["middle"], any_space),
                gate=(state["gate"], any_space),
                up=(state["up"], any_space),
                gains=(gains[layer], vmem),
                **piece_inputs(layer, "w_back", "w_units"),
            )
            outputs.update(
                low=(everything, BF16, any_space),
                grad_gate=((row_count, units), BF16, any_space),
                grad_up=((row_count, units), BF16, any_space),
                grad=(everything, F32, any_space),
                branch=(everything, BF16, vmem),
                sends=((ctx, hp, block_rows, 128), BF16, vmem),
                gain_grad=((8, model_width), F32, vmem),
            )
            scratch.update(
                base=pltpu.VMEM(everything, grad_base.dtype),
                values=pltpu.VMEM(everything, F32),
                grad_keep=pltpu.VMEM(everything, F32),
                low_keep=pltpu.VMEM(everything, BF16),
                gate_keep=pltpu.VMEM((row_count, units), BF16),
                up_keep=pltpu.VMEM((row_count, units), BF16),
                turned=pltpu.VMEM((row_count, width), BF16),
                w_o=pltpu.VMEM((width, model_width), BF16),
                w_g=pltpu.VMEM((model_width, units), BF16),
                w_d=pltpu.VMEM((units, model_width), BF16),
                **pair_scratch(2 if upper is None else 4, tp_steps, block_rows, model_width),
            )
        return named_call(
            functools.partial(
                back_kernel,
                pack,
                ctx,
                width,
                units,
                unit_block,
                tp_steps,
                upper,
                layer is not None,
            ),
            "back_top" if upper is None else "back_end" if layer is None else "back",
            inputs,
            outputs,
            scratch,
            None if layer is None else 6 if upper is None else 7,
        )

    def begin_qkv(layer, out):
        bias_grads[layer] = out["bias_grad"][0, :heads_here]
        begin(
            ("qkv", layer),
            *[weight_grad(part, out["grads"]) for part in halves(kept[layer]["normed_one"])],
            0,
            "core",
        )

    ffn = ("down", "gate", "up", "out")
    grad_base = to_local(all_columns(cot_pieces))
    back_got, upper = None, None
    for layer in reversed(range(layer_count)):
        state = kept[layer]
        out = back_call(layer, upper, grad_base, back_got)
        if upper is None:
            out, out_got = lax.optimization_barrier((out, out_got))
        if upper is not None:
            gain_grads[2 * upper] = out["gain_grad"][0]
            begin_qkv(upper, out)
        gain_grads[2 * layer + 1] = out["gain_grad"][1]
        grad_base = out["grad"]
        lefts = [state["hidden"], state["normed_two"], state["normed_two"], state["attended"]]
        rights = [out["low"], out["grad_gate"], out["grad_up"], out["branch"]]
        for name, left, right in zip(ffn, lefts, rights):
            if name in ("down", "out"):
                pairs = [weight_grad(left, part) for part in halves(right)]
            else:
                pairs = [weight_grad(part, right) for part in halves(left)]
            reach = "core"
            if name in ("down", "gate"):
                reach = "fsdp" if layer else "pair"
            if upper is not None and name == "gate":
                pairs, background = lax.optimization_barrier((pairs, background))
                grads["down", upper], grads["gate", upper] = background
            begin((name, layer), *pairs, 1 if name in ("down", "out") else 0, reach)
        sends = tick(out["sends"], [(name, layer) for name in ("down", "gate")])
        if upper is None:
            mixed = jnp.concatenate(
                [pick(out_got, output_places[half]) for half in range(2)], axis=0
            )
        if layer == 0:
            sends, mixed = lax.optimization_barrier((sends, mixed))
            mixed_pieces = column_pieces(mixed)
        back_got = attend_back(
            pack, place, blk, seq_ends, state["received"], state["lse"], state["att_turned"], sends
        )
        back_got = tick(back_got, [(name, layer) for name in ffn] + [("qkv", layer + 1)])
        if layer == 0:
            back_got, mixed_pieces = lax.optimization_barrier((back_got, mixed_pieces))
            mixed_out = from_local(all_columns(mixed_pieces)).astype(F32)
        if layer:
            background = lax.psum([grads["down", layer], grads["gate", layer]], "ctx")
        upper = layer
    out = back_call(None, 0, None, back_got)
    begin_qkv(0, out)
    one_pairs = []
    for half in range(2):
        part = out["one_part"][half * block_rows : (half + 1) * block_rows]
        for step in tp_steps[:-1]:
            part = add_low(part, swap(part, "tp", tp, step))
        one_pairs.append((part, swap(part, "tp", tp, tp_steps[-1])))
    names = [(name, 0) for name in ("down", "gate")]
    arrays = [grads[name][0] for name in names]
    given = {unit: grads[name][1] for unit, name in enumerate(names)}
    far_units = {}
    for name in [("up", 0), ("out", 0)] + [
        (name, layer) for layer in range(1, layer_count) for name in ("up", "out", "qkv")
    ] + [("qkv", 0)]:
        near, far = finished(name)
        far_units[len(arrays)] = far
        arrays.append(near)
        names.append(name)
    reduced = tail(arrays, given, far_units, fsdp_steps[0])
    one_pairs, reduced = lax.optimization_barrier((one_pairs, reduced))
    for name, item in zip(names, reduced):
        grads[name] = item
    grad_normed_one = jnp.concatenate(
        [left.astype(F32) + right.astype(F32) for left, right in one_pairs], axis=0
    )
    first = kept[0]["residual"]
    grad_from_one, gain_grads[0] = norm_back(grad_normed_one, first, unit_factor(first), gains[0][0:1])
    grad_tokens = from_local(grad_base + grad_from_one)

    small = jnp.concatenate(
        [from_local(jnp.stack(gain_grads)).reshape(-1), jnp.sum(jnp.stack([item for row in stat_rows for item in row]), axis=1)]
        + bias_grads
    )
    used = small.shape[0]
    small = jnp.pad(small, (0, -used % 2048)).reshape(-1, 128)
    small = small_sum(small, list(reversed(fsdp_steps))).reshape(-1)
    gain_size = 2 * layer_count * model_width
    grad_gains = lax.dynamic_slice_in_dim(
        small[:gain_size].reshape(layer_count, 2, model_width), f_index * piece, piece, axis=2
    )
    stat_sums = small[gain_size : gain_size + 3 * layer_count].reshape(layer_count, 3)
    bias_sums = small[gain_size + 3 * layer_count : used].reshape(layer_count, heads_here)
    rms_values = jnp.sqrt(stat_sums / (row_count * model_width * fsdp * ctx))

    def both(pick_one):
        return jnp.stack([pick_one(layer).astype(F32) for layer in range(layer_count)])

    kept_columns = heads_here * head_size
    return (
        mixed_out,
        grad_tokens,
        grad_gains,
        both(
            lambda layer: jnp.stack(
                [grads["qkv", layer][:, j * width : j * width + kept_columns] for j in range(3)]
            )
        ),
        both(lambda layer: grads["qkv", layer][:, 3 * width : 3 * width + heads_here]),
        bias_sums,
        both(lambda layer: grads["out", layer][:kept_columns]),
        both(lambda layer: jnp.stack([grads["gate", layer], grads["up", layer]])),
        both(lambda layer: grads["down", layer]),
        rms_values,
    )


def solution(mesh):
    in_specs = (
        P(("fsdp", "ctx"), None),
        P(("fsdp", "ctx"), None),
        P("fsdp", None),
        P("fsdp", None),
        P(None, None, "fsdp"),
        P(None, None, "fsdp", "tp"),
        P(None, "fsdp", "tp"),
        P(None, "tp"),
        P(None, "tp", "fsdp"),
        P(None, None, "fsdp", "tp"),
        P(None, "tp", "fsdp"),
    )
    out_specs = (
        P(("fsdp", "ctx"), None),
        P(("fsdp", "ctx"), None),
        P(None, None, "fsdp"),
        P(None, None, "fsdp", "tp"),
        P(None, "fsdp", "tp"),
        P(None, "tp"),
        P(None, "tp", "fsdp"),
        P(None, None, "fsdp", "tp"),
        P(None, "tp", "fsdp"),
        P(),
    )
    sizes = (mesh.shape["fsdp"], mesh.shape["ctx"], mesh.shape["tp"])
    return jax.shard_map(
        functools.partial(shards, sizes),
        mesh=mesh,
        in_specs=in_specs,
        out_specs=out_specs,
        check_vma=False,
    )
```
